32 devices in a mesh: ctx: 4 (over y, x), fsdp: 8 (over z, core).
Axes of the slice: x: 2, y: 2, z: 4, core: 2. Of those that a mesh axis runs over, the one named last changes fastest.
Arguments:
- layer_input: bfloat16 [2, 8, 1024, 1088], P(None, 'fsdp', 'ctx'), may hold values from -6 to 6
- output_grad: bfloat16 [2, 8, 1024, 1088], P(None, 'fsdp', 'ctx'), may hold values from -6 to 6
- attn_gain: bfloat16 [1088], P('fsdp'), may hold values from 0.5 to 1.5
- attn_shift: bfloat16 [1088], P('fsdp'), may hold values from -1 to 1
- merged_weight: bfloat16 [1088, 3264], P('fsdp'), may hold values from -0.1875 to 0.1875
- query_bias: bfloat16 [1088], P('fsdp'), may hold values from -2.5 to 2.5
- value_bias: bfloat16 [1088], P('fsdp'), may hold values from -1.5 to 1.5
- out_weight: bfloat16 [1088, 1088], P('fsdp'), may hold values from -3 to 3
- out_bias: bfloat16 [1088], P('fsdp'), may hold values from -1 to 1
- mlp_gain: bfloat16 [1088], P('fsdp'), may hold values from 0.5 to 1.5
- mlp_shift: bfloat16 [1088], P('fsdp'), may hold values from -1 to 1
- up_weight: bfloat16 [1088, 4352], P('fsdp'), may hold values from -0.1875 to 0.1875
- up_bias: bfloat16 [4352], P('fsdp'), may hold values from -1.5 to 1.5
- down_weight: bfloat16 [4352, 1088], P('fsdp'), may hold values from -0.1875 to 0.1875
- down_bias: bfloat16 [1088], P('fsdp'), may hold values from -1 to 1
Outputs:
- layer_output: bfloat16 [2, 8, 1024, 1088], P(None, 'fsdp', 'ctx')
- input_grad: float32 [2, 8, 1024, 1088], P(None, 'fsdp', 'ctx')
- grad_attn_gain: float32 [1088], P('fsdp')
- grad_attn_shift: float32 [1088], P('fsdp')
- grad_merged_weight: float32 [1088, 3264], P('fsdp')
- grad_query_bias: float32 [1088], P('fsdp')
- grad_value_bias: float32 [1088], P('fsdp')
- grad_out_weight: float32 [1088, 1088], P('fsdp')
- grad_out_bias: float32 [1088], P('fsdp')
- grad_mlp_gain: float32 [1088], P('fsdp')
- grad_mlp_shift: float32 [1088], P('fsdp')
- grad_up_weight: float32 [1088, 4352], P('fsdp')
- grad_up_bias: float32 [4352], P('fsdp')
- grad_down_weight: float32 [4352, 1088], P('fsdp')
- grad_down_bias: float32 [1088], P('fsdp')
The draws below stay inside these ranges and needn't reach their ends.
All inputs are finite; a program needn't handle non-finite values.
Results may differ from the reference program's by a relative error of at most 0.02.
Values may be sent and summed in bfloat16 or wider, within the bound.
No kernel may reach another device: no remote copies, remote signals or barrier semaphores. Data moves between devices by JAX's collectives and lax.ppermute only.
A program may use at most 256 MiB of HBM per device.

```python
import math
import jax
import jax.numpy as jnp
from jax import lax

D = 1088
HEADS = 17
FF = 4352
MICRO = 2
LENGTH = 1024
GROUPS = 8


def block_scale(key, extent, pieces, smallest, high):
    level, own = 1.0, jax.random.fold_in(key, 6)
    for position, blocks in pieces:
        draws = jnp.exp(jax.random.uniform(jax.random.fold_in(own, position), (blocks,), jnp.float32, smallest / len(pieces), high / len(pieces)))
        level = level * jnp.repeat(draws, extent[position] // blocks).reshape([-1 if axis == position else 1 for axis in range(len(extent))])
    return level


def centred(stream_key, shape, scale, most, shards=(), kind=jnp.bfloat16):
    factor_of = block_scale(stream_key, shape, shards, -0.22, 0.18) if shards else 1.0
    entries = jax.random.normal(stream_key, shape, jnp.float32) * scale * factor_of
    return jnp.minimum(jnp.maximum(entries, -most), most).astype(kind)


def setup_inputs(seed: int = 0) -> dict:
    splits = jax.random.split(jax.random.key(seed), 16)
    return {
        "layer_input": centred(splits[0], (MICRO, GROUPS, LENGTH, D), 1.0, 6.0, ((1, 8), (2, 4))),
        "output_grad": centred(splits[1], (MICRO, GROUPS, LENGTH, D), 1.0, 6.0, ((1, 8), (2, 4))),
        "attn_gain": jnp.clip(1.0 + 0.1 * jax.random.normal(splits[2], (D,), jnp.float32), 0.5, 1.5).astype(jnp.bfloat16),
        "attn_shift": centred(splits[3], (D,), 0.2, 1.0, ((0, 8),)),
        "merged_weight": centred(splits[4], (D, 3 * D), D ** -0.5, 0.1875, ((0, 8),)),
        "query_bias": centred(splits[5], (D,), 0.5, 2.5, ((0, 8),)),
        "value_bias": centred(splits[6], (D,), 0.3, 1.5, ((0, 8),)),
        "out_weight": centred(splits[7], (D, D), (max(D // 256, 1)) ** -0.5, 3.0, ((0, 8),)),
        "out_bias": centred(splits[8], (D,), 0.2, 1.0, ((0, 8),)),
        "mlp_gain": jnp.clip(1.0 + 0.1 * jax.random.normal(splits[9], (D,), jnp.float32), 0.5, 1.5).astype(jnp.bfloat16),
        "mlp_shift": centred(splits[10], (D,), 0.2, 1.0, ((0, 8),)),
        "up_weight": centred(splits[11], (D, FF), D ** -0.5, 0.1875, ((0, 8),)),
        "up_bias": centred(splits[12], (FF,), 0.3, 1.5, ((0, 8),)),
        "down_weight": centred(splits[13], (FF, D), (FF // 4) ** -0.5, 0.1875, ((0, 8),)),
        "down_bias": centred(splits[14], (D,), 0.2, 1.0, ((0, 8),)),
    }


@jax.custom_vjp
def low(v):
    return lax.optimization_barrier(v.astype(jnp.bfloat16)).astype(jnp.float32)

@jax.custom_vjp
def low_back(v):
    return v

def low_keep(v):
    return (low(v), None)

def low_pass(kept, grad):
    return (grad,)

def back_keep(v):
    return (v, None)

def back_low(kept, grad):
    return (low(grad),)
low.defvjp(low_keep, low_pass)
low_back.defvjp(back_keep, back_low)
EPSILON = 1e-05
MASKED = -1e+30

def layer_norm(values, gain_row, shift_row):
    centre = values - lax.optimization_barrier(jnp.mean(values, axis=-1, keepdims=True))
    spread = lax.optimization_barrier(jnp.mean(centre * centre, axis=-1, keepdims=True))
    return centre * lax.rsqrt(spread + EPSILON) * gain_row + shift_row

def both_ways(values):
    return low(low_back(values))

def attention(queries, key_rows, value_rows):
    length = queries.shape[0]
    head_count = queries.shape[1]
    head_size = queries.shape[2]
    block_rows = math.gcd(length, 512)
    score_scale = head_size ** (-0.5)
    key_pos = jnp.arange(length, dtype=jnp.int32)

    def one_block(block_start):
        query_block = lax.dynamic_slice_in_dim(queries, block_start, block_rows, 0)
        raw_scores = low_back(jnp.einsum('qhd,khd->hqk', query_block, key_rows, precision=lax.Precision.HIGHEST))
        scores = raw_scores * score_scale
        query_pos = block_start + jnp.arange(block_rows, dtype=jnp.int32)
        allowed = key_pos[None, :] <= query_pos[:, None]
        scores = jnp.where(allowed[None], scores, MASKED)
        row_peak = lax.optimization_barrier(jnp.max(scores, axis=-1, keepdims=True))
        exp_scores = jnp.exp(scores - row_peak)
        weights_low = low(exp_scores / lax.optimization_barrier(jnp.sum(exp_scores, axis=-1, keepdims=True)))
        return jnp.einsum('hqk,khd->qhd', weights_low, value_rows, precision=lax.Precision.HIGHEST)
    starts = jnp.arange(length // block_rows, dtype=jnp.int32) * block_rows
    blocks = lax.map(jax.checkpoint(one_block), starts)
    return blocks.reshape(length, head_count * head_size)

def forward(params, values):
    attn_gain, attn_shift, merged_weight, query_bias, value_bias, out_weight, out_bias, mlp_gain, mlp_shift, up_weight, up_bias, down_weight, down_bias = params
    model_width = values.shape[-1]
    length = values.shape[0]
    head_size = model_width // HEADS
    normed = low(layer_norm(values, attn_gain, attn_shift))
    merged_rows = jnp.dot(normed, merged_weight, precision=lax.Precision.HIGHEST, preferred_element_type=jnp.float32)
    queries = both_ways(merged_rows[:, :model_width] + query_bias)
    key_rows = both_ways(merged_rows[:, model_width:2 * model_width])
    value_rows = both_ways(merged_rows[:, 2 * model_width:] + value_bias)
    attended = attention(queries.reshape(length, HEADS, head_size), key_rows.reshape(length, HEADS, head_size), value_rows.reshape(length, HEADS, head_size))
    attended = both_ways(attended)
    attn_branch = low_back(jnp.dot(attended, out_weight, precision=lax.Precision.HIGHEST, preferred_element_type=jnp.float32) + out_bias)
    middle = values + attn_branch
    normed_two = low(layer_norm(middle, mlp_gain, mlp_shift))
    pre_act = low_back(jnp.dot(normed_two, up_weight, precision=lax.Precision.HIGHEST, preferred_element_type=jnp.float32) + up_bias)
    hidden = low(jax.nn.gelu(pre_act, approximate=False))
    mlp_branch = low_back(jnp.dot(hidden, down_weight, precision=lax.Precision.HIGHEST, preferred_element_type=jnp.float32) + down_bias)
    return middle + mlp_branch

def reference(layer_input, output_grad, attn_gain, attn_shift, merged_weight, query_bias, value_bias, out_weight, out_bias, mlp_gain, mlp_shift, up_weight, up_bias, down_weight, down_bias):
    params = (attn_gain.astype(jnp.float32), attn_shift.astype(jnp.float32), merged_weight.astype(jnp.float32), query_bias.astype(jnp.float32), value_bias.astype(jnp.float32), out_weight.astype(jnp.float32), out_bias.astype(jnp.float32), mlp_gain.astype(jnp.float32), mlp_shift.astype(jnp.float32), up_weight.astype(jnp.float32), up_bias.astype(jnp.float32), down_weight.astype(jnp.float32), down_bias.astype(jnp.float32))
    full_shape = layer_input.shape
    length = full_shape[2]
    model_width = full_shape[3]
    flat_input = layer_input.reshape(-1, length, model_width).astype(jnp.float32)
    flat_grad = output_grad.reshape(-1, length, model_width).astype(jnp.float32)
    zero_grads = jax.tree.map(jnp.zeros_like, params)

    def one_sequence(totals, sequence_pair):
        seq_input, seq_grad = sequence_pair
        result, pullback = jax.vjp(forward, params, seq_input)
        param_grads, input_grads = pullback(seq_grad)
        totals = jax.tree.map(jnp.add, totals, param_grads)
        return (totals, (result.astype(jnp.bfloat16), input_grads))
    totals, (outputs, input_grads) = lax.scan(one_sequence, zero_grads, (flat_input, flat_grad))
    return (outputs.reshape(full_shape), input_grads.reshape(full_shape), totals[0], totals[1], totals[2], totals[3], totals[4], totals[5], totals[6], totals[7], totals[8], totals[9], totals[10], totals[11], totals[12])
```

```python
import functools

import jax
import jax.numpy as jnp
from jax import lax
from jax.experimental import pallas as pl
from jax.experimental.pallas import tpu as pltpu
from jax.sharding import PartitionSpec as P

HEADS = 17
EPSILON = 1e-05
MASKED = -1e30
VMEM_BYTES = 56 * 1024 * 1024
BF = jnp.bfloat16
F32 = jnp.float32


def swap(block, bit):
    size = lax.axis_size("ctx")
    return lax.ppermute(block, "ctx", [(i, i ^ bit) for i in range(size)])


def gather_ctx(block):
    size = lax.axis_size("ctx")
    if size != 4:
        return [block] + [swap(block, r) for r in range(1, size)]
    half = block.shape[0] // 2
    one = swap(block, 1)
    two = swap(block, 2)
    top = swap(two[:half], 1)
    bottom = swap(one[half:], 2)
    return [block, one, two, jnp.concatenate((top, bottom))]


def add_f32(a, b):
    return a.astype(F32) + b.astype(F32)


def reduce_ctx(parts):
    size = lax.axis_size("ctx")
    if size != 4:
        total = parts[0].astype(F32)
        for r in range(1, size):
            total = total + swap(parts[r], r).astype(F32)
        return total
    half = parts[0].shape[0] // 2
    from_one = swap(parts[3][:half], 1)
    from_two = swap(parts[3][half:], 2)
    for_two = jnp.concatenate(
        (add_f32(parts[2][:half], from_one).astype(BF), parts[2][half:].astype(BF))
    )
    for_one = jnp.concatenate(
        (parts[1][:half].astype(BF), add_f32(parts[1][half:], from_two).astype(BF))
    )
    got_one = swap(for_one, 1)
    got_two = swap(for_two, 2)
    return parts[0].astype(F32) + got_one.astype(F32) + got_two.astype(F32)


def trade_ctx(parts):
    return [parts[0]] + [swap(parts[r], r) for r in range(1, len(parts))]


def normal(values):
    centre = values - jnp.mean(values, axis=-1, keepdims=True)
    spread = jnp.mean(centre * centre, axis=-1, keepdims=True)
    rate = lax.rsqrt(spread + EPSILON)
    return centre * rate, rate


def norm_back(normed, rate, scaled):
    return rate * (
        scaled
        - jnp.mean(scaled, axis=-1, keepdims=True)
        - normed * jnp.mean(scaled * normed, axis=-1, keepdims=True)
    )


def dot(a, b, dims):
    return lax.dot_general(a, b, ((dims[0], dims[1]), ((), ())), preferred_element_type=F32)


NN = ((1,), (0,))
NT = ((1,), (1,))


def head_lanes(shape, head, head_size):
    lane = lax.broadcasted_iota(jnp.int32, shape, 1)
    return (lane >= head * head_size) & (lane < (head + 1) * head_size)


def attend_kernel(
    blocks, rows, heads, head_size, place, qkv, out, tail_out, log, tail_log, keys, values_t, tail_kv
):
    width = heads * head_size
    me = place[0]
    for j in range(blocks):
        slot = pl.ds(pl.multiple_of((me ^ j) * rows, rows), rows)
        here = pl.ds(j * rows, rows)
        keys[here, :] = qkv[slot, width : 2 * width]
        values_t[:width, here] = qkv[slot, 2 * width : 3 * width].T
        pair = qkv[slot, 3 * width : 3 * width + 2 * head_size]
        tail_kv[here, :] = pair
        values_t[width:, here] = pair.T
    key_row = lax.broadcasted_iota(jnp.int32, (rows, rows), 0)
    query_row = lax.broadcasted_iota(jnp.int32, (rows, rows), 1)

    def softmax_values(scores, value_rows):
        peak = scores[0].max(axis=0, keepdims=True)
        for s in scores[1:]:
            peak = jnp.maximum(peak, s.max(axis=0, keepdims=True))
        total = jnp.zeros((1, rows), F32)
        product = jnp.zeros((head_size, rows), F32)
        for j, s in enumerate(scores):
            e = jnp.exp(s - peak)
            total = total + e.sum(axis=0, keepdims=True)
            product = product + dot(
                values_t[value_rows, j * rows : (j + 1) * rows], e.astype(BF), NN
            )
        return product / total, peak + jnp.log(total)

    for i in range(blocks):
        slot = pl.ds(pl.multiple_of((me ^ i) * rows, rows), rows)
        query = qkv[slot, :width]
        products = []
        for h in range(heads):
            masked = jnp.where(head_lanes((rows, width), h, head_size), query, jnp.zeros_like(query))
            scores = []
            for j in range(i + 1):
                s = dot(keys[j * rows : (j + 1) * rows, :], masked, NT)
                if j == i:
                    s = jnp.where(key_row <= query_row, s, MASKED)
                scores.append(s)
            product, total = softmax_values(scores, pl.ds(h * head_size, head_size))
            products.append(product)
            log[h : h + 1, i * rows : (i + 1) * rows] = total
        out[slot, :] = jnp.concatenate(products, axis=0).T.astype(BF)

    query = qkv[0:rows, 3 * width + 2 * head_size : 3 * width + 3 * head_size]
    scores = []
    for j in range(blocks):
        s = dot(tail_kv[j * rows : (j + 1) * rows, :head_size], query, NT)
        scores.append(jnp.where(j * rows + key_row <= me * rows + query_row, s, MASKED))
    product, total = softmax_values(scores, pl.ds(width + head_size, head_size))
    tail_out[...] = product.T.astype(BF)
    tail_log[...] = total


def attend(place, qkv, blocks, rows, heads, head_size):
    width = heads * head_size
    length = blocks * rows
    return pl.pallas_call(
        functools.partial(attend_kernel, blocks, rows, heads, head_size),
        out_shape=(
            jax.ShapeDtypeStruct((length, width), BF),
            jax.ShapeDtypeStruct((rows, head_size), BF),
            jax.ShapeDtypeStruct((heads, length), F32),
            jax.ShapeDtypeStruct((1, rows), F32),
        ),
        in_specs=[
            pl.BlockSpec(memory_space=pltpu.SMEM),
            pl.BlockSpec(memory_space=pltpu.VMEM),
        ],
        out_specs=(pl.BlockSpec(memory_space=pltpu.VMEM),) * 4,
        scratch_shapes=[
            pltpu.VMEM((length, width), BF),
            pltpu.VMEM((width + 2 * head_size, length), BF),
            pltpu.VMEM((length, 2 * head_size), BF),
        ],
        compiler_params=pltpu.CompilerParams(vmem_limit_bytes=VMEM_BYTES),
        cost_estimate=pl.CostEstimate(
            flops=10 * 4 * length * length * width, bytes_accessed=6 * length * width, transcendentals=0
        ),
    )(place, qkv)


def attend_back_kernel(
    blocks,
    rows,
    heads,
    head_size,
    place,
    qkv,
    grad,
    tail_grad,
    log,
    tail_log,
    out,
    keys,
    values,
    keys_t,
    tail_kv,
    key_sum,
    value_sum,
    tail_key_sum,
    tail_value_sum,
):
    width = heads * head_size
    me = place[0]
    for j in range(blocks):
        slot = pl.ds(pl.multiple_of((me ^ j) * rows, rows), rows)
        here = pl.ds(j * rows, rows)
        block = qkv[slot, width : 2 * width]
        keys[here, :] = block
        keys_t[:width, here] = block.T
        values[here, :] = qkv[slot, 2 * width : 3 * width]
        pair = qkv[slot, 3 * width : 3 * width + 2 * head_size]
        tail_kv[here, :] = pair
        keys_t[width:, here] = pair.T
    key_row = lax.broadcasted_iota(jnp.int32, (rows, rows), 0)
    query_row = lax.broadcasted_iota(jnp.int32, (rows, rows), 1)
    scale = head_size**-0.5

    for i in range(blocks):
        slot = pl.ds(pl.multiple_of((me ^ i) * rows, rows), rows)
        query = qkv[slot, :width]
        grad_out = grad[slot, :]
        lanes = [head_lanes((rows, width), h, head_size) for h in range(heads)]
        queries = [jnp.where(m, query, jnp.zeros_like(query)) for m in lanes]
        grads = [jnp.where(m, grad_out, jnp.zeros_like(grad_out)) for m in lanes]
        query_parts = []
        for h in range(heads):
            shift = log[h : h + 1, i * rows : (i + 1) * rows]
            probs, weighted = [], []
            delta = jnp.zeros((1, rows), F32)
            for j in range(i + 1):
                here = slice(j * rows, (j + 1) * rows)
                s = dot(keys[here, :], queries[h], NT)
                if j == i:
                    s = jnp.where(key_row <= query_row, s, MASKED)
                p = jnp.exp(s - shift)
                g = dot(values[here, :], grads[h], NT)
                delta = delta + (p * g).sum(axis=0, keepdims=True)
                probs.append(p)
                weighted.append(g)
            part = jnp.zeros((head_size, rows), F32)
            for j in range(i + 1):
                here = slice(j * rows, (j + 1) * rows)
                ds = (probs[j] * (weighted[j] - delta)).astype(BF)
                p = probs[j].astype(BF)
                key_part = dot(ds, queries[h], NN)
                value_part = dot(p, grads[h], NN)
                if h == 0 and j == i:
                    key_sum[here, :] = key_part
                    value_sum[here, :] = value_part
                else:
                    key_sum[here, :] += key_part
                    value_sum[here, :] += value_part
                part = part + dot(keys_t[h * head_size : (h + 1) * head_size, here], ds, NN)
            query_parts.append(part)
        out[slot, :width] = (jnp.concatenate(query_parts, axis=0) * scale).T.astype(BF)

    query = qkv[0:rows, 3 * width + 2 * head_size : 3 * width + 3 * head_size]
    grad_out = tail_grad[...]
    probs, weighted = [], []
    delta = jnp.zeros((1, rows), F32)
    for j in range(blocks):
        here = slice(j * rows, (j + 1) * rows)
        s = dot(tail_kv[here, :head_size], query, NT)
        s = jnp.where(j * rows + key_row <= me * rows + query_row, s, MASKED)
        p = jnp.exp(s - tail_log[...])
        g = dot(tail_kv[here, head_size:], grad_out, NT)
        delta = delta + (p * g).sum(axis=0, keepdims=True)
        probs.append(p)
        weighted.append(g)
    part = jnp.zeros((head_size, rows), F32)
    for j in range(blocks):
        here = slice(j * rows, (j + 1) * rows)
        slot = pl.ds(pl.multiple_of((me ^ j) * rows, rows), rows)
        ds = (probs[j] * (weighted[j] - delta)).astype(BF)
        key_part = dot(ds, query, NN)
        value_part = dot(probs[j].astype(BF), grad_out, NN)
        part = part + dot(keys_t[width : width + head_size, here], ds, NN)
        out[slot, width : 2 * width] = key_sum[here, :].astype(BF)
        out[slot, 2 * width : 3 * width] = value_sum[here, :].astype(BF)
        out[slot, 3 * width : 3 * width + 2 * head_size] = jnp.concatenate(
            (key_part, value_part), axis=1
        ).astype(BF)
    tail_columns = slice(3 * width + 2 * head_size, 3 * width + 3 * head_size)
    out[0:rows, tail_columns] = (part * scale).T.astype(BF)
    for j in range(1, blocks):
        out[j * rows : (j + 1) * rows, tail_columns] = jnp.zeros((rows, head_size), BF)


def attend_back(place, qkv, grad, tail_grad, log, tail_log, blocks, rows, heads, head_size):
    width = heads * head_size
    length = blocks * rows
    return pl.pallas_call(
        functools.partial(attend_back_kernel, blocks, rows, heads, head_size),
        out_shape=jax.ShapeDtypeStruct(qkv.shape, BF),
        in_specs=[pl.BlockSpec(memory_space=pltpu.SMEM)]
        + [pl.BlockSpec(memory_space=pltpu.VMEM)] * 5,
        out_specs=pl.BlockSpec(memory_space=pltpu.VMEM),
        scratch_shapes=[
            pltpu.VMEM((length, width), BF),
            pltpu.VMEM((length, width), BF),
            pltpu.VMEM((width + 2 * head_size, length), BF),
            pltpu.VMEM((length, 2 * head_size), BF),
            pltpu.VMEM((length, width), F32),
            pltpu.VMEM((length, width), F32),
            pltpu.VMEM((length, head_size), F32),
            pltpu.VMEM((length, head_size), F32),
        ],
        compiler_params=pltpu.CompilerParams(vmem_limit_bytes=VMEM_BYTES),
        cost_estimate=pl.CostEstimate(
            flops=10 * 10 * length * length * width, bytes_accessed=9 * length * width, transcendentals=0
        ),
    )(place, qkv, grad, tail_grad, log, tail_log)


def mlp_kernel(
    normed, grad, up, down, bias, hidden_out, grad_pre_out, part_out, grad_part_out, bias_out
):
    pre = dot(normed[...], up[...], NN) + bias[...]
    bell = jnp.exp(-0.5 * pre * pre) * 0.3989422804014327
    below = 0.5 + 0.5 * lax.erf(pre * 0.7071067811865476)
    hidden = (pre * below).astype(BF)
    hidden_out[...] = hidden
    part_out[...] = dot(hidden, down[...], NN).astype(BF)
    grad_pre = ((below + pre * bell) * dot(grad[...], down[...], NT)).astype(BF)
    grad_pre_out[...] = grad_pre
    grad_part_out[...] = dot(grad_pre, up[...], NT).astype(BF)
    sums = grad_pre.astype(F32).sum(axis=0, keepdims=True)

    @pl.when(pl.program_id(0) == 0)
    def _():
        bias_out[...] = sums

    @pl.when(pl.program_id(0) > 0)
    def _():
        bias_out[...] += sums


def mlp(normed, grad, up, down, bias, rows):
    length, wide = normed.shape
    hidden = up.shape[1]
    row_block = pl.BlockSpec((rows, wide), lambda i: (i, 0))
    hidden_block = pl.BlockSpec((rows, hidden), lambda i: (i, 0))
    whole = pl.BlockSpec(memory_space=pltpu.VMEM)
    return pl.pallas_call(
        mlp_kernel,
        grid=(length // rows,),
        out_shape=(
            jax.ShapeDtypeStruct((length, hidden), BF),
            jax.ShapeDtypeStruct((length, hidden), BF),
            jax.ShapeDtypeStruct((length, wide), BF),
            jax.ShapeDtypeStruct((length, wide), BF),
            jax.ShapeDtypeStruct((1, hidden), F32),
        ),
        in_specs=[row_block, row_block, whole, whole, whole],
        out_specs=(
            hidden_block,
            hidden_block,
            row_block,
            row_block,
            pl.BlockSpec((1, hidden), lambda i: (0, 0)),
        ),
        compiler_params=pltpu.CompilerParams(vmem_limit_bytes=VMEM_BYTES),
        cost_estimate=pl.CostEstimate(
            flops=12 * length * wide * hidden,
            bytes_accessed=2 * (6 * length * wide + 2 * wide * hidden),
            transcendentals=0,
        ),
    )(normed, grad, up, down, bias)


def on_device(
    layer_input,
    output_grad,
    attn_gain,
    attn_shift,
    merged_weight,
    query_bias,
    value_bias,
    out_weight,
    out_bias,
    mlp_gain,
    mlp_shift,
    up_weight,
    up_bias,
    down_weight,
    down_bias,
):
    micros = layer_input.shape[0]
    rows = layer_input.shape[2]
    wide = layer_input.shape[3]
    head_size = wide // HEADS
    blocks = lax.axis_size("ctx")
    shards = lax.axis_size("fsdp")
    me = lax.axis_index("ctx")
    heads = HEADS // blocks
    width = heads * head_size
    main = blocks * width
    own = merged_weight.shape[0]
    hidden = up_weight.shape[1]
    piece = hidden // shards // blocks
    quads = hidden // wide
    used = 3 * width + 3 * head_size
    assert HEADS - heads * blocks == 1
    place = me.astype(jnp.int32).reshape(1)
    relative = jnp.arange(blocks, dtype=jnp.int32) ^ me
    start = me * width

    vectors = jnp.concatenate(
        (
            attn_gain,
            attn_shift,
            query_bias,
            value_bias,
            out_bias,
            mlp_gain,
            mlp_shift,
            down_bias,
            up_bias,
        )
    ).reshape(8 + quads, own)
    first = jnp.concatenate(
        (
            lax.dynamic_slice_in_dim(merged_weight, start, width, 1),
            lax.dynamic_slice_in_dim(merged_weight, wide + start, width, 1),
            lax.dynamic_slice_in_dim(merged_weight, 2 * wide + start, width, 1),
            merged_weight[:, wide + main : 2 * wide],
            merged_weight[:, 2 * wide + main :],
            merged_weight[:, main:wide],
            vectors.T,
        ),
        axis=1,
    )
    first = lax.all_gather(first, "fsdp", axis=0, tiled=True)
    merged_own = first[:, :used]
    vectors = first[:, used:].T.astype(F32)
    gain_one, shift_one, query_row, value_row, out_row, gain_two, shift_two, down_row = [
        vectors[i] for i in range(8)
    ]
    up_row = (
        vectors[8:]
        .reshape(quads, shards, own)
        .transpose(1, 0, 2)
        .reshape(shards, blocks, piece)
    )
    up_row = lax.dynamic_index_in_dim(up_row, me, 1, keepdims=False).reshape(1, shards * piece)
    zero_tail = jnp.zeros((head_size,), F32)
    merged_row = jnp.concatenate(
        (
            lax.dynamic_slice_in_dim(query_row, start, width),
            jnp.zeros((width,), F32),
            lax.dynamic_slice_in_dim(value_row, start, width),
            zero_tail,
            value_row[main:],
            query_row[main:],
        )
    )
    scale_row = jnp.concatenate(
        (
            jnp.full((width,), head_size**-0.5, BF),
            jnp.ones((2 * width + 2 * head_size,), BF),
            jnp.full((head_size,), head_size**-0.5, BF),
        )
    )
    out_full = lax.all_gather(out_weight, "fsdp", axis=0, tiled=True)
    up_own = lax.dynamic_index_in_dim(
        up_weight.reshape(own, shards, blocks, piece), me, 2, keepdims=False
    ).reshape(own, shards * piece)
    down_own = lax.dynamic_slice_in_dim(down_weight, me * piece, piece, 0)
    up_own = lax.all_gather(up_own, "fsdp", axis=0, tiled=True)
    down_own = lax.all_gather(down_own, "fsdp", axis=0, tiled=True)

    values = [layer_input[m, 0] for m in range(micros)]
    values_ctx = [gather_ctx(v) for v in values]
    grads = [output_grad[m, 0] for m in range(micros)]
    grads_ctx = [jnp.concatenate(gather_ctx(g)) for g in grads]

    unscaled, normed, qkv, log, tail_log, attended, middle, normed_two = ([] for _ in range(8))
    for m in range(micros):
        centred, rate = normal(jnp.concatenate(values_ctx[m]).astype(F32))
        unscaled.append((centred, rate))
        normed.append((centred * gain_one + shift_one).astype(BF))
        rows_out = jnp.dot(normed[m], merged_own, preferred_element_type=F32) + merged_row
        qkv.append(rows_out.astype(BF) * scale_row)
        out, tail_out, total, tail_total = attend(place, qkv[m], blocks, rows, heads, head_size)
        log.append(total)
        tail_log.append(tail_total)
        traded = jnp.stack(trade_ctx(list(out.reshape(blocks, rows, width))))
        traded = jnp.take(traded, relative, axis=0).transpose(1, 0, 2).reshape(rows, main)
        attended.append(jnp.concatenate((traded, tail_out), axis=1))
        middle.append(
            values[m].astype(F32)
            + jnp.dot(attended[m], out_full, preferred_element_type=F32)
            + out_row
        )
        centred, rate = normal(middle[m])
        normed_two.append((centred * gain_two + shift_two).astype(BF))

    hiddens, grad_pres, normed_two_ctx, layer_output, grad_middle = ([] for _ in range(5))
    grad_up_row = 0.0
    grad_gain_two = 0.0
    grad_shift_two = 0.0
    for m in range(micros):
        normed_two_ctx.append(jnp.concatenate(gather_ctx(normed_two[m])))
        act, grad_pre, part, grad_part, bias_part = mlp(
            normed_two_ctx[m], grads_ctx[m], up_own, down_own, up_row, rows
        )
        hiddens.append(act)
        grad_pres.append(grad_pre)
        grad_up_row = grad_up_row + bias_part
        grad_normed = reduce_ctx(list(grad_part.reshape(blocks, rows, wide)))
        centred, rate = normal(middle[m])
        grad_gain_two = grad_gain_two + jnp.sum(grad_normed * centred, axis=0)
        grad_shift_two = grad_shift_two + jnp.sum(grad_normed, axis=0)
        grad_middle.append(
            grads[m].astype(F32) + norm_back(centred, rate, grad_normed * gain_two)
        )
        total = reduce_ctx(list(part.reshape(blocks, rows, wide)))
        layer_output.append((middle[m] + total + down_row).astype(BF))
    grad_down = sum(dot(a, g, ((0,), (0,))) for a, g in zip(hiddens, grads_ctx, strict=True))
    grad_up = sum(dot(n, g, ((0,), (0,))) for n, g in zip(normed_two_ctx, grad_pres, strict=True))
    grad_down = lax.psum_scatter(grad_down.astype(BF), "fsdp", scatter_dimension=0, tiled=True)
    grad_up = lax.psum_scatter(grad_up.astype(BF), "fsdp", scatter_dimension=0, tiled=True)

    grad_out_weight = 0.0
    grad_out_row = 0.0
    grad_down_row = 0.0
    grad_merged = 0.0
    grad_merged_row = 0.0
    grad_gain_one = 0.0
    grad_shift_one = 0.0
    input_grad = []
    for m in range(micros):
        grad_attn = grad_middle[m].astype(BF)
        grad_out_weight = grad_out_weight + dot(attended[m], grad_attn, ((0,), (0,)))
        grad_out_row = grad_out_row + jnp.sum(grad_attn.astype(F32), axis=0)
        grad_down_row = grad_down_row + jnp.sum(grads[m].astype(F32), axis=0)
        grad_attended = dot(grad_attn, out_full, NT).astype(BF)
        to_trade = grad_attended[:, :main].reshape(rows, blocks, width).transpose(1, 0, 2)
        to_trade = jnp.take(to_trade, relative, axis=0)
        traded = jnp.concatenate(trade_ctx(list(to_trade)))
        grad_qkv = attend_back(
            place,
            qkv[m],
            traded,
            grad_attended[:, main:],
            log[m],
            tail_log[m],
            blocks,
            rows,
            heads,
            head_size,
        )
        grad_merged = grad_merged + dot(normed[m], grad_qkv, ((0,), (0,)))
        grad_merged_row = grad_merged_row + jnp.sum(grad_qkv.astype(F32), axis=0)
        grad_part = dot(grad_qkv, merged_own, NT)
        centred, rate = unscaled[m]
        grad_gain_one = grad_gain_one + jnp.sum(grad_part * centred, axis=0)
        grad_shift_one = grad_shift_one + jnp.sum(grad_part, axis=0)
        grad_normed = reduce_ctx(list(grad_part.astype(BF).reshape(blocks, rows, wide)))
        input_grad.append(
            grad_middle[m] + norm_back(centred[:rows], rate[:rows], grad_normed * gain_one)
        )

    def placed(part, tail):
        row = lax.dynamic_update_slice_in_dim(jnp.zeros((main,), F32), part, start, 0)
        return jnp.concatenate((row, tail))

    up_sums = lax.dynamic_update_slice_in_dim(
        jnp.zeros((shards, blocks, piece), F32), grad_up_row.reshape(shards, 1, piece), me, 1
    )
    up_sums = up_sums.reshape(shards, quads, own).transpose(1, 0, 2).reshape(quads, wide)
    vector_sums = jnp.concatenate(
        (
            jnp.stack(
                (
                    grad_gain_one,
                    grad_shift_one,
                    placed(grad_merged_row[:width], grad_merged_row[used - head_size :]),
                    placed(
                        grad_merged_row[2 * width : 3 * width],
                        grad_merged_row[3 * width + head_size : 3 * width + 2 * head_size],
                    ),
                    grad_out_row,
                    grad_gain_two,
                    grad_shift_two,
                    grad_down_row,
                )
            ),
            up_sums,
        )
    )
    last = jnp.concatenate((grad_merged, vector_sums.T), axis=1).astype(BF)
    last = lax.psum_scatter(last, "fsdp", scatter_dimension=0, tiled=True)
    grad_out_weight = lax.psum_scatter(
        grad_out_weight.astype(BF), "fsdp", scatter_dimension=0, tiled=True
    ).astype(F32)
    bit = 1
    while bit < blocks:
        grad_out_weight = grad_out_weight + swap(grad_out_weight.astype(BF), bit).astype(F32)
        bit *= 2

    def absolute(parts):
        return jnp.take(jnp.stack(parts), relative, axis=0).astype(F32)

    last = absolute(gather_ctx(last))
    tails = jnp.sum(last[:, :, 3 * width :], axis=0)

    def columns(index, tail):
        body = last[:, :, index * width : (index + 1) * width].transpose(1, 0, 2)
        return [body.reshape(own, main), tails[:, tail * head_size : (tail + 1) * head_size]]

    grad_merged = jnp.concatenate(columns(0, 2) + columns(1, 0) + columns(2, 1), axis=1)
    vector_sums = tails[:, 3 * head_size :].T
    grad_up = absolute(gather_ctx(grad_up)).reshape(blocks, own, shards, piece)
    grad_up = grad_up.transpose(1, 2, 0, 3).reshape(own, hidden)
    grad_down = absolute(gather_ctx(grad_down)).reshape(blocks * piece, wide)
    return (
        jnp.stack(layer_output)[:, None],
        jnp.stack(input_grad)[:, None],
        vector_sums[0],
        vector_sums[1],
        grad_merged,
        vector_sums[2],
        vector_sums[3],
        grad_out_weight,
        vector_sums[4],
        vector_sums[5],
        vector_sums[6],
        grad_up,
        vector_sums[8:].reshape(quads * own),
        grad_down,
        vector_sums[7],
    )


def solution(mesh):
    rows = P(None, "fsdp", "ctx", None)
    matrix = P("fsdp", None)
    vector = P("fsdp")
    in_specs = (
        rows,
        rows,
        vector,
        vector,
        matrix,
        vector,
        vector,
        matrix,
        vector,
        vector,
        vector,
        matrix,
        vector,
        matrix,
        vector,
    )
    out_specs = (rows, rows) + in_specs[2:]
    return jax.shard_map(
        on_device, mesh=mesh, in_specs=in_specs, out_specs=out_specs, check_vma=False
    )
```

```python
import functools

import jax
import jax.numpy as jnp
from jax import lax
from jax.experimental import pallas as pl
from jax.experimental.pallas import tpu as pltpu
from jax.sharding import PartitionSpec as P

HEADS = 17
EPSILON = 1e-05
MASKED = -1e30
VMEM_BYTES = 56 * 1024 * 1024
COST = 40
BF = jnp.bfloat16
F32 = jnp.float32


def swap(block, bit):
    size = lax.axis_size("ctx")
    return lax.ppermute(block, "ctx", [(i, i ^ bit) for i in range(size)])


def gather_ctx(block):
    size = lax.axis_size("ctx")
    if size != 4:
        return [block] + [swap(block, r) for r in range(1, size)]
    half = block.shape[0] // 2
    one = swap(block, 1)
    two = swap(block, 2)
    top = swap(two[:half], 1)
    bottom = swap(one[half:], 2)
    return [block, one, two, jnp.concatenate((top, bottom))]


def add_f32(a, b):
    return a.astype(F32) + b.astype(F32)


def reduce_ctx(parts):
    size = lax.axis_size("ctx")
    if size != 4:
        total = parts[0].astype(F32)
        for r in range(1, size):
            total = total + swap(parts[r], r).astype(F32)
        return total
    half = parts[0].shape[0] // 2
    from_one = swap(parts[3][:half], 1)
    from_two = swap(parts[3][half:], 2)
    for_two = jnp.concatenate(
        (add_f32(parts[2][:half], from_one).astype(BF), parts[2][half:].astype(BF))
    )
    for_one = jnp.concatenate(
        (parts[1][:half].astype(BF), add_f32(parts[1][half:], from_two).astype(BF))
    )
    got_one = swap(for_one, 1)
    got_two = swap(for_two, 2)
    return parts[0].astype(F32) + got_one.astype(F32) + got_two.astype(F32)


def trade_ctx(parts):
    return [parts[0]] + [swap(parts[r], r) for r in range(1, len(parts))]


def normal(values):
    centre = values - jnp.mean(values, axis=-1, keepdims=True)
    spread = jnp.mean(centre * centre, axis=-1, keepdims=True)
    rate = lax.rsqrt(spread + EPSILON)
    return centre * rate, rate


def norm_back(normed, rate, scaled):
    return rate * (
        scaled
        - jnp.mean(scaled, axis=-1, keepdims=True)
        - normed * jnp.mean(scaled * normed, axis=-1, keepdims=True)
    )


def dot(a, b, dims):
    return lax.dot_general(a, b, ((dims[0], dims[1]), ((), ())), preferred_element_type=F32)


NN = ((1,), (0,))
NT = ((1,), (1,))


def head_lanes(shape, head, head_size):
    lane = lax.broadcasted_iota(jnp.int32, shape, 1)
    return (lane >= head * head_size) & (lane < (head + 1) * head_size)


def attend_kernel(
    blocks, rows, heads, head_size, place, qkv, out, tail_out, log, tail_log, keys, values_t, tail_kv
):
    width = heads * head_size
    me = place[0]
    for j in range(blocks):
        slot = pl.ds(pl.multiple_of((me ^ j) * rows, rows), rows)
        here = pl.ds(j * rows, rows)
        keys[here, :] = qkv[slot, width : 2 * width]
        values_t[:width, here] = qkv[slot, 2 * width : 3 * width].T
        pair = qkv[slot, 3 * width : 3 * width + 2 * head_size]
        tail_kv[here, :] = pair
        values_t[width:, here] = pair.T
    key_row = lax.broadcasted_iota(jnp.int32, (rows, rows), 0)
    query_row = lax.broadcasted_iota(jnp.int32, (rows, rows), 1)

    def softmax_values(scores, value_rows):
        peak = scores[0].max(axis=0, keepdims=True)
        for s in scores[1:]:
            peak = jnp.maximum(peak, s.max(axis=0, keepdims=True))
        total = jnp.zeros((1, rows), F32)
        product = jnp.zeros((head_size, rows), F32)
        for j, s in enumerate(scores):
            e = jnp.exp(s - peak)
            total = total + e.sum(axis=0, keepdims=True)
            product = product + dot(
                values_t[value_rows, j * rows : (j + 1) * rows], e.astype(BF), NN
            )
        return product / total, peak + jnp.log(total)

    for i in range(blocks):
        slot = pl.ds(pl.multiple_of((me ^ i) * rows, rows), rows)
        query = qkv[slot, :width]
        products = []
        for h in range(heads):
            masked = jnp.where(head_lanes((rows, width), h, head_size), query, jnp.zeros_like(query))
            scores = []
            for j in range(i + 1):
                s = dot(keys[j * rows : (j + 1) * rows, :], masked, NT)
                if j == i:
                    s = jnp.where(key_row <= query_row, s, MASKED)
                scores.append(s)
            product, total = softmax_values(scores, pl.ds(h * head_size, head_size))
            products.append(product)
            log[h : h + 1, i * rows : (i + 1) * rows] = total
        out[slot, :] = jnp.concatenate(products, axis=0).T.astype(BF)

    query = qkv[0:rows, 3 * width + 2 * head_size : 3 * width + 3 * head_size]
    scores = []
    for j in range(blocks):
        s = dot(tail_kv[j * rows : (j + 1) * rows, :head_size], query, NT)
        scores.append(jnp.where(j * rows + key_row <= me * rows + query_row, s, MASKED))
    product, total = softmax_values(scores, pl.ds(width + head_size, head_size))
    tail_out[...] = product.T.astype(BF)
    tail_log[...] = total


def attend(place, qkv, blocks, rows, heads, head_size):
    width = heads * head_size
    length = blocks * rows
    return pl.pallas_call(
        functools.partial(attend_kernel, blocks, rows, heads, head_size),
        out_shape=(
            jax.ShapeDtypeStruct((length, width), BF),
            jax.ShapeDtypeStruct((rows, head_size), BF),
            jax.ShapeDtypeStruct((heads, length), F32),
            jax.ShapeDtypeStruct((1, rows), F32),
        ),
        in_specs=[
            pl.BlockSpec(memory_space=pltpu.SMEM),
            pl.BlockSpec(memory_space=pltpu.VMEM),
        ],
        out_specs=(pl.BlockSpec(memory_space=pltpu.VMEM),) * 4,
        scratch_shapes=[
            pltpu.VMEM((length, width), BF),
            pltpu.VMEM((width + 2 * head_size, length), BF),
            pltpu.VMEM((length, 2 * head_size), BF),
        ],
        compiler_params=pltpu.CompilerParams(vmem_limit_bytes=VMEM_BYTES),
        cost_estimate=pl.CostEstimate(
            flops=10 * 4 * length * length * width, bytes_accessed=6 * length * width, transcendentals=0
        ),
    )(place, qkv)


def attend_back_kernel(
    blocks,
    rows,
    heads,
    head_size,
    place,
    qkv,
    grad,
    tail_grad,
    log,
    tail_log,
    out,
    keys,
    values,
    keys_t,
    tail_kv,
    key_sum,
    value_sum,
    tail_key_sum,
    tail_value_sum,
):
    width = heads * head_size
    me = place[0]
    for j in range(blocks):
        slot = pl.ds(pl.multiple_of((me ^ j) * rows, rows), rows)
        here = pl.ds(j * rows, rows)
        block = qkv[slot, width : 2 * width]
        keys[here, :] = block
        keys_t[:width, here] = block.T
        values[here, :] = qkv[slot, 2 * width : 3 * width]
        pair = qkv[slot, 3 * width : 3 * width + 2 * head_size]
        tail_kv[here, :] = pair
        keys_t[width:, here] = pair.T
    key_row = lax.broadcasted_iota(jnp.int32, (rows, rows), 0)
    query_row = lax.broadcasted_iota(jnp.int32, (rows, rows), 1)
    scale = head_size**-0.5

    for i in range(blocks):
        slot = pl.ds(pl.multiple_of((me ^ i) * rows, rows), rows)
        query = qkv[slot, :width]
        grad_out = grad[slot, :]
        lanes = [head_lanes((rows, width), h, head_size) for h in range(heads)]
        queries = [jnp.where(m, query, jnp.zeros_like(query)) for m in lanes]
        grads = [jnp.where(m, grad_out, jnp.zeros_like(grad_out)) for m in lanes]
        query_parts = []
        for h in range(heads):
            shift = log[h : h + 1, i * rows : (i + 1) * rows]
            probs, weighted = [], []
            delta = jnp.zeros((1, rows), F32)
            for j in range(i + 1):
                here = slice(j * rows, (j + 1) * rows)
                s = dot(keys[here, :], queries[h], NT)
                if j == i:
                    s = jnp.where(key_row <= query_row, s, MASKED)
                p = jnp.exp(s - shift)
                g = dot(values[here, :], grads[h], NT)
                delta = delta + (p * g).sum(axis=0, keepdims=True)
                probs.append(p)
                weighted.append(g)
            part = jnp.zeros((head_size, rows), F32)
            for j in range(i + 1):
                here = slice(j * rows, (j + 1) * rows)
                ds = (probs[j] * (weighted[j] - delta)).astype(BF)
                p = probs[j].astype(BF)
                key_part = dot(ds, queries[h], NN)
                value_part = dot(p, grads[h], NN)
                if h == 0 and j == i:
                    key_sum[here, :] = key_part
                    value_sum[here, :] = value_part
                else:
                    key_sum[here, :] += key_part
                    value_sum[here, :] += value_part
                part = part + dot(keys_t[h * head_size : (h + 1) * head_size, here], ds, NN)
            query_parts.append(part)
        out[slot, :width] = (jnp.concatenate(query_parts, axis=0) * scale).T.astype(BF)

    query = qkv[0:rows, 3 * width + 2 * head_size : 3 * width + 3 * head_size]
    grad_out = tail_grad[...]
    probs, weighted = [], []
    delta = jnp.zeros((1, rows), F32)
    for j in range(blocks):
        here = slice(j * rows, (j + 1) * rows)
        s = dot(tail_kv[here, :head_size], query, NT)
        s = jnp.where(j * rows + key_row <= me * rows + query_row, s, MASKED)
        p = jnp.exp(s - tail_log[...])
        g = dot(tail_kv[here, head_size:], grad_out, NT)
        delta = delta + (p * g).sum(axis=0, keepdims=True)
        probs.append(p)
        weighted.append(g)
    part = jnp.zeros((head_size, rows), F32)
    for j in range(blocks):
        here = slice(j * rows, (j + 1) * rows)
        slot = pl.ds(pl.multiple_of((me ^ j) * rows, rows), rows)
        ds = (probs[j] * (weighted[j] - delta)).astype(BF)
        key_part = dot(ds, query, NN)
        value_part = dot(probs[j].astype(BF), grad_out, NN)
        part = part + dot(keys_t[width : width + head_size, here], ds, NN)
        out[slot, width : 2 * width] = key_sum[here, :].astype(BF)
        out[slot, 2 * width : 3 * width] = value_sum[here, :].astype(BF)
        out[slot, 3 * width : 3 * width + 2 * head_size] = jnp.concatenate(
            (key_part, value_part), axis=1
        ).astype(BF)
    tail_columns = slice(3 * width + 2 * head_size, 3 * width + 3 * head_size)
    out[0:rows, tail_columns] = (part * scale).T.astype(BF)
    for j in range(1, blocks):
        out[j * rows : (j + 1) * rows, tail_columns] = jnp.zeros((rows, head_size), BF)


def attend_back(place, qkv, grad, tail_grad, log, tail_log, blocks, rows, heads, head_size):
    width = heads * head_size
    length = blocks * rows
    return pl.pallas_call(
        functools.partial(attend_back_kernel, blocks, rows, heads, head_size),
        out_shape=jax.ShapeDtypeStruct(qkv.shape, BF),
        in_specs=[pl.BlockSpec(memory_space=pltpu.SMEM)]
        + [pl.BlockSpec(memory_space=pltpu.VMEM)] * 5,
        out_specs=pl.BlockSpec(memory_space=pltpu.VMEM),
        scratch_shapes=[
            pltpu.VMEM((length, width), BF),
            pltpu.VMEM((length, width), BF),
            pltpu.VMEM((width + 2 * head_size, length), BF),
            pltpu.VMEM((length, 2 * head_size), BF),
            pltpu.VMEM((length, width), F32),
            pltpu.VMEM((length, width), F32),
            pltpu.VMEM((length, head_size), F32),
            pltpu.VMEM((length, head_size), F32),
        ],
        compiler_params=pltpu.CompilerParams(vmem_limit_bytes=VMEM_BYTES),
        cost_estimate=pl.CostEstimate(
            flops=10 * 10 * length * length * width, bytes_accessed=9 * length * width, transcendentals=0
        ),
    )(place, qkv, grad, tail_grad, log, tail_log)


def mlp_kernel(
    normed, grad, up, down, bias, hidden_out, grad_pre_out, part_out, grad_part_out, bias_out
):
    pre = dot(normed[...], up[...], NN) + bias[...]
    bell = jnp.exp(-0.5 * pre * pre) * 0.3989422804014327
    below = 0.5 + 0.5 * lax.erf(pre * 0.7071067811865476)
    hidden = (pre * below).astype(BF)
    hidden_out[...] = hidden
    part_out[...] = dot(hidden, down[...], NN).astype(BF)
    grad_pre = ((below + pre * bell) * dot(grad[...], down[...], NT)).astype(BF)
    grad_pre_out[...] = grad_pre
    grad_part_out[...] = dot(grad_pre, up[...], NT).astype(BF)
    sums = grad_pre.astype(F32).sum(axis=0, keepdims=True)

    @pl.when(pl.program_id(0) == 0)
    def _():
        bias_out[...] = sums

    @pl.when(pl.program_id(0) > 0)
    def _():
        bias_out[...] += sums


def mlp(normed, grad, up, down, bias, rows):
    length, wide = normed.shape
    hidden = up.shape[1]
    row_block = pl.BlockSpec((rows, wide), lambda i: (i, 0))
    hidden_block = pl.BlockSpec((rows, hidden), lambda i: (i, 0))
    whole = pl.BlockSpec(memory_space=pltpu.VMEM)
    return pl.pallas_call(
        mlp_kernel,
        grid=(length // rows,),
        out_shape=(
            jax.ShapeDtypeStruct((length, hidden), BF),
            jax.ShapeDtypeStruct((length, hidden), BF),
            jax.ShapeDtypeStruct((length, wide), BF),
            jax.ShapeDtypeStruct((length, wide), BF),
            jax.ShapeDtypeStruct((1, hidden), F32),
        ),
        in_specs=[row_block, row_block, whole, whole, whole],
        out_specs=(
            hidden_block,
            hidden_block,
            row_block,
            row_block,
            pl.BlockSpec((1, hidden), lambda i: (0, 0)),
        ),
        compiler_params=pltpu.CompilerParams(vmem_limit_bytes=VMEM_BYTES),
        cost_estimate=pl.CostEstimate(
            flops=12 * length * wide * hidden,
            bytes_accessed=2 * (6 * length * wide + 2 * wide * hidden),
            transcendentals=0,
        ),
    )(normed, grad, up, down, bias)


def general_device(
    layer_input,
    output_grad,
    attn_gain,
    attn_shift,
    merged_weight,
    query_bias,
    value_bias,
    out_weight,
    out_bias,
    mlp_gain,
    mlp_shift,
    up_weight,
    up_bias,
    down_weight,
    down_bias,
):
    micros = layer_input.shape[0]
    rows = layer_input.shape[2]
    wide = layer_input.shape[3]
    head_size = wide // HEADS
    blocks = lax.axis_size("ctx")
    shards = lax.axis_size("fsdp")
    me = lax.axis_index("ctx")
    heads = HEADS // blocks
    width = heads * head_size
    main = blocks * width
    own = merged_weight.shape[0]
    hidden = up_weight.shape[1]
    piece = hidden // shards // blocks
    quads = hidden // wide
    used = 3 * width + 3 * head_size
    assert HEADS - heads * blocks == 1
    place = me.astype(jnp.int32).reshape(1)
    relative = jnp.arange(blocks, dtype=jnp.int32) ^ me
    start = me * width

    vectors = jnp.concatenate(
        (
            attn_gain,
            attn_shift,
            query_bias,
            value_bias,
            out_bias,
            mlp_gain,
            mlp_shift,
            down_bias,
            up_bias,
        )
    ).reshape(8 + quads, own)
    first = jnp.concatenate(
        (
            lax.dynamic_slice_in_dim(merged_weight, start, width, 1),
            lax.dynamic_slice_in_dim(merged_weight, wide + start, width, 1),
            lax.dynamic_slice_in_dim(merged_weight, 2 * wide + start, width, 1),
            merged_weight[:, wide + main : 2 * wide],
            merged_weight[:, 2 * wide + main :],
            merged_weight[:, main:wide],
            vectors.T,
        ),
        axis=1,
    )
    first = lax.all_gather(first, "fsdp", axis=0, tiled=True)
    merged_own = first[:, :used]
    vectors = first[:, used:].T.astype(F32)
    gain_one, shift_one, query_row, value_row, out_row, gain_two, shift_two, down_row = [
        vectors[i] for i in range(8)
    ]
    up_row = (
        vectors[8:]
        .reshape(quads, shards, own)
        .transpose(1, 0, 2)
        .reshape(shards, blocks, piece)
    )
    up_row = lax.dynamic_index_in_dim(up_row, me, 1, keepdims=False).reshape(1, shards * piece)
    zero_tail = jnp.zeros((head_size,), F32)
    merged_row = jnp.concatenate(
        (
            lax.dynamic_slice_in_dim(query_row, start, width),
            jnp.zeros((width,), F32),
            lax.dynamic_slice_in_dim(value_row, start, width),
            zero_tail,
            value_row[main:],
            query_row[main:],
        )
    )
    scale_row = jnp.concatenate(
        (
            jnp.full((width,), head_size**-0.5, BF),
            jnp.ones((2 * width + 2 * head_size,), BF),
            jnp.full((head_size,), head_size**-0.5, BF),
        )
    )
    out_full = lax.all_gather(out_weight, "fsdp", axis=0, tiled=True)
    up_own = lax.dynamic_index_in_dim(
        up_weight.reshape(own, shards, blocks, piece), me, 2, keepdims=False
    ).reshape(own, shards * piece)
    down_own = lax.dynamic_slice_in_dim(down_weight, me * piece, piece, 0)
    up_own = lax.all_gather(up_own, "fsdp", axis=0, tiled=True)
    down_own = lax.all_gather(down_own, "fsdp", axis=0, tiled=True)

    values = [layer_input[m, 0] for m in range(micros)]
    values_ctx = [gather_ctx(v) for v in values]
    grads = [output_grad[m, 0] for m in range(micros)]
    grads_ctx = [jnp.concatenate(gather_ctx(g)) for g in grads]

    unscaled, normed, qkv, log, tail_log, attended, middle, normed_two = ([] for _ in range(8))
    for m in range(micros):
        centred, rate = normal(jnp.concatenate(values_ctx[m]).astype(F32))
        unscaled.append((centred, rate))
        normed.append((centred * gain_one + shift_one).astype(BF))
        rows_out = jnp.dot(normed[m], merged_own, preferred_element_type=F32) + merged_row
        qkv.append(rows_out.astype(BF) * scale_row)
        out, tail_out, total, tail_total = attend(place, qkv[m], blocks, rows, heads, head_size)
        log.append(total)
        tail_log.append(tail_total)
        traded = jnp.stack(trade_ctx(list(out.reshape(blocks, rows, width))))
        traded = jnp.take(traded, relative, axis=0).transpose(1, 0, 2).reshape(rows, main)
        attended.append(jnp.concatenate((traded, tail_out), axis=1))
        middle.append(
            values[m].astype(F32)
            + jnp.dot(attended[m], out_full, preferred_element_type=F32)
            + out_row
        )
        centred, rate = normal(middle[m])
        normed_two.append((centred * gain_two + shift_two).astype(BF))

    hiddens, grad_pres, normed_two_ctx, layer_output, grad_middle = ([] for _ in range(5))
    grad_up_row = 0.0
    grad_gain_two = 0.0
    grad_shift_two = 0.0
    for m in range(micros):
        normed_two_ctx.append(jnp.concatenate(gather_ctx(normed_two[m])))
        act, grad_pre, part, grad_part, bias_part = mlp(
            normed_two_ctx[m], grads_ctx[m], up_own, down_own, up_row, rows
        )
        hiddens.append(act)
        grad_pres.append(grad_pre)
        grad_up_row = grad_up_row + bias_part
        grad_normed = reduce_ctx(list(grad_part.reshape(blocks, rows, wide)))
        centred, rate = normal(middle[m])
        grad_gain_two = grad_gain_two + jnp.sum(grad_normed * centred, axis=0)
        grad_shift_two = grad_shift_two + jnp.sum(grad_normed, axis=0)
        grad_middle.append(
            grads[m].astype(F32) + norm_back(centred, rate, grad_normed * gain_two)
        )
        total = reduce_ctx(list(part.reshape(blocks, rows, wide)))
        layer_output.append((middle[m] + total + down_row).astype(BF))
    grad_down = sum(dot(a, g, ((0,), (0,))) for a, g in zip(hiddens, grads_ctx, strict=True))
    grad_up = sum(dot(n, g, ((0,), (0,))) for n, g in zip(normed_two_ctx, grad_pres, strict=True))
    grad_down = lax.psum_scatter(grad_down.astype(BF), "fsdp", scatter_dimension=0, tiled=True)
    grad_up = lax.psum_scatter(grad_up.astype(BF), "fsdp", scatter_dimension=0, tiled=True)

    grad_out_weight = 0.0
    grad_out_row = 0.0
    grad_down_row = 0.0
    grad_merged = 0.0
    grad_merged_row = 0.0
    grad_gain_one = 0.0
    grad_shift_one = 0.0
    input_grad = []
    for m in range(micros):
        grad_attn = grad_middle[m].astype(BF)
        grad_out_weight = grad_out_weight + dot(attended[m], grad_attn, ((0,), (0,)))
        grad_out_row = grad_out_row + jnp.sum(grad_attn.astype(F32), axis=0)
        grad_down_row = grad_down_row + jnp.sum(grads[m].astype(F32), axis=0)
        grad_attended = dot(grad_attn, out_full, NT).astype(BF)
        to_trade = grad_attended[:, :main].reshape(rows, blocks, width).transpose(1, 0, 2)
        to_trade = jnp.take(to_trade, relative, axis=0)
        traded = jnp.concatenate(trade_ctx(list(to_trade)))
        grad_qkv = attend_back(
            place,
            qkv[m],
            traded,
            grad_attended[:, main:],
            log[m],
            tail_log[m],
            blocks,
            rows,
            heads,
            head_size,
        )
        grad_merged = grad_merged + dot(normed[m], grad_qkv, ((0,), (0,)))
        grad_merged_row = grad_merged_row + jnp.sum(grad_qkv.astype(F32), axis=0)
        grad_part = dot(grad_qkv, merged_own, NT)
        centred, rate = unscaled[m]
        grad_gain_one = grad_gain_one + jnp.sum(grad_part * centred, axis=0)
        grad_shift_one = grad_shift_one + jnp.sum(grad_part, axis=0)
        grad_normed = reduce_ctx(list(grad_part.astype(BF).reshape(blocks, rows, wide)))
        input_grad.append(
            grad_middle[m] + norm_back(centred[:rows], rate[:rows], grad_normed * gain_one)
        )

    def placed(part, tail):
        row = lax.dynamic_update_slice_in_dim(jnp.zeros((main,), F32), part, start, 0)
        return jnp.concatenate((row, tail))

    up_sums = lax.dynamic_update_slice_in_dim(
        jnp.zeros((shards, blocks, piece), F32), grad_up_row.reshape(shards, 1, piece), me, 1
    )
    up_sums = up_sums.reshape(shards, quads, own).transpose(1, 0, 2).reshape(quads, wide)
    vector_sums = jnp.concatenate(
        (
            jnp.stack(
                (
                    grad_gain_one,
                    grad_shift_one,
                    placed(grad_merged_row[:width], grad_merged_row[used - head_size :]),
                    placed(
                        grad_merged_row[2 * width : 3 * width],
                        grad_merged_row[3 * width + head_size : 3 * width + 2 * head_size],
                    ),
                    grad_out_row,
                    grad_gain_two,
                    grad_shift_two,
                    grad_down_row,
                )
            ),
            up_sums,
        )
    )
    last = jnp.concatenate((grad_merged, vector_sums.T), axis=1).astype(BF)
    last = lax.psum_scatter(last, "fsdp", scatter_dimension=0, tiled=True)
    grad_out_weight = lax.psum_scatter(
        grad_out_weight.astype(BF), "fsdp", scatter_dimension=0, tiled=True
    ).astype(F32)
    bit = 1
    while bit < blocks:
        grad_out_weight = grad_out_weight + swap(grad_out_weight.astype(BF), bit).astype(F32)
        bit *= 2

    def absolute(parts):
        return jnp.take(jnp.stack(parts), relative, axis=0).astype(F32)

    last = absolute(gather_ctx(last))
    tails = jnp.sum(last[:, :, 3 * width :], axis=0)

    def columns(index, tail):
        body = last[:, :, index * width : (index + 1) * width].transpose(1, 0, 2)
        return [body.reshape(own, main), tails[:, tail * head_size : (tail + 1) * head_size]]

    grad_merged = jnp.concatenate(columns(0, 2) + columns(1, 0) + columns(2, 1), axis=1)
    vector_sums = tails[:, 3 * head_size :].T
    grad_up = absolute(gather_ctx(grad_up)).reshape(blocks, own, shards, piece)
    grad_up = grad_up.transpose(1, 2, 0, 3).reshape(own, hidden)
    grad_down = absolute(gather_ctx(grad_down)).reshape(blocks * piece, wide)
    return (
        jnp.stack(layer_output)[:, None],
        jnp.stack(input_grad)[:, None],
        vector_sums[0],
        vector_sums[1],
        grad_merged,
        vector_sums[2],
        vector_sums[3],
        grad_out_weight,
        vector_sums[4],
        vector_sums[5],
        vector_sums[6],
        grad_up,
        vector_sums[8:].reshape(quads * own),
        grad_down,
        vector_sums[7],
    )


def gather_blocks(array):
    one = swap(array, 1)
    two = swap(array, 2)
    fourth = [swap(two[m], 1) if m % 2 == 0 else swap(one[m], 2) for m in range(array.shape[0])]
    return [array, one, two], fourth


def exchange(parts):
    return lax.all_to_all(parts, "ctx", 0, 0, tiled=True)


def trade_four(parts):
    return [parts[0]] + [swap(parts[r], r) for r in range(1, 4)]


def gather_four(block, which):
    one = swap(block, 1)
    two = swap(block, 2)
    return [block, one, two, swap(two, 1) if which % 2 == 0 else swap(one, 2)]


class Reduction:
    def __init__(self, parts, which):
        self.parts = parts
        self.near, self.far = (1, 2) if which % 2 == 0 else (2, 1)
        self.coming = swap(parts[3], self.near)

    def relay(self, after):
        parts = self.parts
        self.through, straight = relay(parts[self.far], self.coming, parts[self.near], after)
        self.got = [parts[0], swap(self.through, self.far), swap(straight, self.near)]
        return self.through


def whole_spec():
    return pl.BlockSpec(memory_space=pltpu.VMEM)


def scalar_spec():
    return pl.BlockSpec(memory_space=pltpu.SMEM)


def any_spec():
    return pl.BlockSpec(memory_space=pl.ANY)


def micro_spec(shape, which):
    return pl.BlockSpec((1,) + tuple(shape[1:]), lambda i: (which, 0, 0))


def call(kernel, operands, in_specs, outs, out_specs, flops, scratch=(), after=(), old=None):
    extra = list(after)
    aliases = {}
    for index, array in (old or {}).items():
        aliases[len(operands) + len(extra)] = index
        extra.append(array)
    count = len(operands)

    def body(*refs):
        kernel(*refs[:count], *refs[count + len(extra) :])

    moved = sum(o.size * o.dtype.itemsize for o in (*operands, *outs))
    return pl.pallas_call(
        body,
        grid=(1,),
        out_shape=tuple(outs),
        in_specs=list(in_specs) + [any_spec()] * len(extra),
        out_specs=tuple(out_specs),
        scratch_shapes=list(scratch),
        input_output_aliases=aliases,
        compiler_params=pltpu.CompilerParams(vmem_limit_bytes=VMEM_BYTES),
        cost_estimate=pl.CostEstimate(
            flops=COST * flops, bytes_accessed=COST * moved, transcendentals=0
        ),
    )(*operands, *extra)


def shape(*sizes, dtype=BF):
    return jax.ShapeDtypeStruct(sizes, dtype)


def relay_kernel(mine, got, out):
    out[...] = add_f32(mine[...], got[...]).astype(BF)


def relay(mine, got, held, after):
    wide, rows = mine.shape
    return pl.pallas_call(
        lambda mine, got, held, *refs: relay_kernel(mine, got, refs[-2]),
        out_shape=(shape(wide, rows), shape(*held.shape)),
        in_specs=[whole_spec(), whole_spec()] + [any_spec()] * (1 + len(after)),
        out_specs=(whole_spec(), any_spec()),
        input_output_aliases={2: 1},
        compiler_params=pltpu.CompilerParams(vmem_limit_bytes=VMEM_BYTES),
        cost_estimate=pl.CostEstimate(
            flops=wide * rows, bytes_accessed=6 * wide * rows, transcendentals=0
        ),
    )(mine, got, held, *after)


def pass_kernel(source, out):
    out[...] = source[...]


def pass_micro_kernel(source, out):
    out[...] = source[0]


def pass_micro(array, which, after):
    return call(
        pass_micro_kernel,
        [array],
        [micro_spec(array.shape, which)],
        [shape(*array.shape[1:])],
        [whole_spec()],
        0,
        after=after,
    )[0]


def pass_on(array, after):
    return call(
        pass_kernel,
        [array],
        [whole_spec()],
        [shape(*array.shape)],
        [whole_spec()],
        0,
        after=after,
    )[0]


def padded(columns):
    return (columns + 127) // 128 * 128


def pick_kernel(width, head_size, wide, place, weight, *refs):
    vectors, out = refs[:-1], refs[-1]
    own = out.shape[0]
    main = 4 * width
    for k in range(4):

        @pl.when(place[0] == k)
        def _(k=k):
            for part in range(3):
                begin = part * wide + k * width
                out[:, part * width : (part + 1) * width] = weight[:, begin : begin + width]

    for place_to, begin in enumerate((wide + main, 2 * wide + main, main)):
        at = 3 * width + place_to * head_size
        out[:, at : at + head_size] = weight[:, begin : begin + head_size]
    at = 3 * width + 3 * head_size
    rows = []
    for vector in vectors:
        row = vector[...].astype(F32).reshape(1, vector.shape[0])
        rows += [row[:, begin : begin + own] for begin in range(0, vector.shape[0], own)]
    row_id = lax.broadcasted_iota(jnp.int32, (len(rows), own), 0)
    table = jnp.zeros((len(rows), own), F32)
    for index, row in enumerate(rows):
        table = jnp.where(row_id == index, row, table)
    out[:, at:] = table.T.astype(BF)


def pick(place, weight, vectors, width, head_size):
    own, wide = weight.shape[0], weight.shape[1] // 3
    columns = 3 * width + 3 * head_size + sum(v.shape[0] for v in vectors) // own
    return call(
        functools.partial(pick_kernel, width, head_size, wide),
        [place, weight, *vectors],
        [scalar_spec()] + [whole_spec()] * (1 + len(vectors)),
        [shape(own, columns)],
        [whole_spec()],
        0,
    )[0]


def pick_hidden_kernel(shards, piece, second, place, up, down, out):
    for k in range(4):

        @pl.when(place[0] == k)
        def _(k=k):
            for f in range(shards):
                begin = (f * 4 + k) * piece
                out[:, f * piece : (f + 1) * piece] = up[:, begin : begin + piece]

    rows = out.shape[0]
    filled = shards * piece
    out[:, filled:second] = jnp.zeros((rows, second - filled), BF)
    out[:, second : second + down.shape[1]] = down[...]
    end = second + down.shape[1]
    out[:, end:] = jnp.zeros((rows, out.shape[1] - end), BF)


def pick_hidden(place, up, down, shards, piece, after=()):
    own = up.shape[0]
    second = padded(shards * piece)
    return call(
        functools.partial(pick_hidden_kernel, shards, piece, second),
        [place, up, down],
        [scalar_spec(), whole_spec(), whole_spec()],
        [shape(own, second + padded(down.shape[1]))],
        [whole_spec()],
        0,
        after=after,
    )[0]


def feature_mean(v):
    return jnp.sum(v, axis=0, keepdims=True) * (1.0 / v.shape[0])


def normal_columns(values):
    centre = values - feature_mean(values)
    rate = lax.rsqrt(feature_mean(centre * centre) + EPSILON)
    return centre * rate, rate


def norm_back_columns(normed, rate, scaled):
    return rate * (scaled - feature_mean(scaled) - normed * feature_mean(scaled * normed))


def column(vectors, index):
    return vectors[:, index : index + 1].astype(F32)


def front_kernel(heads, head_size, first_call, place, *refs):
    x = refs[:4]
    weight, vectors = refs[4:6]
    refs = refs[6:]
    if first_call:
        normed_out, qkv, attended, tail_out, log, tail_log, turned, keys = refs
        turned[...] = weight[:, : turned.shape[0]].T
    else:
        turned, normed_out, qkv, attended, tail_out, log, tail_log, keys = refs
    wide, rows = x[3].shape
    width = heads * head_size
    used = 3 * width + 3 * head_size
    me = place[0]
    gain, shift = column(vectors, 0), column(vectors, 1)
    mine = pl.ds(pl.multiple_of(me * width, width), width)
    query_bias = vectors[mine, 2:3].astype(F32)
    value_bias = vectors[mine, 3:4].astype(F32)
    last = slice(4 * width, 4 * width + head_size)
    bias = jnp.concatenate(
        (
            query_bias,
            jnp.zeros((width, 1), F32),
            value_bias,
            jnp.zeros((head_size, 1), F32),
            vectors[last, 3:4].astype(F32),
            vectors[last, 2:3].astype(F32),
        ),
        axis=0,
    )
    row = lax.broadcasted_iota(jnp.int32, (used, 1), 0)
    scale = jnp.where((row < width) | (row >= used - head_size), head_size**-0.5, 1.0)
    for r in range(4):
        normed, _ = normal_columns((x[r][...] if r == 3 else x[r][0]).astype(F32))
        normed_out[:, r * rows : (r + 1) * rows] = normed.astype(BF)
        full = (normed * gain + shift).astype(BF)
        projected = dot(turned[...], full, NN) + bias
        projected = (projected.astype(BF).astype(F32) * scale).astype(BF)
        qkv[:, r * rows : (r + 1) * rows] = projected
        here = slice(r * rows, (r + 1) * rows)
        keys[here, :width] = projected[width : 2 * width, :].T
        keys[here, width:] = projected[3 * width : 3 * width + 2 * head_size, :].T
    key_row = lax.broadcasted_iota(jnp.int32, (rows, rows), 0)
    query_row = lax.broadcasted_iota(jnp.int32, (rows, rows), 1)
    head_row = lax.broadcasted_iota(jnp.int32, (width, rows), 0) // head_size

    def slot(j):
        return pl.ds(pl.multiple_of((me ^ j) * rows, rows), rows)

    def softmax_values(scores, value_rows):
        peak = scores[0].max(axis=0, keepdims=True)
        for s in scores[1:]:
            peak = jnp.maximum(peak, s.max(axis=0, keepdims=True))
        total = jnp.zeros((1, rows), F32)
        product = jnp.zeros((head_size, rows), F32)
        for j, s in enumerate(scores):
            e = jnp.exp(s - peak)
            total = total + e.sum(axis=0, keepdims=True)
            product = product + dot(qkv[value_rows, slot(j)], e.astype(BF), NN)
        return product / total, peak + jnp.log(total)

    for i in range(4):
        query = qkv[:width, slot(i)]
        for h in range(heads):
            masked = jnp.where(head_row == h, query, jnp.zeros_like(query))
            scores = []
            for j in range(i + 1):
                s = dot(keys[slot(j), :width], masked, NN)
                if j == i:
                    s = jnp.where(key_row <= query_row, s, MASKED)
                scores.append(s)
            begin = 2 * width + h * head_size
            product, total = softmax_values(scores, slice(begin, begin + head_size))
            attended[i, h * head_size : (h + 1) * head_size, :] = product.astype(BF)
            log[h : h + 1, i * rows : (i + 1) * rows] = total
    begin = 3 * width + head_size
    query = qkv[begin + head_size :, 0:rows]
    query = jnp.concatenate((query, jnp.zeros_like(query)), axis=0)
    scores = []
    for j in range(4):
        s = dot(keys[slot(j), width:], query, NN)
        scores.append(jnp.where(j * rows + key_row <= me * rows + query_row, s, MASKED))
    product, total = softmax_values(scores, slice(begin, begin + head_size))
    tail_out[...] = product.astype(BF)
    tail_log[...] = total


def front(place, x, fourth, which, weight, vectors, turned, heads, head_size, after=()):
    wide, rows = fourth.shape
    length = 4 * rows
    width = heads * head_size
    used = 3 * width + 3 * head_size
    first_call = turned is None
    outs = [
        shape(wide, length),
        shape(used, length),
        shape(4, width, rows),
        shape(head_size, rows),
        shape(heads, length, dtype=F32),
        shape(1, rows, dtype=F32),
    ]
    operands = [place, *x, fourth, weight, vectors]
    in_specs = [scalar_spec()] + [micro_spec(x[0].shape, which)] * 3 + [whole_spec()] * 3
    if first_call:
        outs.append(shape(used, wide))
    else:
        operands.append(turned)
        in_specs.append(whole_spec())
    return call(
        functools.partial(front_kernel, heads, head_size, first_call),
        operands,
        in_specs,
        outs,
        [whole_spec()] * len(outs),
        12_000_000_000,
        scratch=[pltpu.VMEM((length, width + 2 * head_size), BF)],
        after=after,
    )


def middle_kernel(first_call, traded, tail, x, weight, vectors, *refs):
    if first_call:
        middle, normed_two, attended, turned = refs
        turned[...] = weight[...].T
    else:
        turned, middle, normed_two, attended = refs
    width = traded.shape[1]
    for j in range(4):
        attended[0, j * width : (j + 1) * width, :] = traded[j]
    attended[0, 4 * width :, :] = tail[...]
    sums = x[0].astype(F32) + dot(turned[...], attended[0], NN) + column(vectors, 4)
    middle[...] = sums
    normed, _ = normal_columns(sums)
    normed_two[...] = (normed * column(vectors, 5) + column(vectors, 6)).astype(BF)


def middle_part(
    traded, tail, x, which, weight, vectors, turned, attended, after=()
):
    micros, wide, rows = x.shape
    first_call = turned is None
    operands = [traded, tail, x, weight, vectors]
    in_specs = [whole_spec()] * 2 + [micro_spec(x.shape, which)] + [whole_spec()] * 2
    outs = [shape(wide, rows, dtype=F32), shape(wide, rows), shape(*x.shape)]
    out_specs = [whole_spec(), whole_spec(), micro_spec(x.shape, which)]
    if first_call:
        outs.append(shape(weight.shape[1], weight.shape[0]))
        out_specs.append(whole_spec())
    else:
        operands.append(turned)
        in_specs.append(whole_spec())
    return call(
        functools.partial(middle_kernel, first_call),
        operands,
        in_specs,
        outs,
        out_specs,
        2 * rows * wide * wide,
        after=after,
        old=None if attended is None else {2: attended},
    )


def feed_kernel(second, first_call, place, *refs):
    normed = refs[:4]
    grad = refs[4:8]
    weights, vectors = refs[8:10]
    refs = refs[10:]
    if first_call:
        kept_hidden, kept_grad_pre = refs[:2]
        grad_parts = refs[2:6]
        bias_out, up_turned = refs[6:]
    else:
        up_turned, kept_hidden, kept_grad_pre = refs[:3]
        grad_parts = refs[3:7]
        bias_out = refs[7]
    wide, rows = normed[0].shape
    hidden_size = up_turned.shape[0]
    if first_call:
        up_turned[...] = weights[:, :hidden_size].T
    lane = lax.broadcasted_iota(jnp.int32, (hidden_size, 4), 1)
    bias = jnp.where(lane == place[0], vectors[:, 8:12].astype(F32), 0.0)
    bias = bias.sum(axis=1, keepdims=True)
    total = jnp.zeros((hidden_size, rows), F32)
    for r in range(4):
        here = slice(r * rows, (r + 1) * rows)
        pre = dot(up_turned[...], normed[r][...], NN) + bias
        bell = jnp.exp(-0.5 * pre * pre) * 0.3989422804014327
        below = 0.5 + 0.5 * lax.erf(pre * 0.7071067811865476)
        kept_hidden[:, here] = (pre * below).astype(BF)
        back = grad[r][...] if r == 3 else grad[r][0]
        grad_pre = (below + pre * bell) * dot(weights[:, second : second + wide], back, NN)
        grad_pre = grad_pre.astype(BF)
        kept_grad_pre[:, here] = grad_pre
        grad_parts[r][...] = dot(weights[:, :hidden_size], grad_pre, NN).astype(BF)
        total = total + grad_pre.astype(F32)
    bias_out[...] = total.sum(axis=1, keepdims=True)


def feed(place, normed, grads, fourth, which, weights, vectors, turned, after=()):
    wide, rows = fourth.shape
    hidden_size = weights.shape[0]
    second = padded(hidden_size)
    length = 4 * rows
    first_call = turned is None
    operands = [place, *normed, *grads, fourth, weights, vectors]
    in_specs = [scalar_spec()] + [whole_spec()] * 4
    in_specs += [micro_spec(grads[0].shape, which)] * 3 + [whole_spec()] * 3
    outs = [shape(hidden_size, length)] * 2 + [shape(wide, rows)] * 4
    outs.append(shape(hidden_size, 1, dtype=F32))
    if first_call:
        outs.append(shape(hidden_size, wide))
    else:
        operands.append(turned)
        in_specs.append(whole_spec())
    return call(
        functools.partial(feed_kernel, second, first_call),
        operands,
        in_specs,
        outs,
        [whole_spec()] * len(outs),
        6 * length * wide * hidden_size,
        after=after,
    )


def feed_out_kernel(second, micros, *refs):
    hiddens, weights = refs[:micros], refs[micros]
    parts, turned = refs[micros + 1 : -1], refs[-1]
    turned[...] = weights[:, second : second + turned.shape[0]].T
    rows = parts[0].shape[1]
    for m in range(micros):
        for r in range(4):
            here = slice(r * rows, (r + 1) * rows)
            parts[4 * m + r][...] = dot(turned[...], hiddens[m][:, here], NN).astype(BF)


def feed_out(hiddens, weights, wide, after=()):
    micros = len(hiddens)
    hidden_size, length = hiddens[0].shape
    return call(
        functools.partial(feed_out_kernel, padded(hidden_size), micros),
        [*hiddens, weights],
        [whole_spec()] * (micros + 1),
        [shape(wide, length // 4)] * (4 * micros),
        [whole_spec()] * (4 * micros),
        2 * micros * length * wide * hidden_size,
        scratch=[pltpu.VMEM((wide, hidden_size), BF)],
        after=after,
    )


def weights_kernel(second, micros, *refs):
    hiddens, grad_pres = refs[:micros], refs[micros : 2 * micros]
    normeds = refs[2 * micros : 6 * micros]
    grads = refs[6 * micros : 9 * micros]
    fourths = refs[9 * micros : 10 * micros]
    out, left, right = refs[10 * micros :]
    wide, rows = fourths[0].shape
    hidden_size, length = hiddens[0].shape
    for m in range(micros):
        for r in range(4):
            here = slice(m * length + r * rows, m * length + (r + 1) * rows)
            left[:, here] = normeds[4 * m + r][...]
        right[:, m * length : (m + 1) * length] = grad_pres[m][...]
    out[:, :hidden_size] = dot(left[...], right[...], NT).astype(BF)
    out[:, hidden_size:second] = jnp.zeros((wide, second - hidden_size), BF)
    for m in range(micros):
        left[:, m * length : (m + 1) * length] = hiddens[m][...]
        for r in range(4):
            here = slice(m * length + r * rows, m * length + (r + 1) * rows)
            right[:, here] = fourths[m][...] if r == 3 else grads[3 * m + r][0]
    out[:, second : second + wide] = dot(left[...], right[...], NT).astype(BF)
    end = second + wide
    out[:, end:] = jnp.zeros((wide, out.shape[1] - end), BF)


def weights_part(hiddens, grad_pres, normeds, grads, fourths, after=()):
    micros = len(hiddens)
    wide, rows = fourths[0].shape
    hidden_size, length = hiddens[0].shape
    second = padded(hidden_size)
    operands = [*hiddens, *grad_pres]
    for n in normeds:
        operands += list(n)
    in_specs = [whole_spec()] * len(operands)
    for m in range(micros):
        operands += list(grads)
        in_specs += [micro_spec(grads[0].shape, m)] * 3
    operands += list(fourths)
    in_specs += [whole_spec()] * micros
    return call(
        functools.partial(weights_kernel, second, micros),
        operands,
        in_specs,
        [shape(hidden_size, second + padded(wide))],
        [whole_spec()],
        4 * micros * length * wide * hidden_size,
        scratch=[pltpu.VMEM((wide, micros * length), BF)] * 2,
        after=after,
    )[0]


def turn_kernel(width, *refs):
    got = refs[:3]
    middle, grad, weight, vectors = refs[3:7]
    refs = refs[7:]
    grad_middle, grad_attn, traded, tail, sums = refs
    dy = grad[0].astype(F32)
    total = got[0][...].astype(F32) + got[1][...].astype(F32) + got[2][...].astype(F32)
    normed, rate = normal_columns(middle[...])
    result = dy + norm_back_columns(normed, rate, total * column(vectors, 5))
    grad_middle[...] = result
    low = result.astype(BF)
    grad_attn[0] = low
    for j in range(4):
        traded[j] = dot(weight[j * width : (j + 1) * width, :], low, NN).astype(BF)
    tail[...] = dot(weight[4 * width :, :], low, NN).astype(BF)
    sums[:, 0:1] = low.astype(F32).sum(axis=1, keepdims=True)
    sums[:, 1:2] = (total * normed).sum(axis=1, keepdims=True)
    sums[:, 2:3] = total.sum(axis=1, keepdims=True)
    sums[:, 3:4] = dy.sum(axis=1, keepdims=True)


def turn(got, middle, grads, which, weight, vectors, old, heads, head_size, after=()):
    wide, rows = middle.shape
    width = heads * head_size
    outs = [shape(wide, rows, dtype=F32), shape(*grads.shape), shape(4, width, rows)]
    outs += [shape(head_size, rows), shape(wide, 4, dtype=F32)]
    return call(
        functools.partial(turn_kernel, width),
        [*got, middle, grads, weight, vectors],
        [whole_spec()] * 4
        + [micro_spec(grads.shape, which)]
        + [whole_spec()] * 2,
        outs,
        [whole_spec(), micro_spec(grads.shape, which)] + [whole_spec()] * 3,
        2 * rows * wide * wide,
        after=after,
        old=None if old is None else {1: old},
    )


def rear_kernel(heads, head_size, place, *refs):
    qkv, traded, tail_grad, log, tail_log, weight = refs[:6]
    out = refs[6]
    parts = refs[7:11]
    sums = refs[11]
    keys, values, key_sum, value_sum = refs[12:]
    rows = tail_grad.shape[1]
    used = qkv.shape[0]
    width = heads * head_size
    me = place[0]
    scale = head_size**-0.5
    tail_at = 3 * width
    for r in range(4):
        here = slice(r * rows, (r + 1) * rows)
        keys[here, :width] = qkv[width : 2 * width, here].T
        keys[here, width:] = qkv[tail_at : tail_at + 2 * head_size, here].T
        values[here, :] = qkv[2 * width : 3 * width, here].T
    key_row = lax.broadcasted_iota(jnp.int32, (rows, rows), 0)
    query_row = lax.broadcasted_iota(jnp.int32, (rows, rows), 1)
    head_row = lax.broadcasted_iota(jnp.int32, (width, rows), 0) // head_size

    def slot(j):
        return pl.ds(pl.multiple_of((me ^ j) * rows, rows), rows)

    for i in range(4):
        query = qkv[:width, slot(i)]
        grad_out = traded[i]
        for h in range(heads):
            band = slice(h * head_size, (h + 1) * head_size)
            masked = jnp.where(head_row == h, query, jnp.zeros_like(query))
            masked_grad = jnp.where(head_row == h, grad_out, jnp.zeros_like(grad_out))
            shift = log[h : h + 1, i * rows : (i + 1) * rows]
            probs, weighted = [], []
            delta = jnp.zeros((1, rows), F32)
            for j in range(i + 1):
                s = dot(keys[slot(j), :width], masked, NN)
                if j == i:
                    s = jnp.where(key_row <= query_row, s, MASKED)
                p = jnp.exp(s - shift)
                g = dot(values[slot(j), :], masked_grad, NN)
                delta = delta + (p * g).sum(axis=0, keepdims=True)
                probs.append(p)
                weighted.append(g)
            part = jnp.zeros((head_size, rows), F32)
            for j in range(i + 1):
                here = slice(j * rows, (j + 1) * rows)
                ds = (probs[j] * (weighted[j] - delta)).astype(BF)
                p = probs[j].astype(BF)
                key_part = dot(query[band, :], ds, NT)
                value_part = dot(grad_out[band, :], p, NT)
                if j == i:
                    key_sum[band, here] = key_part
                    value_sum[band, here] = value_part
                else:
                    key_sum[band, here] += key_part
                    value_sum[band, here] += value_part
                at = width + h * head_size
                part = part + dot(qkv[at : at + head_size, slot(j)], ds, NN)
            out[band, slot(i)] = (part * scale).astype(BF)

    query = qkv[used - head_size :, 0:rows]
    grad_out = tail_grad[...]
    blank = jnp.zeros_like(query)
    wide_query = jnp.concatenate((query, blank), axis=0)
    wide_grad = jnp.concatenate((blank, grad_out), axis=0)
    probs, weighted = [], []
    delta = jnp.zeros((1, rows), F32)
    for j in range(4):
        s = dot(keys[slot(j), width:], wide_query, NN)
        s = jnp.where(j * rows + key_row <= me * rows + query_row, s, MASKED)
        p = jnp.exp(s - tail_log[...])
        g = dot(keys[slot(j), width:], wide_grad, NN)
        delta = delta + (p * g).sum(axis=0, keepdims=True)
        probs.append(p)
        weighted.append(g)
    part = jnp.zeros((head_size, rows), F32)
    for j in range(4):
        here = slice(j * rows, (j + 1) * rows)
        ds = (probs[j] * (weighted[j] - delta)).astype(BF)
        part = part + dot(qkv[tail_at : tail_at + head_size, slot(j)], ds, NN)
        out[tail_at : tail_at + head_size, slot(j)] = dot(query, ds, NT).astype(BF)
        out[tail_at + head_size : tail_at + 2 * head_size, slot(j)] = dot(
            grad_out, probs[j].astype(BF), NT
        ).astype(BF)
        out[width : 2 * width, slot(j)] = key_sum[:, here].astype(BF)
        out[2 * width : 3 * width, slot(j)] = value_sum[:, here].astype(BF)
    out[used - head_size :, 0:rows] = (part * scale).astype(BF)
    out[used - head_size :, rows:] = jnp.zeros((head_size, 3 * rows), BF)
    total = jnp.zeros((used, rows), F32)
    for r in range(4):
        block = out[:, r * rows : (r + 1) * rows]
        parts[r][...] = dot(weight[:, :used], block, NN).astype(BF)
        total = total + block.astype(F32)
    sums[...] = total.sum(axis=1, keepdims=True)


def rear(place, qkv, traded, tail_grad, log, tail_log, weight, heads, head_size, after=()):
    used, length = qkv.shape
    rows = tail_grad.shape[1]
    wide = weight.shape[0]
    width = heads * head_size
    outs = [shape(used, length)] + [shape(wide, rows)] * 4 + [shape(used, 1, dtype=F32)]
    return call(
        functools.partial(rear_kernel, heads, head_size),
        [place, qkv, traded, tail_grad, log, tail_log, weight],
        [scalar_spec()] + [whole_spec()] * 6,
        outs,
        [whole_spec()] * 6,
        20_000_000_000,
        scratch=[
            pltpu.VMEM((length, width + 2 * head_size), BF),
            pltpu.VMEM((length, width), BF),
            pltpu.VMEM((width, length), F32),
            pltpu.VMEM((width, length), F32),
        ],
        after=after,
    )


def merged_kernel(heads, head_size, micros, place, *refs):
    normeds, grads = refs[:micros], refs[micros : 2 * micros]
    columns, rows_of = refs[2 * micros : 3 * micros], refs[3 * micros : 4 * micros]
    ups = refs[4 * micros : 5 * micros]
    weight, vectors = refs[5 * micros : 5 * micros + 2]
    got = refs[5 * micros + 2 : 5 * micros + 5]
    out, small = refs[5 * micros + 5 :]
    used, length = grads[0].shape
    wide = normeds[0].shape[0]
    width = heads * head_size
    me = place[0]
    ones = jnp.ones((8, length), BF)
    product = dot(normeds[0][...], grads[0][...], NT)
    total = dot(ones, grads[0][...], NT)
    down_columns = columns[0][...]
    others = rows_of[0][...]
    up_sum = ups[0][...]
    for m in range(1, micros):
        product = product + dot(normeds[m][...], grads[m][...], NT)
        total = total + dot(ones, grads[m][...], NT)
        down_columns = down_columns + columns[m][...]
        others = others + rows_of[m][...]
        up_sum = up_sum + ups[m][...]
    total = total[0:1, :]
    matrix = weight[:, :used].astype(F32)
    out[:, :used] = (column(vectors, 0) * product + column(vectors, 1) * total).astype(BF)
    gain = (product * matrix).sum(axis=1, keepdims=True)
    shift = (matrix * total).sum(axis=1, keepdims=True)
    small[...] = jnp.zeros(small.shape, F32)
    mine = pl.ds(pl.multiple_of(me * width, width), width)
    small[:, 0:1] = gain
    small[:, 1:2] = shift
    small[mine, 2:3] = down_columns[:width, :]
    small[mine, 3:4] = down_columns[2 * width : 3 * width, :]
    small[4 * width :, 2:3] = down_columns[used - head_size :, :]
    small[4 * width :, 3:4] = down_columns[3 * width + head_size : 3 * width + 2 * head_size, :]
    small[:, 4:8] = others
    lane = lax.broadcasted_iota(jnp.int32, (wide, 4), 1)
    small[:, 8:12] = jnp.where(lane == me, up_sum, 0.0)
    end = weight.shape[1]
    out[:, used:end] = small[:, : end - used].astype(BF)
    total = got[0][...].astype(F32) + got[1][...].astype(F32) + got[2][...].astype(F32)
    out[:, end:] = total.astype(BF).T


def merged_part(
    place, normeds, grads, columns, rows_of, ups, weight, vectors, got, heads, head_size, after=()
):
    micros = len(normeds)
    wide, length = normeds[0].shape
    used = grads[0].shape[0]
    operands = [place, *normeds, *grads, *columns, *rows_of, *ups, weight, vectors, *got]
    return call(
        functools.partial(merged_kernel, heads, head_size, micros),
        operands,
        [scalar_spec()] + [whole_spec()] * (len(operands) - 1),
        [shape(wide, weight.shape[1] + got[0].shape[0])],
        [whole_spec()],
        2 * micros * length * wide * used,
        scratch=[pltpu.VMEM((wide, 128), F32)],
        after=after,
    )[0]


def out_weight_kernel(place, attended, grads, *outs):
    band_rows = outs[0].shape[0]
    for r in range(4):
        band = pl.ds(pl.multiple_of((place[0] ^ r) * band_rows, band_rows), band_rows)
        total = dot(grads[0, band, :], attended[0], NT)
        for m in range(1, attended.shape[0]):
            total = total + dot(grads[m, band, :], attended[m], NT)
        outs[r][...] = total.astype(BF)


def out_weight_part(place, attended, grads, after=()):
    micros, wide, rows = attended.shape
    return call(
        out_weight_kernel,
        [place, attended, grads],
        [scalar_spec()] + [whole_spec()] * 2,
        [shape(wide // 4, wide)] * 4,
        [whole_spec()] * 4,
        2 * micros * rows * wide * wide,
        after=after,
    )


def finish_input_kernel(got_one, got_two, got_three, x, grad_middle, vectors, out):
    total = got_one[...].astype(F32) + got_two[...].astype(F32) + got_three[...].astype(F32)
    normed, rate = normal_columns(x[0].astype(F32))
    out[0] = grad_middle[...] + norm_back_columns(normed, rate, total * column(vectors, 0))


def finish_output_kernel(got_one, got_two, got_three, middle, vectors, out):
    total = got_one[...].astype(F32) + got_two[...].astype(F32) + got_three[...].astype(F32)
    out[0] = (middle[...] + total + column(vectors, 7)).astype(BF)


def finish(kernel, got, x, rest, which, old, dims, dtype, after=()):
    operands = list(got)
    in_specs = [whole_spec()] * 3
    if x is not None:
        operands.append(x)
        in_specs.append(micro_spec(x.shape, which))
    operands += list(rest)
    in_specs += [whole_spec()] * len(rest)
    return call(
        kernel,
        operands,
        in_specs,
        [shape(*dims, dtype=dtype)],
        [micro_spec(dims, which)],
        20 * dims[1] * dims[2],
        after=after,
        old=None if old is None else {0: old},
    )[0]


def spread_kernel(piece, place, *refs):
    ups, downs = refs[:4], refs[4:8]
    grad_up, grad_down = refs[8:]
    shards = grad_up.shape[1] // (4 * piece)
    wide = grad_down.shape[1]
    for k in range(4):

        @pl.when(place[0] == k)
        def _(k=k):
            for j in range(4):
                source = ups[j ^ k]
                for f in range(shards):
                    at = (f * 4 + j) * piece
                    grad_up[:, at : at + piece] = source[:, f * piece : (f + 1) * piece].astype(F32)
                grad_down[j * piece : (j + 1) * piece, :] = downs[j ^ k][:, :wide].astype(F32)


def spread(place, halves, shards, piece, wide, after=()):
    own = halves[0][0].shape[0]
    return call(
        functools.partial(spread_kernel, piece),
        [place, *halves[0], *halves[1]],
        [scalar_spec()] + [whole_spec()] * 8,
        [shape(own, 4 * shards * piece, dtype=F32), shape(4 * piece, wide, dtype=F32)],
        [whole_spec()] * 2,
        0,
        after=after,
    )


def spread_heads_kernel(width, head_size, place, *refs):
    sources = refs[:4]
    grad_merged, grad_out = refs[4:6]
    rows = refs[6:]
    wide = grad_merged.shape[1] // 3
    band = wide // 4
    end = sources[0].shape[1] - band
    total = sources[0][:, 3 * width : end].astype(F32)
    for r in range(1, 4):
        total = total + sources[r][:, 3 * width : end].astype(F32)
    table = total[:, 3 * head_size :].T
    own = table.shape[1]
    for index, row in enumerate(rows):
        if index < 8:
            row[...] = table[index]
        else:
            for part in range(row.shape[0] // own):
                row[part * own : (part + 1) * own] = table[8 + part]
    for part, tail in enumerate((2, 0, 1)):
        at = part * wide + 4 * width
        grad_merged[:, at : at + head_size] = total[:, tail * head_size : (tail + 1) * head_size]
    for k in range(4):

        @pl.when(place[0] == k)
        def _(k=k):
            for j in range(4):
                source = sources[j ^ k]
                for part in range(3):
                    at = part * wide + j * width
                    grad_merged[:, at : at + width] = source[
                        :, part * width : (part + 1) * width
                    ].astype(F32)
                grad_out[:, j * band : (j + 1) * band] = source[:, end:].astype(F32)


def spread_heads(place, sources, width, head_size, wide, after=()):
    own, columns = sources[0].shape
    quads = columns - 3 * width - 3 * head_size - wide // 4 - 8
    return call(
        functools.partial(spread_heads_kernel, width, head_size),
        [place, *sources],
        [scalar_spec()] + [whole_spec()] * 4,
        [
            shape(own, 3 * wide, dtype=F32),
            shape(own, wide, dtype=F32),
        ]
        + [shape(own, dtype=F32)] * 8
        + [shape(own * quads, dtype=F32)],
        [whole_spec()] * 11,
        0,
        after=after,
    )


def on_device(
    layer_input,
    output_grad,
    attn_gain,
    attn_shift,
    merged_weight,
    query_bias,
    value_bias,
    out_weight,
    out_bias,
    mlp_gain,
    mlp_shift,
    up_weight,
    up_bias,
    down_weight,
    down_bias,
):
    micros, _, rows, wide = layer_input.shape
    head_size = wide // HEADS
    shards = lax.axis_size("fsdp")
    me = lax.axis_index("ctx")
    heads = HEADS // 4
    width = heads * head_size
    own = merged_weight.shape[0]
    hidden = up_weight.shape[1]
    piece = hidden // shards // 4
    quads = hidden // wide
    used = 3 * width + 3 * head_size
    place = me.astype(jnp.int32).reshape(1)
    x = layer_input.transpose(0, 1, 3, 2).reshape(micros, wide, rows)
    dy = output_grad.transpose(0, 1, 3, 2).reshape(micros, wide, rows)

    small = [
        attn_gain,
        attn_shift,
        query_bias,
        value_bias,
        out_bias,
        mlp_gain,
        mlp_shift,
        down_bias,
        up_bias,
    ]
    first = pick(place, merged_weight, small, width, head_size)
    x_ctx, x_fourth = gather_blocks(x)
    dy_ctx = [dy] + [swap(pass_on(dy, x_fourth), bit) for bit in (1, 2)]
    first = lax.all_gather(first, "fsdp", axis=0, tiled=True)
    vectors = first[:, used:]
    out_full = lax.all_gather(out_weight, "fsdp", axis=0, tiled=True)
    second = pick_hidden(
        place,
        up_weight,
        lax.dynamic_slice_in_dim(down_weight, me * piece, piece, 0),
        shards,
        piece,
        after=x_ctx[1:],
    )
    second = lax.all_gather(second, "fsdp", axis=0, tiled=True)

    done = []

    def then(*others):
        return (*done[-1:], *others)

    fronts = []
    for m in range(micros):
        fronts.append(
            front(
                place,
                x_ctx,
                x_fourth[m],
                m,
                first,
                vectors,
                fronts[0][6] if m else None,
                heads,
                head_size,
                after=then(),
            )
        )
        done.append(fronts[-1][0])
    dy_fourth = []
    for m in range(micros):
        bit = 1 if m % 2 == 0 else 2
        done.append(pass_micro(dy_ctx[3 - bit], m, then()))
        dy_fourth.append(swap(done[-1], bit))
    middles = []
    normed_two = []
    for m in range(micros):
        middles.append(
            middle_part(
                exchange(fronts[m][2]),
                fronts[m][3],
                x,
                m,
                out_full,
                vectors,
                middles[0][3] if m else None,
                middles[-1][2] if m else None,
                after=then(),
            )
        )
        done.append(middles[-1][0])
        normed_two.append(gather_four(middles[m][1], m))
    attended = middles[-1][2]
    middle = [result[0] for result in middles]

    feeds = []
    back = []
    for m in range(micros):
        feeds.append(
            feed(
                place,
                normed_two[m],
                dy_ctx,
                dy_fourth[m],
                m,
                second,
                vectors,
                feeds[0][7] if m else None,
                after=then(),
            )
        )
        done.append(feeds[-1][0])
        back.append(Reduction(list(feeds[m][2:6]), m))
    done.append(back[0].relay(then()))
    parts = feed_out([result[0] for result in feeds], second, wide, after=then())
    done.append(parts[0])
    outs = [Reduction(list(parts[4 * m : 4 * m + 4]), m) for m in range(micros)]
    for m in range(1, micros):
        done.append(back[m].relay(then()))

    turns = []
    traded = []
    for m in range(micros):
        turns.append(
            turn(
                back[m].got,
                middle[m],
                dy,
                m,
                out_full,
                vectors,
                turns[-1][1] if m else None,
                heads,
                head_size,
                after=then(),
            )
        )
        done.append(turns[-1][0])
        traded.append(exchange(turns[m][2]))
        if m == 0:
            grad_second = weights_part(
                [result[0] for result in feeds],
                [result[1] for result in feeds],
                normed_two,
                dy_ctx,
                dy_fourth,
                after=then(),
            )
            done.append(grad_second)
            summed_second = lax.psum_scatter(
                grad_second, "fsdp", scatter_dimension=0, tiled=True
            )
        done.append(outs[m].relay(then()))
    out_parts = out_weight_part(place, attended, turns[-1][1], after=then())
    done.append(out_parts[0])
    grad_out_weight = Reduction(list(out_parts), 0)
    rears = []
    summed = []
    for m in range(micros):
        result = fronts[m]
        rears.append(
            rear(
                place,
                result[1],
                traded[m],
                turns[m][3],
                result[4],
                result[5],
                first,
                heads,
                head_size,
                after=then(),
            )
        )
        done.append(rears[-1][0])
        summed.append(Reduction(list(rears[m][1:5]), m))
        if m == 0:
            done.append(grad_out_weight.relay(then(*outs[0].got[1:])))
        else:
            done.append(summed[m - 1].relay(then(*outs[m].got[1:])))
    last = merged_part(
        place,
        [result[0] for result in fronts],
        [result[0] for result in rears],
        [result[5] for result in rears],
        [result[4] for result in turns],
        [result[6] for result in feeds],
        first,
        vectors,
        grad_out_weight.got,
        heads,
        head_size,
        after=then(summed_second),
    )
    done.append(last)
    summed_last = lax.psum_scatter(last, "fsdp", scatter_dimension=0, tiled=True)
    done.append(summed[-1].relay(then()))
    layer_output = None
    for m in range(micros):
        layer_output = finish(
            finish_output_kernel,
            outs[m].got,
            None,
            (middle[m], vectors),
            m,
            layer_output,
            x.shape,
            BF,
            after=() if m else then(),
        )
    done.append(layer_output)
    input_grad = None
    for m in range(micros):
        input_grad = finish(
            finish_input_kernel,
            summed[m].got,
            x,
            (turns[m][0], vectors),
            m,
            input_grad,
            x.shape,
            F32,
            after=() if m else then(),
        )
    done.append(input_grad)

    half = summed_second.shape[1] // 2
    halves = [
        gather_four(summed_second[:, i * half : (i + 1) * half], i) for i in range(2)
    ]
    grad_up, grad_down = spread(place, halves, shards, piece, wide, after=then())
    done.append(grad_up)
    parts = trade_four([summed_last] * 4)
    grad_merged, grad_out_weight, *vector_sums = spread_heads(
        place, parts, width, head_size, wide, after=then()
    )
    def rows_first(a):
        return a.reshape(micros, 1, wide, rows).transpose(0, 1, 3, 2)

    return (
        rows_first(layer_output),
        rows_first(input_grad),
        vector_sums[0],
        vector_sums[1],
        grad_merged,
        vector_sums[2],
        vector_sums[3],
        grad_out_weight,
        vector_sums[4],
        vector_sums[5],
        vector_sums[6],
        grad_up,
        vector_sums[8],
        grad_down,
        vector_sums[7],
    )


def solution(mesh):
    rows = P(None, "fsdp", "ctx", None)
    matrix = P("fsdp", None)
    vector = P("fsdp")
    in_specs = (
        rows,
        rows,
        vector,
        vector,
        matrix,
        vector,
        vector,
        matrix,
        vector,
        vector,
        vector,
        matrix,
        vector,
        matrix,
        vector,
    )
    out_specs = (rows, rows) + in_specs[2:]
    step = on_device if mesh.shape["ctx"] == 4 else general_device
    return jax.shard_map(
        step, mesh=mesh, in_specs=in_specs, out_specs=out_specs, check_vma=False
    )
```

```python
import functools

import jax
import jax.numpy as jnp
from jax import lax
from jax.experimental import pallas as pl
from jax.experimental.pallas import tpu as pltpu
from jax.sharding import PartitionSpec as P

HEADS = 17
EPSILON = 1e-05
MASKED = -1e30
VMEM_BYTES = 56 * 1024 * 1024
COST = 40
BF = jnp.bfloat16
F32 = jnp.float32


def swap(block, bit):
    size = lax.axis_size("ctx")
    return lax.ppermute(block, "ctx", [(i, i ^ bit) for i in range(size)])


def gather_ctx(block):
    size = lax.axis_size("ctx")
    if size != 4:
        return [block] + [swap(block, r) for r in range(1, size)]
    half = block.shape[0] // 2
    one = swap(block, 1)
    two = swap(block, 2)
    top = swap(two[:half], 1)
    bottom = swap(one[half:], 2)
    return [block, one, two, jnp.concatenate((top, bottom))]


def add_f32(a, b):
    return a.astype(F32) + b.astype(F32)


def reduce_ctx(parts):
    size = lax.axis_size("ctx")
    if size != 4:
        total = parts[0].astype(F32)
        for r in range(1, size):
            total = total + swap(parts[r], r).astype(F32)
        return total
    half = parts[0].shape[0] // 2
    from_one = swap(parts[3][:half], 1)
    from_two = swap(parts[3][half:], 2)
    for_two = jnp.concatenate(
        (add_f32(parts[2][:half], from_one).astype(BF), parts[2][half:].astype(BF))
    )
    for_one = jnp.concatenate(
        (parts[1][:half].astype(BF), add_f32(parts[1][half:], from_two).astype(BF))
    )
    got_one = swap(for_one, 1)
    got_two = swap(for_two, 2)
    return parts[0].astype(F32) + got_one.astype(F32) + got_two.astype(F32)


def trade_ctx(parts):
    return [parts[0]] + [swap(parts[r], r) for r in range(1, len(parts))]


def normal(values):
    centre = values - jnp.mean(values, axis=-1, keepdims=True)
    spread = jnp.mean(centre * centre, axis=-1, keepdims=True)
    rate = lax.rsqrt(spread + EPSILON)
    return centre * rate, rate


def norm_back(normed, rate, scaled):
    return rate * (
        scaled
        - jnp.mean(scaled, axis=-1, keepdims=True)
        - normed * jnp.mean(scaled * normed, axis=-1, keepdims=True)
    )


def dot(a, b, dims):
    return lax.dot_general(a, b, ((dims[0], dims[1]), ((), ())), preferred_element_type=F32)


NN = ((1,), (0,))
NT = ((1,), (1,))


def head_lanes(shape, head, head_size):
    lane = lax.broadcasted_iota(jnp.int32, shape, 1)
    return (lane >= head * head_size) & (lane < (head + 1) * head_size)


def attend_kernel(
    blocks, rows, heads, head_size, place, qkv, out, tail_out, log, tail_log, keys, values_t, tail_kv
):
    width = heads * head_size
    me = place[0]
    for j in range(blocks):
        slot = pl.ds(pl.multiple_of((me ^ j) * rows, rows), rows)
        here = pl.ds(j * rows, rows)
        keys[here, :] = qkv[slot, width : 2 * width]
        values_t[:width, here] = qkv[slot, 2 * width : 3 * width].T
        pair = qkv[slot, 3 * width : 3 * width + 2 * head_size]
        tail_kv[here, :] = pair
        values_t[width:, here] = pair.T
    key_row = lax.broadcasted_iota(jnp.int32, (rows, rows), 0)
    query_row = lax.broadcasted_iota(jnp.int32, (rows, rows), 1)

    def softmax_values(scores, value_rows):
        peak = scores[0].max(axis=0, keepdims=True)
        for s in scores[1:]:
            peak = jnp.maximum(peak, s.max(axis=0, keepdims=True))
        total = jnp.zeros((1, rows), F32)
        product = jnp.zeros((head_size, rows), F32)
        for j, s in enumerate(scores):
            e = jnp.exp(s - peak)
            total = total + e.sum(axis=0, keepdims=True)
            product = product + dot(
                values_t[value_rows, j * rows : (j + 1) * rows], e.astype(BF), NN
            )
        return product / total, peak + jnp.log(total)

    for i in range(blocks):
        slot = pl.ds(pl.multiple_of((me ^ i) * rows, rows), rows)
        query = qkv[slot, :width]
        products = []
        for h in range(heads):
            masked = jnp.where(head_lanes((rows, width), h, head_size), query, jnp.zeros_like(query))
            scores = []
            for j in range(i + 1):
                s = dot(keys[j * rows : (j + 1) * rows, :], masked, NT)
                if j == i:
                    s = jnp.where(key_row <= query_row, s, MASKED)
                scores.append(s)
            product, total = softmax_values(scores, pl.ds(h * head_size, head_size))
            products.append(product)
            log[h : h + 1, i * rows : (i + 1) * rows] = total
        out[slot, :] = jnp.concatenate(products, axis=0).T.astype(BF)

    query = qkv[0:rows, 3 * width + 2 * head_size : 3 * width + 3 * head_size]
    scores = []
    for j in range(blocks):
        s = dot(tail_kv[j * rows : (j + 1) * rows, :head_size], query, NT)
        scores.append(jnp.where(j * rows + key_row <= me * rows + query_row, s, MASKED))
    product, total = softmax_values(scores, pl.ds(width + head_size, head_size))
    tail_out[...] = product.T.astype(BF)
    tail_log[...] = total


def attend(place, qkv, blocks, rows, heads, head_size):
    width = heads * head_size
    length = blocks * rows
    return pl.pallas_call(
        functools.partial(attend_kernel, blocks, rows, heads, head_size),
        out_shape=(
            jax.ShapeDtypeStruct((length, width), BF),
            jax.ShapeDtypeStruct((rows, head_size), BF),
            jax.ShapeDtypeStruct((heads, length), F32),
            jax.ShapeDtypeStruct((1, rows), F32),
        ),
        in_specs=[
            pl.BlockSpec(memory_space=pltpu.SMEM),
            pl.BlockSpec(memory_space=pltpu.VMEM),
        ],
        out_specs=(pl.BlockSpec(memory_space=pltpu.VMEM),) * 4,
        scratch_shapes=[
            pltpu.VMEM((length, width), BF),
            pltpu.VMEM((width + 2 * head_size, length), BF),
            pltpu.VMEM((length, 2 * head_size), BF),
        ],
        compiler_params=pltpu.CompilerParams(vmem_limit_bytes=VMEM_BYTES),
        cost_estimate=pl.CostEstimate(
            flops=10 * 4 * length * length * width, bytes_accessed=6 * length * width, transcendentals=0
        ),
    )(place, qkv)


def attend_back_kernel(
    blocks,
    rows,
    heads,
    head_size,
    place,
    qkv,
    grad,
    tail_grad,
    log,
    tail_log,
    out,
    keys,
    values,
    keys_t,
    tail_kv,
    key_sum,
    value_sum,
    tail_key_sum,
    tail_value_sum,
):
    width = heads * head_size
    me = place[0]
    for j in range(blocks):
        slot = pl.ds(pl.multiple_of((me ^ j) * rows, rows), rows)
        here = pl.ds(j * rows, rows)
        block = qkv[slot, width : 2 * width]
        keys[here, :] = block
        keys_t[:width, here] = block.T
        values[here, :] = qkv[slot, 2 * width : 3 * width]
        pair = qkv[slot, 3 * width : 3 * width + 2 * head_size]
        tail_kv[here, :] = pair
        keys_t[width:, here] = pair.T
    key_row = lax.broadcasted_iota(jnp.int32, (rows, rows), 0)
    query_row = lax.broadcasted_iota(jnp.int32, (rows, rows), 1)
    scale = head_size**-0.5

    for i in range(blocks):
        slot = pl.ds(pl.multiple_of((me ^ i) * rows, rows), rows)
        query = qkv[slot, :width]
        grad_out = grad[slot, :]
        lanes = [head_lanes((rows, width), h, head_size) for h in range(heads)]
        queries = [jnp.where(m, query, jnp.zeros_like(query)) for m in lanes]
        grads = [jnp.where(m, grad_out, jnp.zeros_like(grad_out)) for m in lanes]
        query_parts = []
        for h in range(heads):
            shift = log[h : h + 1, i * rows : (i + 1) * rows]
            probs, weighted = [], []
            delta = jnp.zeros((1, rows), F32)
            for j in range(i + 1):
                here = slice(j * rows, (j + 1) * rows)
                s = dot(keys[here, :], queries[h], NT)
                if j == i:
                    s = jnp.where(key_row <= query_row, s, MASKED)
                p = jnp.exp(s - shift)
                g = dot(values[here, :], grads[h], NT)
                delta = delta + (p * g).sum(axis=0, keepdims=True)
                probs.append(p)
                weighted.append(g)
            part = jnp.zeros((head_size, rows), F32)
            for j in range(i + 1):
                here = slice(j * rows, (j + 1) * rows)
                ds = (probs[j] * (weighted[j] - delta)).astype(BF)
                p = probs[j].astype(BF)
                key_part = dot(ds, queries[h], NN)
                value_part = dot(p, grads[h], NN)
                if h == 0 and j == i:
                    key_sum[here, :] = key_part
                    value_sum[here, :] = value_part
                else:
                    key_sum[here, :] += key_part
                    value_sum[here, :] += value_part
                part = part + dot(keys_t[h * head_size : (h + 1) * head_size, here], ds, NN)
            query_parts.append(part)
        out[slot, :width] = (jnp.concatenate(query_parts, axis=0) * scale).T.astype(BF)

    query = qkv[0:rows, 3 * width + 2 * head_size : 3 * width + 3 * head_size]
    grad_out = tail_grad[...]
    probs, weighted = [], []
    delta = jnp.zeros((1, rows), F32)
    for j in range(blocks):
        here = slice(j * rows, (j + 1) * rows)
        s = dot(tail_kv[here, :head_size], query, NT)
        s = jnp.where(j * rows + key_row <= me * rows + query_row, s, MASKED)
        p = jnp.exp(s - tail_log[...])
        g = dot(tail_kv[here, head_size:], grad_out, NT)
        delta = delta + (p * g).sum(axis=0, keepdims=True)
        probs.append(p)
        weighted.append(g)
    part = jnp.zeros((head_size, rows), F32)
    for j in range(blocks):
        here = slice(j * rows, (j + 1) * rows)
        slot = pl.ds(pl.multiple_of((me ^ j) * rows, rows), rows)
        ds = (probs[j] * (weighted[j] - delta)).astype(BF)
        key_part = dot(ds, query, NN)
        value_part = dot(probs[j].astype(BF), grad_out, NN)
        part = part + dot(keys_t[width : width + head_size, here], ds, NN)
        out[slot, width : 2 * width] = key_sum[here, :].astype(BF)
        out[slot, 2 * width : 3 * width] = value_sum[here, :].astype(BF)
        out[slot, 3 * width : 3 * width + 2 * head_size] = jnp.concatenate(
            (key_part, value_part), axis=1
        ).astype(BF)
    tail_columns = slice(3 * width + 2 * head_size, 3 * width + 3 * head_size)
    out[0:rows, tail_columns] = (part * scale).T.astype(BF)
    for j in range(1, blocks):
        out[j * rows : (j + 1) * rows, tail_columns] = jnp.zeros((rows, head_size), BF)


def attend_back(place, qkv, grad, tail_grad, log, tail_log, blocks, rows, heads, head_size):
    width = heads * head_size
    length = blocks * rows
    return pl.pallas_call(
        functools.partial(attend_back_kernel, blocks, rows, heads, head_size),
        out_shape=jax.ShapeDtypeStruct(qkv.shape, BF),
        in_specs=[pl.BlockSpec(memory_space=pltpu.SMEM)]
        + [pl.BlockSpec(memory_space=pltpu.VMEM)] * 5,
        out_specs=pl.BlockSpec(memory_space=pltpu.VMEM),
        scratch_shapes=[
            pltpu.VMEM((length, width), BF),
            pltpu.VMEM((length, width), BF),
            pltpu.VMEM((width + 2 * head_size, length), BF),
            pltpu.VMEM((length, 2 * head_size), BF),
            pltpu.VMEM((length, width), F32),
            pltpu.VMEM((length, width), F32),
            pltpu.VMEM((length, head_size), F32),
            pltpu.VMEM((length, head_size), F32),
        ],
        compiler_params=pltpu.CompilerParams(vmem_limit_bytes=VMEM_BYTES),
        cost_estimate=pl.CostEstimate(
            flops=10 * 10 * length * length * width, bytes_accessed=9 * length * width, transcendentals=0
        ),
    )(place, qkv, grad, tail_grad, log, tail_log)


def mlp_kernel(
    normed, grad, up, down, bias, hidden_out, grad_pre_out, part_out, grad_part_out, bias_out
):
    pre = dot(normed[...], up[...], NN) + bias[...]
    bell = jnp.exp(-0.5 * pre * pre) * 0.3989422804014327
    below = 0.5 + 0.5 * lax.erf(pre * 0.7071067811865476)
    hidden = (pre * below).astype(BF)
    hidden_out[...] = hidden
    part_out[...] = dot(hidden, down[...], NN).astype(BF)
    grad_pre = ((below + pre * bell) * dot(grad[...], down[...], NT)).astype(BF)
    grad_pre_out[...] = grad_pre
    grad_part_out[...] = dot(grad_pre, up[...], NT).astype(BF)
    sums = grad_pre.astype(F32).sum(axis=0, keepdims=True)

    @pl.when(pl.program_id(0) == 0)
    def _():
        bias_out[...] = sums

    @pl.when(pl.program_id(0) > 0)
    def _():
        bias_out[...] += sums


def mlp(normed, grad, up, down, bias, rows):
    length, wide = normed.shape
    hidden = up.shape[1]
    row_block = pl.BlockSpec((rows, wide), lambda i: (i, 0))
    hidden_block = pl.BlockSpec((rows, hidden), lambda i: (i, 0))
    whole = pl.BlockSpec(memory_space=pltpu.VMEM)
    return pl.pallas_call(
        mlp_kernel,
        grid=(length // rows,),
        out_shape=(
            jax.ShapeDtypeStruct((length, hidden), BF),
            jax.ShapeDtypeStruct((length, hidden), BF),
            jax.ShapeDtypeStruct((length, wide), BF),
            jax.ShapeDtypeStruct((length, wide), BF),
            jax.ShapeDtypeStruct((1, hidden), F32),
        ),
        in_specs=[row_block, row_block, whole, whole, whole],
        out_specs=(
            hidden_block,
            hidden_block,
            row_block,
            row_block,
            pl.BlockSpec((1, hidden), lambda i: (0, 0)),
        ),
        compiler_params=pltpu.CompilerParams(vmem_limit_bytes=VMEM_BYTES),
        cost_estimate=pl.CostEstimate(
            flops=12 * length * wide * hidden,
            bytes_accessed=2 * (6 * length * wide + 2 * wide * hidden),
            transcendentals=0,
        ),
    )(normed, grad, up, down, bias)


def general_device(
    layer_input,
    output_grad,
    attn_gain,
    attn_shift,
    merged_weight,
    query_bias,
    value_bias,
    out_weight,
    out_bias,
    mlp_gain,
    mlp_shift,
    up_weight,
    up_bias,
    down_weight,
    down_bias,
):
    micros = layer_input.shape[0]
    rows = layer_input.shape[2]
    wide = layer_input.shape[3]
    head_size = wide // HEADS
    blocks = lax.axis_size("ctx")
    shards = lax.axis_size("fsdp")
    me = lax.axis_index("ctx")
    heads = HEADS // blocks
    width = heads * head_size
    main = blocks * width
    own = merged_weight.shape[0]
    hidden = up_weight.shape[1]
    piece = hidden // shards // blocks
    quads = hidden // wide
    used = 3 * width + 3 * head_size
    assert HEADS - heads * blocks == 1
    place = me.astype(jnp.int32).reshape(1)
    relative = jnp.arange(blocks, dtype=jnp.int32) ^ me
    start = me * width

    vectors = jnp.concatenate(
        (
            attn_gain,
            attn_shift,
            query_bias,
            value_bias,
            out_bias,
            mlp_gain,
            mlp_shift,
            down_bias,
            up_bias,
        )
    ).reshape(8 + quads, own)
    first = jnp.concatenate(
        (
            lax.dynamic_slice_in_dim(merged_weight, start, width, 1),
            lax.dynamic_slice_in_dim(merged_weight, wide + start, width, 1),
            lax.dynamic_slice_in_dim(merged_weight, 2 * wide + start, width, 1),
            merged_weight[:, wide + main : 2 * wide],
            merged_weight[:, 2 * wide + main :],
            merged_weight[:, main:wide],
            vectors.T,
        ),
        axis=1,
    )
    first = lax.all_gather(first, "fsdp", axis=0, tiled=True)
    merged_own = first[:, :used]
    vectors = first[:, used:].T.astype(F32)
    gain_one, shift_one, query_row, value_row, out_row, gain_two, shift_two, down_row = [
        vectors[i] for i in range(8)
    ]
    up_row = (
        vectors[8:]
        .reshape(quads, shards, own)
        .transpose(1, 0, 2)
        .reshape(shards, blocks, piece)
    )
    up_row = lax.dynamic_index_in_dim(up_row, me, 1, keepdims=False).reshape(1, shards * piece)
    zero_tail = jnp.zeros((head_size,), F32)
    merged_row = jnp.concatenate(
        (
            lax.dynamic_slice_in_dim(query_row, start, width),
            jnp.zeros((width,), F32),
            lax.dynamic_slice_in_dim(value_row, start, width),
            zero_tail,
            value_row[main:],
            query_row[main:],
        )
    )
    scale_row = jnp.concatenate(
        (
            jnp.full((width,), head_size**-0.5, BF),
            jnp.ones((2 * width + 2 * head_size,), BF),
            jnp.full((head_size,), head_size**-0.5, BF),
        )
    )
    out_full = lax.all_gather(out_weight, "fsdp", axis=0, tiled=True)
    up_own = lax.dynamic_index_in_dim(
        up_weight.reshape(own, shards, blocks, piece), me, 2, keepdims=False
    ).reshape(own, shards * piece)
    down_own = lax.dynamic_slice_in_dim(down_weight, me * piece, piece, 0)
    up_own = lax.all_gather(up_own, "fsdp", axis=0, tiled=True)
    down_own = lax.all_gather(down_own, "fsdp", axis=0, tiled=True)

    values = [layer_input[m, 0] for m in range(micros)]
    values_ctx = [gather_ctx(v) for v in values]
    grads = [output_grad[m, 0] for m in range(micros)]
    grads_ctx = [jnp.concatenate(gather_ctx(g)) for g in grads]

    unscaled, normed, qkv, log, tail_log, attended, middle, normed_two = ([] for _ in range(8))
    for m in range(micros):
        centred, rate = normal(jnp.concatenate(values_ctx[m]).astype(F32))
        unscaled.append((centred, rate))
        normed.append((centred * gain_one + shift_one).astype(BF))
        rows_out = jnp.dot(normed[m], merged_own, preferred_element_type=F32) + merged_row
        qkv.append(rows_out.astype(BF) * scale_row)
        out, tail_out, total, tail_total = attend(place, qkv[m], blocks, rows, heads, head_size)
        log.append(total)
        tail_log.append(tail_total)
        traded = jnp.stack(trade_ctx(list(out.reshape(blocks, rows, width))))
        traded = jnp.take(traded, relative, axis=0).transpose(1, 0, 2).reshape(rows, main)
        attended.append(jnp.concatenate((traded, tail_out), axis=1))
        middle.append(
            values[m].astype(F32)
            + jnp.dot(attended[m], out_full, preferred_element_type=F32)
            + out_row
        )
        centred, rate = normal(middle[m])
        normed_two.append((centred * gain_two + shift_two).astype(BF))

    hiddens, grad_pres, normed_two_ctx, layer_output, grad_middle = ([] for _ in range(5))
    grad_up_row = 0.0
    grad_gain_two = 0.0
    grad_shift_two = 0.0
    for m in range(micros):
        normed_two_ctx.append(jnp.concatenate(gather_ctx(normed_two[m])))
        act, grad_pre, part, grad_part, bias_part = mlp(
            normed_two_ctx[m], grads_ctx[m], up_own, down_own, up_row, rows
        )
        hiddens.append(act)
        grad_pres.append(grad_pre)
        grad_up_row = grad_up_row + bias_part
        grad_normed = reduce_ctx(list(grad_part.reshape(blocks, rows, wide)))
        centred, rate = normal(middle[m])
        grad_gain_two = grad_gain_two + jnp.sum(grad_normed * centred, axis=0)
        grad_shift_two = grad_shift_two + jnp.sum(grad_normed, axis=0)
        grad_middle.append(
            grads[m].astype(F32) + norm_back(centred, rate, grad_normed * gain_two)
        )
        total = reduce_ctx(list(part.reshape(blocks, rows, wide)))
        layer_output.append((middle[m] + total + down_row).astype(BF))
    grad_down = sum(dot(a, g, ((0,), (0,))) for a, g in zip(hiddens, grads_ctx, strict=True))
    grad_up = sum(dot(n, g, ((0,), (0,))) for n, g in zip(normed_two_ctx, grad_pres, strict=True))
    grad_down = lax.psum_scatter(grad_down.astype(BF), "fsdp", scatter_dimension=0, tiled=True)
    grad_up = lax.psum_scatter(grad_up.astype(BF), "fsdp", scatter_dimension=0, tiled=True)

    grad_out_weight = 0.0
    grad_out_row = 0.0
    grad_down_row = 0.0
    grad_merged = 0.0
    grad_merged_row = 0.0
    grad_gain_one = 0.0
    grad_shift_one = 0.0
    input_grad = []
    for m in range(micros):
        grad_attn = grad_middle[m].astype(BF)
        grad_out_weight = grad_out_weight + dot(attended[m], grad_attn, ((0,), (0,)))
        grad_out_row = grad_out_row + jnp.sum(grad_attn.astype(F32), axis=0)
        grad_down_row = grad_down_row + jnp.sum(grads[m].astype(F32), axis=0)
        grad_attended = dot(grad_attn, out_full, NT).astype(BF)
        to_trade = grad_attended[:, :main].reshape(rows, blocks, width).transpose(1, 0, 2)
        to_trade = jnp.take(to_trade, relative, axis=0)
        traded = jnp.concatenate(trade_ctx(list(to_trade)))
        grad_qkv = attend_back(
            place,
            qkv[m],
            traded,
            grad_attended[:, main:],
            log[m],
            tail_log[m],
            blocks,
            rows,
            heads,
            head_size,
        )
        grad_merged = grad_merged + dot(normed[m], grad_qkv, ((0,), (0,)))
        grad_merged_row = grad_merged_row + jnp.sum(grad_qkv.astype(F32), axis=0)
        grad_part = dot(grad_qkv, merged_own, NT)
        centred, rate = unscaled[m]
        grad_gain_one = grad_gain_one + jnp.sum(grad_part * centred, axis=0)
        grad_shift_one = grad_shift_one + jnp.sum(grad_part, axis=0)
        grad_normed = reduce_ctx(list(grad_part.astype(BF).reshape(blocks, rows, wide)))
        input_grad.append(
            grad_middle[m] + norm_back(centred[:rows], rate[:rows], grad_normed * gain_one)
        )

    def placed(part, tail):
        row = lax.dynamic_update_slice_in_dim(jnp.zeros((main,), F32), part, start, 0)
        return jnp.concatenate((row, tail))

    up_sums = lax.dynamic_update_slice_in_dim(
        jnp.zeros((shards, blocks, piece), F32), grad_up_row.reshape(shards, 1, piece), me, 1
    )
    up_sums = up_sums.reshape(shards, quads, own).transpose(1, 0, 2).reshape(quads, wide)
    vector_sums = jnp.concatenate(
        (
            jnp.stack(
                (
                    grad_gain_one,
                    grad_shift_one,
                    placed(grad_merged_row[:width], grad_merged_row[used - head_size :]),
                    placed(
                        grad_merged_row[2 * width : 3 * width],
                        grad_merged_row[3 * width + head_size : 3 * width + 2 * head_size],
                    ),
                    grad_out_row,
                    grad_gain_two,
                    grad_shift_two,
                    grad_down_row,
                )
            ),
            up_sums,
        )
    )
    last = jnp.concatenate((grad_merged, vector_sums.T), axis=1).astype(BF)
    last = lax.psum_scatter(last, "fsdp", scatter_dimension=0, tiled=True)
    grad_out_weight = lax.psum_scatter(
        grad_out_weight.astype(BF), "fsdp", scatter_dimension=0, tiled=True
    ).astype(F32)
    bit = 1
    while bit < blocks:
        grad_out_weight = grad_out_weight + swap(grad_out_weight.astype(BF), bit).astype(F32)
        bit *= 2

    def absolute(parts):
        return jnp.take(jnp.stack(parts), relative, axis=0).astype(F32)

    last = absolute(gather_ctx(last))
    tails = jnp.sum(last[:, :, 3 * width :], axis=0)

    def columns(index, tail):
        body = last[:, :, index * width : (index + 1) * width].transpose(1, 0, 2)
        return [body.reshape(own, main), tails[:, tail * head_size : (tail + 1) * head_size]]

    grad_merged = jnp.concatenate(columns(0, 2) + columns(1, 0) + columns(2, 1), axis=1)
    vector_sums = tails[:, 3 * head_size :].T
    grad_up = absolute(gather_ctx(grad_up)).reshape(blocks, own, shards, piece)
    grad_up = grad_up.transpose(1, 2, 0, 3).reshape(own, hidden)
    grad_down = absolute(gather_ctx(grad_down)).reshape(blocks * piece, wide)
    return (
        jnp.stack(layer_output)[:, None],
        jnp.stack(input_grad)[:, None],
        vector_sums[0],
        vector_sums[1],
        grad_merged,
        vector_sums[2],
        vector_sums[3],
        grad_out_weight,
        vector_sums[4],
        vector_sums[5],
        vector_sums[6],
        grad_up,
        vector_sums[8:].reshape(quads * own),
        grad_down,
        vector_sums[7],
    )


def gather_blocks(array):
    one = swap(array, 1)
    two = swap(array, 2)
    fourth = [swap(two[m], 1) if m % 2 == 0 else swap(one[m], 2) for m in range(array.shape[0])]
    return [array, one, two], fourth


def exchange(parts):
    return lax.all_to_all(parts, "ctx", 0, 0, tiled=True)


def gather_straight(block):
    return [block] + [swap(block, r) for r in range(1, 4)]


def gather_four(block, which):
    one = swap(block, 1)
    two = swap(block, 2)
    return [block, one, two, swap(two, 1) if which % 2 == 0 else swap(one, 2)]


class Reduction:
    def __init__(self, parts, fourths):
        self.parts = parts
        self.coming = [swap(fourths[0], 1), swap(fourths[1], 2)]

    def relay(self, after):
        own, one, two = self.parts
        one, two = relay(one, two, *self.coming, after)
        self.got = [own, swap(one, 1), swap(two, 2)]
        return one


def whole_spec():
    return pl.BlockSpec(memory_space=pltpu.VMEM)


def scalar_spec():
    return pl.BlockSpec(memory_space=pltpu.SMEM)


def any_spec():
    return pl.BlockSpec(memory_space=pl.ANY)


def micro_spec(shape, which):
    rest = tuple(shape[1:])
    return pl.BlockSpec((1,) + rest, lambda i: (which,) + (0,) * len(rest))


def each_spec(dims):
    rest = tuple(dims[1:])
    return pl.BlockSpec((1,) + rest, lambda i: (i,) + (0,) * len(rest))


def call(
    kernel,
    operands,
    in_specs,
    outs,
    out_specs,
    flops,
    scratch=(),
    after=(),
    old=None,
    cost=COST,
    steps=1,
):
    extra = list(after)
    aliases = {}
    for index, array in (old or {}).items():
        aliases[len(operands) + len(extra)] = index
        extra.append(array)
    count = len(operands)

    def body(*refs):
        kernel(*refs[:count], *refs[count + len(extra) :])

    moved = sum(o.size * o.dtype.itemsize for o in (*operands, *outs))
    return pl.pallas_call(
        body,
        grid=(steps,),
        out_shape=tuple(outs),
        in_specs=list(in_specs) + [any_spec()] * len(extra),
        out_specs=tuple(out_specs),
        scratch_shapes=list(scratch),
        input_output_aliases=aliases,
        compiler_params=pltpu.CompilerParams(vmem_limit_bytes=VMEM_BYTES),
        cost_estimate=pl.CostEstimate(
            flops=cost * flops, bytes_accessed=cost * moved, transcendentals=0
        ),
        name=getattr(kernel, "func", kernel).__name__,
    )(*operands, *extra)


def shape(*sizes, dtype=BF):
    return jax.ShapeDtypeStruct(sizes, dtype)


def relay_kernel(one, two, first, second, one_out, two_out):
    two_out[0] = add_f32(two[0], first[...]).astype(BF)
    one_out[0] = add_f32(one[0], second[...]).astype(BF)


def relay(one, two, first, second, after):
    count = len(after)
    dims = one.shape
    return pl.pallas_call(
        lambda *refs: relay_kernel(*refs[:4], *refs[4 + count :]),
        grid=(1,),
        out_shape=(shape(*dims), shape(*dims)),
        in_specs=[micro_spec(dims, 1), micro_spec(dims, 0)] + [whole_spec()] * 2 + [any_spec()] * count,
        out_specs=(micro_spec(dims, 1), micro_spec(dims, 0)),
        input_output_aliases={0: 0, 1: 1},
        compiler_params=pltpu.CompilerParams(vmem_limit_bytes=VMEM_BYTES),
        cost_estimate=pl.CostEstimate(
            flops=dims[1] * dims[2], bytes_accessed=12 * dims[1] * dims[2], transcendentals=0
        ),
        name="relay_kernel",
    )(one, two, first, second, *after)


def pass_kernel(source, out):
    out[...] = source[...]


def pass_micro_kernel(source, out):
    out[...] = source[0]


def pass_micro(array, which, after):
    return call(
        pass_micro_kernel,
        [array],
        [micro_spec(array.shape, which)],
        [shape(*array.shape[1:])],
        [whole_spec()],
        0,
        after=after,
        cost=0,
    )[0]


def pass_on(array, after):
    return call(
        pass_kernel,
        [array],
        [whole_spec()],
        [shape(*array.shape)],
        [whole_spec()],
        0,
        after=after,
        cost=0,
    )[0]


def padded(columns):
    return (columns + 127) // 128 * 128


def pick_kernel(width, head_size, wide, place, weight, *refs):
    vectors, out = refs[:-1], refs[-1]
    own = out.shape[0]
    main = 4 * width
    for k in range(4):

        @pl.when(place[0] == k)
        def _(k=k):
            for part in range(3):
                begin = part * wide + k * width
                out[:, part * width : (part + 1) * width] = weight[:, begin : begin + width]

    for place_to, begin in enumerate((wide + main, 2 * wide + main, main)):
        at = 3 * width + place_to * head_size
        out[:, at : at + head_size] = weight[:, begin : begin + head_size]
    at = 3 * width + 3 * head_size
    rows = []
    for vector in vectors:
        row = vector[...].astype(F32).reshape(1, vector.shape[0])
        rows += [row[:, begin : begin + own] for begin in range(0, vector.shape[0], own)]
    row_id = lax.broadcasted_iota(jnp.int32, (len(rows), own), 0)
    table = jnp.zeros((len(rows), own), F32)
    for index, row in enumerate(rows):
        table = jnp.where(row_id == index, row, table)
    out[:, at:] = table.T.astype(BF)


def pick(place, weight, vectors, width, head_size):
    own, wide = weight.shape[0], weight.shape[1] // 3
    columns = 3 * width + 3 * head_size + sum(v.shape[0] for v in vectors) // own
    return call(
        functools.partial(pick_kernel, width, head_size, wide),
        [place, weight, *vectors],
        [scalar_spec()] + [whole_spec()] * (1 + len(vectors)),
        [shape(own, columns)],
        [whole_spec()],
        0,
    )[0]


def pick_hidden_kernel(shards, piece, second, place, up, down, out):
    for k in range(4):

        @pl.when(place[0] == k)
        def _(k=k):
            for f in range(shards):
                begin = (f * 4 + k) * piece
                out[:, f * piece : (f + 1) * piece] = up[:, begin : begin + piece]

    rows = out.shape[0]
    filled = shards * piece
    out[:, filled:second] = jnp.zeros((rows, second - filled), BF)
    out[:, second : second + down.shape[1]] = down[...]
    end = second + down.shape[1]
    out[:, end:] = jnp.zeros((rows, out.shape[1] - end), BF)


def pick_hidden(place, up, down, shards, piece, after=()):
    own = up.shape[0]
    second = padded(shards * piece)
    return call(
        functools.partial(pick_hidden_kernel, shards, piece, second),
        [place, up, down],
        [scalar_spec(), whole_spec(), whole_spec()],
        [shape(own, second + padded(down.shape[1]))],
        [whole_spec()],
        0,
        after=after,
        cost=0,
    )[0]


def feature_mean(v):
    return jnp.sum(v, axis=0, keepdims=True) * (1.0 / v.shape[0])


def normal_columns(values):
    centre = values - feature_mean(values)
    rate = lax.rsqrt(feature_mean(centre * centre) + EPSILON)
    return centre * rate, rate


def norm_back_columns(normed, rate, scaled):
    return rate * (scaled - feature_mean(scaled) - normed * feature_mean(scaled * normed))


def column(vectors, index):
    return vectors[:, index : index + 1].astype(F32)


def front_kernel(heads, head_size, first_call, place, *refs):
    x = refs[:4]
    weight, vectors = refs[4:6]
    refs = refs[6:]
    if first_call:
        normed_out, qkv, attended, log, tail_log, turned, keys = refs
        turned[...] = weight[:, : turned.shape[0]].T
    else:
        turned, normed_out, qkv, attended, log, tail_log, keys = refs
    normed_out, qkv, log, tail_log = (ref.at[0] for ref in (normed_out, qkv, log, tail_log))
    wide, rows = x[3].shape
    width = heads * head_size
    used = 3 * width + 3 * head_size
    me = place[0]
    gain, shift = column(vectors, 0), column(vectors, 1)
    mine = pl.ds(pl.multiple_of(me * width, width), width)
    query_bias = vectors[mine, 2:3].astype(F32)
    value_bias = vectors[mine, 3:4].astype(F32)
    last = slice(4 * width, 4 * width + head_size)
    bias = jnp.concatenate(
        (
            query_bias,
            jnp.zeros((width, 1), F32),
            value_bias,
            jnp.zeros((head_size, 1), F32),
            vectors[last, 3:4].astype(F32),
            vectors[last, 2:3].astype(F32),
        ),
        axis=0,
    )
    row = lax.broadcasted_iota(jnp.int32, (used, 1), 0)
    scale = jnp.where((row < width) | (row >= used - head_size), head_size**-0.5, 1.0)
    for r in range(4):
        normed, _ = normal_columns((x[r][...] if r == 3 else x[r][0]).astype(F32))
        normed_out[:, r * rows : (r + 1) * rows] = normed.astype(BF)
        full = (normed * gain + shift).astype(BF)
        projected = dot(turned[...], full, NN) + bias
        projected = (projected.astype(BF).astype(F32) * scale).astype(BF)
        qkv[:, r * rows : (r + 1) * rows] = projected
        here = slice(r * rows, (r + 1) * rows)
        keys[here, :width] = projected[width : 2 * width, :].T
        keys[here, width:] = projected[3 * width : 3 * width + 2 * head_size, :].T
    key_row = lax.broadcasted_iota(jnp.int32, (rows, rows), 0)
    query_row = lax.broadcasted_iota(jnp.int32, (rows, rows), 1)
    head_row = lax.broadcasted_iota(jnp.int32, (width, rows), 0) // head_size

    def slot(j):
        return pl.ds(pl.multiple_of((me ^ j) * rows, rows), rows)

    def softmax_values(scores, value_rows):
        peak = scores[0].max(axis=0, keepdims=True)
        for s in scores[1:]:
            peak = jnp.maximum(peak, s.max(axis=0, keepdims=True))
        total = jnp.zeros((1, rows), F32)
        product = jnp.zeros((head_size, rows), F32)
        for j, s in enumerate(scores):
            e = jnp.exp(s - peak)
            total = total + e.sum(axis=0, keepdims=True)
            product = product + dot(qkv[value_rows, slot(j)], e.astype(BF), NN)
        return product / total, peak + jnp.log(total)

    for i in range(4):
        query = qkv[:width, slot(i)]
        for h in range(heads):
            masked = jnp.where(head_row == h, query, jnp.zeros_like(query))
            scores = []
            for j in range(i + 1):
                s = dot(keys[slot(j), :width], masked, NN)
                if j == i:
                    s = jnp.where(key_row <= query_row, s, MASKED)
                scores.append(s)
            begin = 2 * width + h * head_size
            product, total = softmax_values(scores, slice(begin, begin + head_size))
            band = slice(h * head_size, (h + 1) * head_size)
            attended[band, i * rows : (i + 1) * rows] = product.astype(BF)
            log[h : h + 1, i * rows : (i + 1) * rows] = total
    begin = 3 * width + head_size
    query = qkv[begin + head_size :, 0:rows]
    query = jnp.concatenate((query, jnp.zeros_like(query)), axis=0)
    scores = []
    for j in range(4):
        s = dot(keys[slot(j), width:], query, NN)
        scores.append(jnp.where(j * rows + key_row <= me * rows + query_row, s, MASKED))
    product, total = softmax_values(scores, slice(begin, begin + head_size))
    quarter = head_size // 4
    for j in range(4):
        attended[width:, j * rows : (j + 1) * rows] = product[
            j * quarter : (j + 1) * quarter, :
        ].astype(BF)
    tail_log[...] = total


def front(place, x, fourth, which, weight, vectors, turned, old, heads, head_size, after=()):
    wide, rows = fourth.shape
    length = 4 * rows
    width = heads * head_size
    used = 3 * width + 3 * head_size
    first_call = turned is None
    micros = x[0].shape[0]
    outs = [
        shape(micros, wide, length),
        shape(micros, used, length),
        shape(width + head_size // 4, length),
        shape(micros, heads, length, dtype=F32),
        shape(micros, 1, rows, dtype=F32),
    ]
    out_specs = [micro_spec(o.shape, which) if len(o.shape) == 3 else whole_spec() for o in outs]
    operands = [place, *x, fourth, weight, vectors]
    in_specs = [scalar_spec()] + [micro_spec(x[0].shape, which)] * 3 + [whole_spec()] * 3
    if first_call:
        outs.append(shape(used, wide))
        out_specs.append(whole_spec())
    else:
        operands.append(turned)
        in_specs.append(whole_spec())
    return call(
        functools.partial(front_kernel, heads, head_size, first_call),
        operands,
        in_specs,
        outs,
        out_specs,
        12_000_000_000,
        old=None if old is None else {k: old[k] for k in (0, 1, 3, 4)},
        scratch=[pltpu.VMEM((length, width + 2 * head_size), BF)],
        after=after,
        cost=2,
    )


def middle_kernel(heads, head_size, first_call, place, *refs):
    parts = refs[:4]
    x = refs[4:8]
    weight, vectors = refs[8:10]
    refs = refs[10:]
    if first_call:
        middle, normed_two, attended, turned = refs
        turned[...] = weight[...].T
    else:
        turned, middle, normed_two, attended = refs
    middle, normed_two = middle.at[0], normed_two.at[0]
    wide, rows = x[3].shape
    width = heads * head_size
    me = place[0]
    own = pl.ds(pl.multiple_of(me * rows, rows), rows)
    for source in range(4):
        band = pl.ds(pl.multiple_of((me ^ source) * width, width), width)
        attended[0, band, :] = parts[source][:width, own]
    for r in range(4):
        lanes = pl.ds(pl.multiple_of((me ^ r) * rows, rows), rows)
        sums = (x[r][...] if r == 3 else x[r][0]).astype(F32) + column(vectors, 4)
        for source in range(4):
            band = pl.ds(pl.multiple_of((me ^ source) * width, width), width)
            sums = sums + dot(turned[:, band], parts[source][:width, lanes], NN)
        tail = jnp.concatenate(
            [parts[r][width:, j * rows : (j + 1) * rows] for j in range(4)], axis=0
        )
        sums = sums + dot(turned[:, 4 * width :], tail, NN)
        if r == 0:
            attended[0, 4 * width :, :] = tail
        if r == 0:
            middle[...] = sums
        normed, _ = normal_columns(sums)
        normed = normed * column(vectors, 5) + column(vectors, 6)
        normed_two[:, r * rows : (r + 1) * rows] = normed.astype(BF)


def middle_part(
    place, parts, x, fourth, which, weight, vectors, turned, old, heads, head_size, after=()
):
    wide, rows = fourth.shape
    first_call = turned is None
    operands = [place, *parts, *x, fourth, weight, vectors]
    in_specs = [scalar_spec()] + [whole_spec()] * 4 + [micro_spec(x[0].shape, which)] * 3
    in_specs += [whole_spec()] * 3
    dims = x[0].shape
    outs = [shape(*dims, dtype=F32), shape(dims[0], wide, 4 * rows), shape(*dims)]
    out_specs = [micro_spec(o.shape, which) for o in outs]
    if first_call:
        outs.append(shape(weight.shape[1], weight.shape[0]))
        out_specs.append(whole_spec())
    else:
        operands.append(turned)
        in_specs.append(whole_spec())
    return call(
        functools.partial(middle_kernel, heads, head_size, first_call),
        operands,
        in_specs,
        outs,
        out_specs,
        8 * rows * wide * wide,
        after=after,
        old=None if old is None else {k: old[k] for k in range(3)},
        cost=6,
    )


def keep_fourth(step, fourths, value):
    for m, target in enumerate(fourths):

        @pl.when(step == m)
        def _(target=target):
            target[...] = value


def feed_kernel(second, place, normed, *refs):
    grad = refs[:3]
    fourths = refs[3:5]
    weights, vectors = refs[5:7]
    kept_hidden, kept_grad_pre = refs[7].at[0], refs[8].at[0]
    grad_parts = refs[9:12]
    part_fourths = refs[12:14]
    bias_out, turned = refs[14:]
    step = pl.program_id(0)
    wide, rows = fourths[0].shape
    hidden_size = turned.shape[0]

    @pl.when(step == 0)
    def _():
        turned[...] = weights[:, :hidden_size].T

    lane = lax.broadcasted_iota(jnp.int32, (hidden_size, 4), 1)
    bias = jnp.where(lane == place[0], vectors[:, 8:12].astype(F32), 0.0)
    bias = bias.sum(axis=1, keepdims=True)
    total = jnp.zeros((hidden_size, rows), F32)
    for r in range(4):
        here = slice(r * rows, (r + 1) * rows)
        pre = dot(turned[...], normed[0, :, here], NN) + bias
        bell = jnp.exp(-0.5 * pre * pre) * 0.3989422804014327
        below = 0.5 + 0.5 * lax.erf(pre * 0.7071067811865476)
        kept_hidden[:, here] = (pre * below).astype(BF)
        back = jnp.where(step == 0, fourths[0][...], fourths[1][...]) if r == 3 else grad[r][0]
        grad_pre = (below + pre * bell) * dot(weights[:, second : second + wide], back, NN)
        grad_pre = grad_pre.astype(BF)
        kept_grad_pre[:, here] = grad_pre
        part = dot(weights[:, :hidden_size], grad_pre, NN).astype(BF)
        if r == 3:
            keep_fourth(step, part_fourths, part)
        else:
            grad_parts[r][0] = part
        total = total + grad_pre.astype(F32)
    total = total.sum(axis=1, keepdims=True)

    @pl.when(step == 0)
    def _():
        bias_out[...] = total

    @pl.when(step > 0)
    def _():
        bias_out[...] += total


def feed(place, normed, grads, fourths, weights, vectors, after=()):
    wide, rows = fourths[0].shape
    micros = len(fourths)
    hidden_size = weights.shape[0]
    length = 4 * rows
    dims = (micros, wide, rows)
    operands = [place, normed, *grads, *fourths, weights, vectors]
    in_specs = [scalar_spec(), each_spec(normed.shape)] + [each_spec(dims)] * 3
    in_specs += [whole_spec()] * (micros + 2)
    outs = [shape(micros, hidden_size, length)] * 2 + [shape(*dims)] * 3
    out_specs = [each_spec(o.shape) for o in outs] + [whole_spec()] * (micros + 1)
    outs += [shape(wide, rows)] * micros + [shape(hidden_size, 1, dtype=F32)]
    return call(
        functools.partial(feed_kernel, padded(hidden_size)),
        operands,
        in_specs,
        outs,
        out_specs,
        6 * micros * length * wide * hidden_size,
        scratch=[pltpu.VMEM((hidden_size, wide), BF)],
        after=after,
        steps=micros,
    )


def feed_out_kernel(second, hidden, weights, *refs):
    parts, fourths, turned = refs[:3], refs[3:-1], refs[-1]
    step = pl.program_id(0)

    @pl.when(step == 0)
    def _():
        turned[...] = weights[:, second : second + turned.shape[0]].T

    rows = fourths[0].shape[1]
    for r in range(4):
        here = slice(r * rows, (r + 1) * rows)
        part = dot(turned[...], hidden[0, :, here], NN).astype(BF)
        if r == 3:
            keep_fourth(step, fourths, part)
        else:
            parts[r][0] = part


def feed_out(hidden, weights, wide, after=()):
    micros, hidden_size, length = hidden.shape
    rows = length // 4
    outs = [shape(micros, wide, rows)] * 3
    return call(
        functools.partial(feed_out_kernel, padded(hidden_size)),
        [hidden, weights],
        [each_spec(hidden.shape), whole_spec()],
        outs + [shape(wide, rows)] * micros,
        [each_spec(o.shape) for o in outs] + [whole_spec()] * micros,
        2 * micros * length * wide * hidden_size,
        scratch=[pltpu.VMEM((wide, hidden_size), BF)],
        after=after,
        steps=micros,
    )


def weights_kernel(second, hidden, grad_pre, normed, *refs):
    grads, fourths = refs[:3], refs[3:5]
    out, left, right = refs[5:]
    micros, hidden_size, length = hidden.shape
    wide, rows = fourths[0].shape
    for m in range(micros):
        here = slice(m * length, (m + 1) * length)
        left[:, here] = normed[m]
        right[:, here] = grad_pre[m]
    out[:, :hidden_size] = dot(left[...], right[...], NT).astype(BF)
    out[:, hidden_size:second] = jnp.zeros((wide, second - hidden_size), BF)
    for m in range(micros):
        left[:, m * length : (m + 1) * length] = hidden[m]
        for r in range(4):
            here = slice(m * length + r * rows, m * length + (r + 1) * rows)
            right[:, here] = fourths[m][...] if r == 3 else grads[r][m]
    out[:, second : second + wide] = dot(left[...], right[...], NT).astype(BF)
    end = second + wide
    out[:, end:] = jnp.zeros((wide, out.shape[1] - end), BF)


def weights_part(hidden, grad_pre, normed, grads, fourths, after=()):
    micros, hidden_size, length = hidden.shape
    wide = fourths[0].shape[0]
    second = padded(hidden_size)
    operands = [hidden, grad_pre, normed, *grads, *fourths]
    return call(
        functools.partial(weights_kernel, second),
        operands,
        [whole_spec()] * len(operands),
        [shape(hidden_size, second + padded(wide))],
        [whole_spec()],
        4 * micros * length * wide * hidden_size,
        scratch=[pltpu.VMEM((wide, micros * length), BF)] * 2,
        after=after,
    )[0]


def turn_kernel(width, *refs):
    got = refs[:3]
    middle, grad, weight, vectors = refs[3:7]
    grad_middle, grad_attn, traded, tail, sums = refs[7:]
    step = pl.program_id(0)
    dy = grad[0].astype(F32)
    total = got[0][0].astype(F32) + got[1][0].astype(F32) + got[2][0].astype(F32)
    normed, rate = normal_columns(middle[0])
    result = dy + norm_back_columns(normed, rate, total * column(vectors, 5))
    grad_middle[0] = result
    low = result.astype(BF)
    grad_attn[0] = low
    for j in range(4):
        traded[j, 0] = dot(weight[j * width : (j + 1) * width, :], low, NN).astype(BF)
    tail[0] = dot(weight[4 * width :, :], low, NN).astype(BF)

    @pl.when(step == 0)
    def _():
        sums[...] = jnp.zeros(sums.shape, F32)

    for k, rows in enumerate((low.astype(F32), total * normed, total, dy)):
        sums[:, k : k + 1] += rows.sum(axis=1, keepdims=True)


def turn(got, middle, grads, weight, vectors, heads, head_size, after=()):
    micros, wide, rows = middle.shape
    width = heads * head_size
    dims = middle.shape
    outs = [shape(*dims, dtype=F32), shape(*dims), shape(4, micros, width, rows)]
    outs += [shape(micros, head_size, rows), shape(wide, 4, dtype=F32)]
    traded_spec = pl.BlockSpec((4, 1, width, rows), lambda i: (0, i, 0, 0))
    return call(
        functools.partial(turn_kernel, width),
        [*got, middle, grads, weight, vectors],
        [each_spec(dims)] * 5 + [whole_spec()] * 2,
        outs,
        [each_spec(dims)] * 2 + [traded_spec, each_spec(outs[3].shape), whole_spec()],
        2 * micros * rows * wide * wide,
        after=after,
        steps=micros,
    )


def rear_kernel(heads, head_size, place, *refs):
    step = pl.program_id(0)
    qkv, tail_grad, log, tail_log, out, sums = (refs[k].at[0] for k in (0, 2, 3, 4, 6, 12))
    traded, weight = refs[1], refs[5]
    parts, fourths = refs[7:10], refs[10:12]
    keys, values, key_sum, value_sum = refs[13:]
    rows = tail_grad.shape[1]
    used = qkv.shape[0]
    width = heads * head_size
    me = place[0]
    scale = head_size**-0.5
    tail_at = 3 * width
    for r in range(4):
        here = slice(r * rows, (r + 1) * rows)
        keys[here, :width] = qkv[width : 2 * width, here].T
        keys[here, width:] = qkv[tail_at : tail_at + 2 * head_size, here].T
        values[here, :] = qkv[2 * width : 3 * width, here].T
    key_row = lax.broadcasted_iota(jnp.int32, (rows, rows), 0)
    query_row = lax.broadcasted_iota(jnp.int32, (rows, rows), 1)
    head_row = lax.broadcasted_iota(jnp.int32, (width, rows), 0) // head_size

    def slot(j):
        return pl.ds(pl.multiple_of((me ^ j) * rows, rows), rows)

    for i in range(4):
        query = qkv[:width, slot(i)]
        grad_out = traded[i, 0]
        for h in range(heads):
            band = slice(h * head_size, (h + 1) * head_size)
            masked = jnp.where(head_row == h, query, jnp.zeros_like(query))
            masked_grad = jnp.where(head_row == h, grad_out, jnp.zeros_like(grad_out))
            shift = log[h : h + 1, i * rows : (i + 1) * rows]
            probs, weighted = [], []
            delta = jnp.zeros((1, rows), F32)
            for j in range(i + 1):
                s = dot(keys[slot(j), :width], masked, NN)
                if j == i:
                    s = jnp.where(key_row <= query_row, s, MASKED)
                p = jnp.exp(s - shift)
                g = dot(values[slot(j), :], masked_grad, NN)
                delta = delta + (p * g).sum(axis=0, keepdims=True)
                probs.append(p)
                weighted.append(g)
            part = jnp.zeros((head_size, rows), F32)
            for j in range(i + 1):
                here = slice(j * rows, (j + 1) * rows)
                ds = (probs[j] * (weighted[j] - delta)).astype(BF)
                p = probs[j].astype(BF)
                key_part = dot(query[band, :], ds, NT)
                value_part = dot(grad_out[band, :], p, NT)
                if j == i:
                    key_sum[band, here] = key_part
                    value_sum[band, here] = value_part
                else:
                    key_sum[band, here] += key_part
                    value_sum[band, here] += value_part
                at = width + h * head_size
                part = part + dot(qkv[at : at + head_size, slot(j)], ds, NN)
            out[band, slot(i)] = (part * scale).astype(BF)

    query = qkv[used - head_size :, 0:rows]
    grad_out = tail_grad[...]
    blank = jnp.zeros_like(query)
    wide_query = jnp.concatenate((query, blank), axis=0)
    wide_grad = jnp.concatenate((blank, grad_out), axis=0)
    probs, weighted = [], []
    delta = jnp.zeros((1, rows), F32)
    for j in range(4):
        s = dot(keys[slot(j), width:], wide_query, NN)
        s = jnp.where(j * rows + key_row <= me * rows + query_row, s, MASKED)
        p = jnp.exp(s - tail_log[...])
        g = dot(keys[slot(j), width:], wide_grad, NN)
        delta = delta + (p * g).sum(axis=0, keepdims=True)
        probs.append(p)
        weighted.append(g)
    part = jnp.zeros((head_size, rows), F32)
    for j in range(4):
        here = slice(j * rows, (j + 1) * rows)
        ds = (probs[j] * (weighted[j] - delta)).astype(BF)
        part = part + dot(qkv[tail_at : tail_at + head_size, slot(j)], ds, NN)
        out[tail_at : tail_at + head_size, slot(j)] = dot(query, ds, NT).astype(BF)
        out[tail_at + head_size : tail_at + 2 * head_size, slot(j)] = dot(
            grad_out, probs[j].astype(BF), NT
        ).astype(BF)
        out[width : 2 * width, slot(j)] = key_sum[:, here].astype(BF)
        out[2 * width : 3 * width, slot(j)] = value_sum[:, here].astype(BF)
    out[used - head_size :, 0:rows] = (part * scale).astype(BF)
    out[used - head_size :, rows:] = jnp.zeros((head_size, 3 * rows), BF)
    total = jnp.zeros((used, rows), F32)
    for r in range(4):
        block = out[:, r * rows : (r + 1) * rows]
        part = dot(weight[:, :used], block, NN).astype(BF)
        if r == 3:
            keep_fourth(step, fourths, part)
        else:
            parts[r][0] = part
        total = total + block.astype(F32)
    sums[...] = total.sum(axis=1, keepdims=True)


def rear(place, qkv, traded, tail_grad, log, tail_log, weight, heads, head_size, after=()):
    micros, used, length = qkv.shape
    rows = length // 4
    wide = weight.shape[0]
    width = heads * head_size
    first = [shape(*qkv.shape)] + [shape(micros, wide, rows)] * 3
    last = shape(micros, used, 1, dtype=F32)
    traded_spec = pl.BlockSpec((4, 1, width, rows), lambda i: (0, i, 0, 0))
    return call(
        functools.partial(rear_kernel, heads, head_size),
        [place, qkv, traded, tail_grad, log, tail_log, weight],
        [scalar_spec(), each_spec(qkv.shape), traded_spec]
        + [each_spec(a.shape) for a in (tail_grad, log, tail_log)]
        + [whole_spec()],
        first + [shape(wide, rows)] * micros + [last],
        [each_spec(o.shape) for o in first] + [whole_spec()] * micros + [each_spec(last.shape)],
        40_000_000_000,
        scratch=[
            pltpu.VMEM((length, width + 2 * head_size), BF),
            pltpu.VMEM((length, width), BF),
            pltpu.VMEM((width, length), F32),
            pltpu.VMEM((width, length), F32),
        ],
        after=after,
        steps=micros,
    )


def merged_kernel(heads, head_size, place, normed, grads, columns, others, up_sum, *refs):
    weight, vectors, out, small = refs
    micros, used, length = grads.shape
    wide = normed.shape[1]
    width = heads * head_size
    me = place[0]
    ones = jnp.ones((8, length), BF)
    product = dot(normed[0], grads[0], NT)
    total = dot(ones, grads[0], NT)
    down_columns = columns[0]
    for m in range(1, micros):
        product = product + dot(normed[m], grads[m], NT)
        total = total + dot(ones, grads[m], NT)
        down_columns = down_columns + columns[m]
    total = total[0:1, :]
    matrix = weight[:, :used].astype(F32)
    out[:, :used] = (column(vectors, 0) * product + column(vectors, 1) * total).astype(BF)
    gain = (product * matrix).sum(axis=1, keepdims=True)
    shift = (matrix * total).sum(axis=1, keepdims=True)
    small[...] = jnp.zeros(small.shape, F32)
    mine = pl.ds(pl.multiple_of(me * width, width), width)
    small[:, 0:1] = gain
    small[:, 1:2] = shift
    small[mine, 2:3] = down_columns[:width, :]
    small[mine, 3:4] = down_columns[2 * width : 3 * width, :]
    small[4 * width :, 2:3] = down_columns[used - head_size :, :]
    small[4 * width :, 3:4] = down_columns[3 * width + head_size : 3 * width + 2 * head_size, :]
    small[:, 4:8] = others[...]
    lane = lax.broadcasted_iota(jnp.int32, (wide, 4), 1)
    small[:, 8:12] = jnp.where(lane == me, up_sum[...], 0.0)
    out[:, used:] = small[:, : out.shape[1] - used].astype(BF)


def merged_part(
    place, normed, grads, columns, others, up_sum, weight, vectors, heads, head_size, after=()
):
    micros, wide, length = normed.shape
    used = grads.shape[1]
    operands = [place, normed, grads, columns, others, up_sum, weight, vectors]
    return call(
        functools.partial(merged_kernel, heads, head_size),
        operands,
        [scalar_spec()] + [whole_spec()] * (len(operands) - 1),
        [shape(*weight.shape)],
        [whole_spec()],
        2 * micros * length * wide * used,
        scratch=[pltpu.VMEM((wide, 128), F32)],
        after=after,
    )[0]


def out_weight_kernel(attended, grads, out):
    total = dot(attended[0], grads[0], NT)
    for m in range(1, attended.shape[0]):
        total = total + dot(attended[m], grads[m], NT)
    out[...] = total.astype(BF)


def out_weight_part(attended, grads, after=()):
    micros, wide, rows = attended.shape
    return call(
        out_weight_kernel,
        [attended, grads],
        [whole_spec()] * 2,
        [shape(wide, wide)],
        [whole_spec()],
        2 * micros * rows * wide * wide,
        after=after,
    )[0]


def finish_input_kernel(one, two, three, x, grad_middle, vectors, out):
    total = one[0].astype(F32) + two[0].astype(F32) + three[0].astype(F32)
    normed, rate = normal_columns(x[0].astype(F32))
    out[0] = grad_middle[0] + norm_back_columns(normed, rate, total * column(vectors, 0))


def finish_output_kernel(one, two, three, middle, vectors, out):
    total = one[0].astype(F32) + two[0].astype(F32) + three[0].astype(F32)
    out[0] = (middle[0] + total + column(vectors, 7)).astype(BF)


def finish(kernel, arrays, vectors, dtype, after=()):
    dims = arrays[0].shape
    return call(
        kernel,
        [*arrays, vectors],
        [each_spec(dims)] * len(arrays) + [whole_spec()],
        [shape(*dims, dtype=dtype)],
        [each_spec(dims)],
        20 * dims[0] * dims[1] * dims[2],
        after=after,
        cost=0,
        steps=dims[0],
    )[0]


def spread_kernel(piece, second, place, *refs):
    sources = refs[:4]
    grad_up, grad_down = refs[4:]
    shards = grad_up.shape[1] // (4 * piece)
    wide = grad_down.shape[1]
    for k in range(4):

        @pl.when(place[0] == k)
        def _(k=k):
            for j in range(4):
                source = sources[j ^ k]
                for f in range(shards):
                    at = (f * 4 + j) * piece
                    grad_up[:, at : at + piece] = source[:, f * piece : (f + 1) * piece].astype(F32)
                grad_down[j * piece : (j + 1) * piece, :] = source[:, second : second + wide].astype(
                    F32
                )


def spread(place, sources, shards, piece, wide, after=()):
    own = sources[0].shape[0]
    return call(
        functools.partial(spread_kernel, piece, padded(shards * piece)),
        [place, *sources],
        [scalar_spec()] + [whole_spec()] * 4,
        [shape(own, 4 * shards * piece, dtype=F32), shape(4 * piece, wide, dtype=F32)],
        [whole_spec()] * 2,
        0,
        after=after,
        cost=0,
    )


def spread_heads_kernel(width, head_size, place, *refs):
    sources = refs[:4]
    out_parts = refs[4:8]
    grad_merged, grad_out = refs[8:10]
    rows = refs[10:]
    wide = grad_merged.shape[1] // 3
    total = sources[0][:, 3 * width :].astype(F32)
    total_out = out_parts[0][...].astype(F32)
    for r in range(1, 4):
        total = total + sources[r][:, 3 * width :].astype(F32)
        total_out = total_out + out_parts[r][...].astype(F32)
    grad_out[...] = total_out
    table = total[:, 3 * head_size :].T
    own = table.shape[1]
    for index, row in enumerate(rows):
        if index < 8:
            row[...] = table[index]
        else:
            for part in range(row.shape[0] // own):
                row[part * own : (part + 1) * own] = table[8 + part]
    for part, tail in enumerate((2, 0, 1)):
        at = part * wide + 4 * width
        grad_merged[:, at : at + head_size] = total[:, tail * head_size : (tail + 1) * head_size]
    for k in range(4):

        @pl.when(place[0] == k)
        def _(k=k):
            for j in range(4):
                source = sources[j ^ k]
                for part in range(3):
                    at = part * wide + j * width
                    grad_merged[:, at : at + width] = source[
                        :, part * width : (part + 1) * width
                    ].astype(F32)


def spread_heads(place, sources, out_parts, width, head_size, wide, after=()):
    own, columns = sources[0].shape
    quads = columns - 3 * width - 3 * head_size - 8
    return call(
        functools.partial(spread_heads_kernel, width, head_size),
        [place, *sources, *out_parts],
        [scalar_spec()] + [whole_spec()] * 8,
        [
            shape(own, 3 * wide, dtype=F32),
            shape(own, wide, dtype=F32),
        ]
        + [shape(own, dtype=F32)] * 8
        + [shape(own * quads, dtype=F32)],
        [whole_spec()] * 11,
        0,
        after=after,
        cost=0,
    )


def on_device(
    layer_input,
    output_grad,
    attn_gain,
    attn_shift,
    merged_weight,
    query_bias,
    value_bias,
    out_weight,
    out_bias,
    mlp_gain,
    mlp_shift,
    up_weight,
    up_bias,
    down_weight,
    down_bias,
):
    micros, _, rows, wide = layer_input.shape
    assert micros == 2
    head_size = wide // HEADS
    shards = lax.axis_size("fsdp")
    me = lax.axis_index("ctx")
    heads = HEADS // 4
    width = heads * head_size
    own = merged_weight.shape[0]
    hidden = up_weight.shape[1]
    piece = hidden // shards // 4
    quads = hidden // wide
    used = 3 * width + 3 * head_size
    place = me.astype(jnp.int32).reshape(1)
    x = layer_input.transpose(0, 1, 3, 2).reshape(micros, wide, rows)
    dy = output_grad.transpose(0, 1, 3, 2).reshape(micros, wide, rows)

    small = [
        attn_gain,
        attn_shift,
        query_bias,
        value_bias,
        out_bias,
        mlp_gain,
        mlp_shift,
        down_bias,
        up_bias,
    ]
    first = pick(place, merged_weight, small, width, head_size)
    x_ctx, x_fourth = gather_blocks(x)
    dy_ctx = [dy] + [swap(pass_on(dy, x_fourth), bit) for bit in (1, 2)]
    first = lax.all_gather(first, "fsdp", axis=0, tiled=True)
    vectors = first[:, used:]
    out_full = lax.all_gather(out_weight, "fsdp", axis=0, tiled=True)
    second = pick_hidden(
        place,
        up_weight,
        lax.dynamic_slice_in_dim(down_weight, me * piece, piece, 0),
        shards,
        piece,
        after=x_ctx[1:],
    )
    done = [second]
    second = lax.all_gather(second, "fsdp", axis=0, tiled=True)

    def then(*others):
        return (*done[-1:], *others)

    fronts = []
    parts = []
    for m in range(micros):
        fronts.append(
            front(
                place,
                x_ctx,
                x_fourth[m],
                m,
                first,
                vectors,
                fronts[0][5] if m else None,
                fronts[-1] if m else None,
                heads,
                head_size,
                after=then(),
            )
        )
        done.append(fronts[-1][2])
        parts.append(gather_four(fronts[m][2], m))
    normed, qkv, _, log, tail_log = fronts[-1][:5]
    dy_fourth = []
    for m in range(micros):
        bit = 1 if m % 2 == 0 else 2
        done.append(pass_micro(dy_ctx[3 - bit], m, then(*([] if m else parts[0][1:3]))))
        dy_fourth.append(swap(done[-1], bit))
    middles = []
    for m in range(micros):
        middles.append(
            middle_part(
                place,
                parts[m],
                x_ctx,
                x_fourth[m],
                m,
                out_full,
                vectors,
                middles[0][3] if m else None,
                middles[-1] if m else None,
                heads,
                head_size,
                after=() if m else then(),
            )
        )
    middle, normed_two, attended = middles[-1][:3]
    done.append(normed_two)

    result = feed(place, normed_two, dy_ctx, dy_fourth, second, vectors, after=then())
    hidden_rows, grad_pre, back, up_sum = result[0], result[1], result[2:7], result[7]
    done.append(hidden_rows)
    back = Reduction(list(back[:3]), list(back[3:]))
    grad_second = weights_part(
        hidden_rows, grad_pre, normed_two, dy_ctx, dy_fourth, after=then()
    )
    done.append(grad_second)
    summed_second = lax.psum_scatter(grad_second, "fsdp", scatter_dimension=0, tiled=True)
    shared_second = gather_straight(summed_second)
    done.append(back.relay(then()))
    result = feed_out(hidden_rows, second, wide, after=then())
    done.append(result[0])
    outs = Reduction(list(result[:3]), list(result[3:]))

    grad_middle, grad_attn, traded, tail_grad, row_sums = turn(
        back.got, middle, dy, out_full, vectors, heads, head_size, after=then()
    )
    done.append(grad_attn)
    traded = exchange(traded)
    done.append(outs.relay(then()))
    grad_out_weight = out_weight_part(attended, grad_attn, after=then())
    done.append(grad_out_weight)
    summed_out = lax.psum_scatter(grad_out_weight, "fsdp", scatter_dimension=0, tiled=True)
    result = rear(
        place, qkv, traded, tail_grad, log, tail_log, first, heads, head_size, after=then()
    )
    grad_qkv, column_sums = result[0], result[6]
    done.append(grad_qkv)
    summed = Reduction(list(result[1:4]), list(result[4:6]))
    layer_output = finish(finish_output_kernel, [*outs.got, middle], vectors, BF, after=then())
    done.append(layer_output)
    done.append(summed.relay(then()))
    last = merged_part(
        place,
        normed,
        grad_qkv,
        column_sums,
        row_sums,
        up_sum,
        first,
        vectors,
        heads,
        head_size,
        after=then(*shared_second, summed_out),
    )
    done.append(last)
    summed_last = lax.psum_scatter(last, "fsdp", scatter_dimension=0, tiled=True)
    parts = pass_on(summed_last, then())
    done.append(parts)
    parts = gather_straight(parts)
    input_grad = finish(
        finish_input_kernel, [*summed.got, x, grad_middle], vectors, F32, after=then()
    )
    done.append(input_grad)

    grad_up, grad_down = spread(
        place, shared_second, shards, piece, wide, after=then()
    )
    done.append(grad_up)
    grad_merged, grad_out_weight, *vector_sums = spread_heads(
        place, parts, gather_straight(summed_out), width, head_size, wide, after=then()
    )
    def rows_first(a):
        return a.reshape(micros, 1, wide, rows).transpose(0, 1, 3, 2)

    return (
        rows_first(layer_output),
        rows_first(input_grad),
        vector_sums[0],
        vector_sums[1],
        grad_merged,
        vector_sums[2],
        vector_sums[3],
        grad_out_weight,
        vector_sums[4],
        vector_sums[5],
        vector_sums[6],
        grad_up,
        vector_sums[8],
        grad_down,
        vector_sums[7],
    )


def solution(mesh):
    rows = P(None, "fsdp", "ctx", None)
    matrix = P("fsdp", None)
    vector = P("fsdp")
    in_specs = (
        rows,
        rows,
        vector,
        vector,
        matrix,
        vector,
        vector,
        matrix,
        vector,
        vector,
        vector,
        matrix,
        vector,
        matrix,
        vector,
    )
    out_specs = (rows, rows) + in_specs[2:]
    step = on_device if mesh.shape["ctx"] == 4 else general_device
    return jax.shard_map(
        step, mesh=mesh, in_specs=in_specs, out_specs=out_specs, check_vma=False
    )
```

```python
import functools

import jax
import jax.numpy as jnp
from jax import lax
from jax.experimental import pallas as pl
from jax.experimental.pallas import tpu as pltpu
from jax.sharding import PartitionSpec as P

HEADS = 17
EPSILON = 1e-05
MASKED = -1e30
VMEM_BYTES = 56 * 1024 * 1024
COST = 40
BF = jnp.bfloat16
F32 = jnp.float32


def swap(block, bit):
    size = lax.axis_size("ctx")
    return lax.ppermute(block, "ctx", [(i, i ^ bit) for i in range(size)])


def gather_ctx(block):
    size = lax.axis_size("ctx")
    if size != 4:
        return [block] + [swap(block, r) for r in range(1, size)]
    half = block.shape[0] // 2
    one = swap(block, 1)
    two = swap(block, 2)
    top = swap(two[:half], 1)
    bottom = swap(one[half:], 2)
    return [block, one, two, jnp.concatenate((top, bottom))]


def add_f32(a, b):
    return a.astype(F32) + b.astype(F32)


def reduce_ctx(parts):
    size = lax.axis_size("ctx")
    if size != 4:
        total = parts[0].astype(F32)
        for r in range(1, size):
            total = total + swap(parts[r], r).astype(F32)
        return total
    half = parts[0].shape[0] // 2
    from_one = swap(parts[3][:half], 1)
    from_two = swap(parts[3][half:], 2)
    for_two = jnp.concatenate(
        (add_f32(parts[2][:half], from_one).astype(BF), parts[2][half:].astype(BF))
    )
    for_one = jnp.concatenate(
        (parts[1][:half].astype(BF), add_f32(parts[1][half:], from_two).astype(BF))
    )
    got_one = swap(for_one, 1)
    got_two = swap(for_two, 2)
    return parts[0].astype(F32) + got_one.astype(F32) + got_two.astype(F32)


def trade_ctx(parts):
    return [parts[0]] + [swap(parts[r], r) for r in range(1, len(parts))]


def normal(values):
    centre = values - jnp.mean(values, axis=-1, keepdims=True)
    spread = jnp.mean(centre * centre, axis=-1, keepdims=True)
    rate = lax.rsqrt(spread + EPSILON)
    return centre * rate, rate


def norm_back(normed, rate, scaled):
    return rate * (
        scaled
        - jnp.mean(scaled, axis=-1, keepdims=True)
        - normed * jnp.mean(scaled * normed, axis=-1, keepdims=True)
    )


def dot(a, b, dims):
    return lax.dot_general(a, b, ((dims[0], dims[1]), ((), ())), preferred_element_type=F32)


NN = ((1,), (0,))
NT = ((1,), (1,))


def head_lanes(shape, head, head_size):
    lane = lax.broadcasted_iota(jnp.int32, shape, 1)
    return (lane >= head * head_size) & (lane < (head + 1) * head_size)


def attend_kernel(
    blocks, rows, heads, head_size, place, qkv, out, tail_out, log, tail_log, keys, values_t, tail_kv
):
    width = heads * head_size
    me = place[0]
    for j in range(blocks):
        slot = pl.ds(pl.multiple_of((me ^ j) * rows, rows), rows)
        here = pl.ds(j * rows, rows)
        keys[here, :] = qkv[slot, width : 2 * width]
        values_t[:width, here] = qkv[slot, 2 * width : 3 * width].T
        pair = qkv[slot, 3 * width : 3 * width + 2 * head_size]
        tail_kv[here, :] = pair
        values_t[width:, here] = pair.T
    key_row = lax.broadcasted_iota(jnp.int32, (rows, rows), 0)
    query_row = lax.broadcasted_iota(jnp.int32, (rows, rows), 1)

    def softmax_values(scores, value_rows):
        peak = scores[0].max(axis=0, keepdims=True)
        for s in scores[1:]:
            peak = jnp.maximum(peak, s.max(axis=0, keepdims=True))
        total = jnp.zeros((1, rows), F32)
        product = jnp.zeros((head_size, rows), F32)
        for j, s in enumerate(scores):
            e = jnp.exp(s - peak)
            total = total + e.sum(axis=0, keepdims=True)
            product = product + dot(
                values_t[value_rows, j * rows : (j + 1) * rows], e.astype(BF), NN
            )
        return product / total, peak + jnp.log(total)

    for i in range(blocks):
        slot = pl.ds(pl.multiple_of((me ^ i) * rows, rows), rows)
        query = qkv[slot, :width]
        products = []
        for h in range(heads):
            masked = jnp.where(head_lanes((rows, width), h, head_size), query, jnp.zeros_like(query))
            scores = []
            for j in range(i + 1):
                s = dot(keys[j * rows : (j + 1) * rows, :], masked, NT)
                if j == i:
                    s = jnp.where(key_row <= query_row, s, MASKED)
                scores.append(s)
            product, total = softmax_values(scores, pl.ds(h * head_size, head_size))
            products.append(product)
            log[h : h + 1, i * rows : (i + 1) * rows] = total
        out[slot, :] = jnp.concatenate(products, axis=0).T.astype(BF)

    query = qkv[0:rows, 3 * width + 2 * head_size : 3 * width + 3 * head_size]
    scores = []
    for j in range(blocks):
        s = dot(tail_kv[j * rows : (j + 1) * rows, :head_size], query, NT)
        scores.append(jnp.where(j * rows + key_row <= me * rows + query_row, s, MASKED))
    product, total = softmax_values(scores, pl.ds(width + head_size, head_size))
    tail_out[...] = product.T.astype(BF)
    tail_log[...] = total


def attend(place, qkv, blocks, rows, heads, head_size):
    width = heads * head_size
    length = blocks * rows
    return pl.pallas_call(
        functools.partial(attend_kernel, blocks, rows, heads, head_size),
        out_shape=(
            jax.ShapeDtypeStruct((length, width), BF),
            jax.ShapeDtypeStruct((rows, head_size), BF),
            jax.ShapeDtypeStruct((heads, length), F32),
            jax.ShapeDtypeStruct((1, rows), F32),
        ),
        in_specs=[
            pl.BlockSpec(memory_space=pltpu.SMEM),
            pl.BlockSpec(memory_space=pltpu.VMEM),
        ],
        out_specs=(pl.BlockSpec(memory_space=pltpu.VMEM),) * 4,
        scratch_shapes=[
            pltpu.VMEM((length, width), BF),
            pltpu.VMEM((width + 2 * head_size, length), BF),
            pltpu.VMEM((length, 2 * head_size), BF),
        ],
        compiler_params=pltpu.CompilerParams(vmem_limit_bytes=VMEM_BYTES),
        cost_estimate=pl.CostEstimate(
            flops=10 * 4 * length * length * width, bytes_accessed=6 * length * width, transcendentals=0
        ),
    )(place, qkv)


def attend_back_kernel(
    blocks,
    rows,
    heads,
    head_size,
    place,
    qkv,
    grad,
    tail_grad,
    log,
    tail_log,
    out,
    keys,
    values,
    keys_t,
    tail_kv,
    key_sum,
    value_sum,
    tail_key_sum,
    tail_value_sum,
):
    width = heads * head_size
    me = place[0]
    for j in range(blocks):
        slot = pl.ds(pl.multiple_of((me ^ j) * rows, rows), rows)
        here = pl.ds(j * rows, rows)
        block = qkv[slot, width : 2 * width]
        keys[here, :] = block
        keys_t[:width, here] = block.T
        values[here, :] = qkv[slot, 2 * width : 3 * width]
        pair = qkv[slot, 3 * width : 3 * width + 2 * head_size]
        tail_kv[here, :] = pair
        keys_t[width:, here] = pair.T
    key_row = lax.broadcasted_iota(jnp.int32, (rows, rows), 0)
    query_row = lax.broadcasted_iota(jnp.int32, (rows, rows), 1)
    scale = head_size**-0.5

    for i in range(blocks):
        slot = pl.ds(pl.multiple_of((me ^ i) * rows, rows), rows)
        query = qkv[slot, :width]
        grad_out = grad[slot, :]
        lanes = [head_lanes((rows, width), h, head_size) for h in range(heads)]
        queries = [jnp.where(m, query, jnp.zeros_like(query)) for m in lanes]
        grads = [jnp.where(m, grad_out, jnp.zeros_like(grad_out)) for m in lanes]
        query_parts = []
        for h in range(heads):
            shift = log[h : h + 1, i * rows : (i + 1) * rows]
            probs, weighted = [], []
            delta = jnp.zeros((1, rows), F32)
            for j in range(i + 1):
                here = slice(j * rows, (j + 1) * rows)
                s = dot(keys[here, :], queries[h], NT)
                if j == i:
                    s = jnp.where(key_row <= query_row, s, MASKED)
                p = jnp.exp(s - shift)
                g = dot(values[here, :], grads[h], NT)
                delta = delta + (p * g).sum(axis=0, keepdims=True)
                probs.append(p)
                weighted.append(g)
            part = jnp.zeros((head_size, rows), F32)
            for j in range(i + 1):
                here = slice(j * rows, (j + 1) * rows)
                ds = (probs[j] * (weighted[j] - delta)).astype(BF)
                p = probs[j].astype(BF)
                key_part = dot(ds, queries[h], NN)
                value_part = dot(p, grads[h], NN)
                if h == 0 and j == i:
                    key_sum[here, :] = key_part
                    value_sum[here, :] = value_part
                else:
                    key_sum[here, :] += key_part
                    value_sum[here, :] += value_part
                part = part + dot(keys_t[h * head_size : (h + 1) * head_size, here], ds, NN)
            query_parts.append(part)
        out[slot, :width] = (jnp.concatenate(query_parts, axis=0) * scale).T.astype(BF)

    query = qkv[0:rows, 3 * width + 2 * head_size : 3 * width + 3 * head_size]
    grad_out = tail_grad[...]
    probs, weighted = [], []
    delta = jnp.zeros((1, rows), F32)
    for j in range(blocks):
        here = slice(j * rows, (j + 1) * rows)
        s = dot(tail_kv[here, :head_size], query, NT)
        s = jnp.where(j * rows + key_row <= me * rows + query_row, s, MASKED)
        p = jnp.exp(s - tail_log[...])
        g = dot(tail_kv[here, head_size:], grad_out, NT)
        delta = delta + (p * g).sum(axis=0, keepdims=True)
        probs.append(p)
        weighted.append(g)
    part = jnp.zeros((head_size, rows), F32)
    for j in range(blocks):
        here = slice(j * rows, (j + 1) * rows)
        slot = pl.ds(pl.multiple_of((me ^ j) * rows, rows), rows)
        ds = (probs[j] * (weighted[j] - delta)).astype(BF)
        key_part = dot(ds, query, NN)
        value_part = dot(probs[j].astype(BF), grad_out, NN)
        part = part + dot(keys_t[width : width + head_size, here], ds, NN)
        out[slot, width : 2 * width] = key_sum[here, :].astype(BF)
        out[slot, 2 * width : 3 * width] = value_sum[here, :].astype(BF)
        out[slot, 3 * width : 3 * width + 2 * head_size] = jnp.concatenate(
            (key_part, value_part), axis=1
        ).astype(BF)
    tail_columns = slice(3 * width + 2 * head_size, 3 * width + 3 * head_size)
    out[0:rows, tail_columns] = (part * scale).T.astype(BF)
    for j in range(1, blocks):
        out[j * rows : (j + 1) * rows, tail_columns] = jnp.zeros((rows, head_size), BF)


def attend_back(place, qkv, grad, tail_grad, log, tail_log, blocks, rows, heads, head_size):
    width = heads * head_size
    length = blocks * rows
    return pl.pallas_call(
        functools.partial(attend_back_kernel, blocks, rows, heads, head_size),
        out_shape=jax.ShapeDtypeStruct(qkv.shape, BF),
        in_specs=[pl.BlockSpec(memory_space=pltpu.SMEM)]
        + [pl.BlockSpec(memory_space=pltpu.VMEM)] * 5,
        out_specs=pl.BlockSpec(memory_space=pltpu.VMEM),
        scratch_shapes=[
            pltpu.VMEM((length, width), BF),
            pltpu.VMEM((length, width), BF),
            pltpu.VMEM((width + 2 * head_size, length), BF),
            pltpu.VMEM((length, 2 * head_size), BF),
            pltpu.VMEM((length, width), F32),
            pltpu.VMEM((length, width), F32),
            pltpu.VMEM((length, head_size), F32),
            pltpu.VMEM((length, head_size), F32),
        ],
        compiler_params=pltpu.CompilerParams(vmem_limit_bytes=VMEM_BYTES),
        cost_estimate=pl.CostEstimate(
            flops=10 * 10 * length * length * width, bytes_accessed=9 * length * width, transcendentals=0
        ),
    )(place, qkv, grad, tail_grad, log, tail_log)


def mlp_kernel(
    normed, grad, up, down, bias, hidden_out, grad_pre_out, part_out, grad_part_out, bias_out
):
    pre = dot(normed[...], up[...], NN) + bias[...]
    bell = jnp.exp(-0.5 * pre * pre) * 0.3989422804014327
    below = 0.5 + 0.5 * lax.erf(pre * 0.7071067811865476)
    hidden = (pre * below).astype(BF)
    hidden_out[...] = hidden
    part_out[...] = dot(hidden, down[...], NN).astype(BF)
    grad_pre = ((below + pre * bell) * dot(grad[...], down[...], NT)).astype(BF)
    grad_pre_out[...] = grad_pre
    grad_part_out[...] = dot(grad_pre, up[...], NT).astype(BF)
    sums = grad_pre.astype(F32).sum(axis=0, keepdims=True)

    @pl.when(pl.program_id(0) == 0)
    def _():
        bias_out[...] = sums

    @pl.when(pl.program_id(0) > 0)
    def _():
        bias_out[...] += sums


def mlp(normed, grad, up, down, bias, rows):
    length, wide = normed.shape
    hidden = up.shape[1]
    row_block = pl.BlockSpec((rows, wide), lambda i: (i, 0))
    hidden_block = pl.BlockSpec((rows, hidden), lambda i: (i, 0))
    whole = pl.BlockSpec(memory_space=pltpu.VMEM)
    return pl.pallas_call(
        mlp_kernel,
        grid=(length // rows,),
        out_shape=(
            jax.ShapeDtypeStruct((length, hidden), BF),
            jax.ShapeDtypeStruct((length, hidden), BF),
            jax.ShapeDtypeStruct((length, wide), BF),
            jax.ShapeDtypeStruct((length, wide), BF),
            jax.ShapeDtypeStruct((1, hidden), F32),
        ),
        in_specs=[row_block, row_block, whole, whole, whole],
        out_specs=(
            hidden_block,
            hidden_block,
            row_block,
            row_block,
            pl.BlockSpec((1, hidden), lambda i: (0, 0)),
        ),
        compiler_params=pltpu.CompilerParams(vmem_limit_bytes=VMEM_BYTES),
        cost_estimate=pl.CostEstimate(
            flops=12 * length * wide * hidden,
            bytes_accessed=2 * (6 * length * wide + 2 * wide * hidden),
            transcendentals=0,
        ),
    )(normed, grad, up, down, bias)


def general_device(
    layer_input,
    output_grad,
    attn_gain,
    attn_shift,
    merged_weight,
    query_bias,
    value_bias,
    out_weight,
    out_bias,
    mlp_gain,
    mlp_shift,
    up_weight,
    up_bias,
    down_weight,
    down_bias,
):
    micros = layer_input.shape[0]
    rows = layer_input.shape[2]
    wide = layer_input.shape[3]
    head_size = wide // HEADS
    blocks = lax.axis_size("ctx")
    shards = lax.axis_size("fsdp")
    me = lax.axis_index("ctx")
    heads = HEADS // blocks
    width = heads * head_size
    main = blocks * width
    own = merged_weight.shape[0]
    hidden = up_weight.shape[1]
    piece = hidden // shards // blocks
    quads = hidden // wide
    used = 3 * width + 3 * head_size
    assert HEADS - heads * blocks == 1
    place = me.astype(jnp.int32).reshape(1)
    relative = jnp.arange(blocks, dtype=jnp.int32) ^ me
    start = me * width

    vectors = jnp.concatenate(
        (
            attn_gain,
            attn_shift,
            query_bias,
            value_bias,
            out_bias,
            mlp_gain,
            mlp_shift,
            down_bias,
            up_bias,
        )
    ).reshape(8 + quads, own)
    first = jnp.concatenate(
        (
            lax.dynamic_slice_in_dim(merged_weight, start, width, 1),
            lax.dynamic_slice_in_dim(merged_weight, wide + start, width, 1),
            lax.dynamic_slice_in_dim(merged_weight, 2 * wide + start, width, 1),
            merged_weight[:, wide + main : 2 * wide],
            merged_weight[:, 2 * wide + main :],
            merged_weight[:, main:wide],
            vectors.T,
        ),
        axis=1,
    )
    first = lax.all_gather(first, "fsdp", axis=0, tiled=True)
    merged_own = first[:, :used]
    vectors = first[:, used:].T.astype(F32)
    gain_one, shift_one, query_row, value_row, out_row, gain_two, shift_two, down_row = [
        vectors[i] for i in range(8)
    ]
    up_row = (
        vectors[8:]
        .reshape(quads, shards, own)
        .transpose(1, 0, 2)
        .reshape(shards, blocks, piece)
    )
    up_row = lax.dynamic_index_in_dim(up_row, me, 1, keepdims=False).reshape(1, shards * piece)
    zero_tail = jnp.zeros((head_size,), F32)
    merged_row = jnp.concatenate(
        (
            lax.dynamic_slice_in_dim(query_row, start, width),
            jnp.zeros((width,), F32),
            lax.dynamic_slice_in_dim(value_row, start, width),
            zero_tail,
            value_row[main:],
            query_row[main:],
        )
    )
    scale_row = jnp.concatenate(
        (
            jnp.full((width,), head_size**-0.5, BF),
            jnp.ones((2 * width + 2 * head_size,), BF),
            jnp.full((head_size,), head_size**-0.5, BF),
        )
    )
    out_full = lax.all_gather(out_weight, "fsdp", axis=0, tiled=True)
    up_own = lax.dynamic_index_in_dim(
        up_weight.reshape(own, shards, blocks, piece), me, 2, keepdims=False
    ).reshape(own, shards * piece)
    down_own = lax.dynamic_slice_in_dim(down_weight, me * piece, piece, 0)
    up_own = lax.all_gather(up_own, "fsdp", axis=0, tiled=True)
    down_own = lax.all_gather(down_own, "fsdp", axis=0, tiled=True)

    values = [layer_input[m, 0] for m in range(micros)]
    values_ctx = [gather_ctx(v) for v in values]
    grads = [output_grad[m, 0] for m in range(micros)]
    grads_ctx = [jnp.concatenate(gather_ctx(g)) for g in grads]

    unscaled, normed, qkv, log, tail_log, attended, middle, normed_two = ([] for _ in range(8))
    for m in range(micros):
        centred, rate = normal(jnp.concatenate(values_ctx[m]).astype(F32))
        unscaled.append((centred, rate))
        normed.append((centred * gain_one + shift_one).astype(BF))
        rows_out = jnp.dot(normed[m], merged_own, preferred_element_type=F32) + merged_row
        qkv.append(rows_out.astype(BF) * scale_row)
        out, tail_out, total, tail_total = attend(place, qkv[m], blocks, rows, heads, head_size)
        log.append(total)
        tail_log.append(tail_total)
        traded = jnp.stack(trade_ctx(list(out.reshape(blocks, rows, width))))
        traded = jnp.take(traded, relative, axis=0).transpose(1, 0, 2).reshape(rows, main)
        attended.append(jnp.concatenate((traded, tail_out), axis=1))
        middle.append(
            values[m].astype(F32)
            + jnp.dot(attended[m], out_full, preferred_element_type=F32)
            + out_row
        )
        centred, rate = normal(middle[m])
        normed_two.append((centred * gain_two + shift_two).astype(BF))

    hiddens, grad_pres, normed_two_ctx, layer_output, grad_middle = ([] for _ in range(5))
    grad_up_row = 0.0
    grad_gain_two = 0.0
    grad_shift_two = 0.0
    for m in range(micros):
        normed_two_ctx.append(jnp.concatenate(gather_ctx(normed_two[m])))
        act, grad_pre, part, grad_part, bias_part = mlp(
            normed_two_ctx[m], grads_ctx[m], up_own, down_own, up_row, rows
        )
        hiddens.append(act)
        grad_pres.append(grad_pre)
        grad_up_row = grad_up_row + bias_part
        grad_normed = reduce_ctx(list(grad_part.reshape(blocks, rows, wide)))
        centred, rate = normal(middle[m])
        grad_gain_two = grad_gain_two + jnp.sum(grad_normed * centred, axis=0)
        grad_shift_two = grad_shift_two + jnp.sum(grad_normed, axis=0)
        grad_middle.append(
            grads[m].astype(F32) + norm_back(centred, rate, grad_normed * gain_two)
        )
        total = reduce_ctx(list(part.reshape(blocks, rows, wide)))
        layer_output.append((middle[m] + total + down_row).astype(BF))
    grad_down = sum(dot(a, g, ((0,), (0,))) for a, g in zip(hiddens, grads_ctx, strict=True))
    grad_up = sum(dot(n, g, ((0,), (0,))) for n, g in zip(normed_two_ctx, grad_pres, strict=True))
    grad_down = lax.psum_scatter(grad_down.astype(BF), "fsdp", scatter_dimension=0, tiled=True)
    grad_up = lax.psum_scatter(grad_up.astype(BF), "fsdp", scatter_dimension=0, tiled=True)

    grad_out_weight = 0.0
    grad_out_row = 0.0
    grad_down_row = 0.0
    grad_merged = 0.0
    grad_merged_row = 0.0
    grad_gain_one = 0.0
    grad_shift_one = 0.0
    input_grad = []
    for m in range(micros):
        grad_attn = grad_middle[m].astype(BF)
        grad_out_weight = grad_out_weight + dot(attended[m], grad_attn, ((0,), (0,)))
        grad_out_row = grad_out_row + jnp.sum(grad_attn.astype(F32), axis=0)
        grad_down_row = grad_down_row + jnp.sum(grads[m].astype(F32), axis=0)
        grad_attended = dot(grad_attn, out_full, NT).astype(BF)
        to_trade = grad_attended[:, :main].reshape(rows, blocks, width).transpose(1, 0, 2)
        to_trade = jnp.take(to_trade, relative, axis=0)
        traded = jnp.concatenate(trade_ctx(list(to_trade)))
        grad_qkv = attend_back(
            place,
            qkv[m],
            traded,
            grad_attended[:, main:],
            log[m],
            tail_log[m],
            blocks,
            rows,
            heads,
            head_size,
        )
        grad_merged = grad_merged + dot(normed[m], grad_qkv, ((0,), (0,)))
        grad_merged_row = grad_merged_row + jnp.sum(grad_qkv.astype(F32), axis=0)
        grad_part = dot(grad_qkv, merged_own, NT)
        centred, rate = unscaled[m]
        grad_gain_one = grad_gain_one + jnp.sum(grad_part * centred, axis=0)
        grad_shift_one = grad_shift_one + jnp.sum(grad_part, axis=0)
        grad_normed = reduce_ctx(list(grad_part.astype(BF).reshape(blocks, rows, wide)))
        input_grad.append(
            grad_middle[m] + norm_back(centred[:rows], rate[:rows], grad_normed * gain_one)
        )

    def placed(part, tail):
        row = lax.dynamic_update_slice_in_dim(jnp.zeros((main,), F32), part, start, 0)
        return jnp.concatenate((row, tail))

    up_sums = lax.dynamic_update_slice_in_dim(
        jnp.zeros((shards, blocks, piece), F32), grad_up_row.reshape(shards, 1, piece), me, 1
    )
    up_sums = up_sums.reshape(shards, quads, own).transpose(1, 0, 2).reshape(quads, wide)
    vector_sums = jnp.concatenate(
        (
            jnp.stack(
                (
                    grad_gain_one,
                    grad_shift_one,
                    placed(grad_merged_row[:width], grad_merged_row[used - head_size :]),
                    placed(
                        grad_merged_row[2 * width : 3 * width],
                        grad_merged_row[3 * width + head_size : 3 * width + 2 * head_size],
                    ),
                    grad_out_row,
                    grad_gain_two,
                    grad_shift_two,
                    grad_down_row,
                )
            ),
            up_sums,
        )
    )
    last = jnp.concatenate((grad_merged, vector_sums.T), axis=1).astype(BF)
    last = lax.psum_scatter(last, "fsdp", scatter_dimension=0, tiled=True)
    grad_out_weight = lax.psum_scatter(
        grad_out_weight.astype(BF), "fsdp", scatter_dimension=0, tiled=True
    ).astype(F32)
    bit = 1
    while bit < blocks:
        grad_out_weight = grad_out_weight + swap(grad_out_weight.astype(BF), bit).astype(F32)
        bit *= 2

    def absolute(parts):
        return jnp.take(jnp.stack(parts), relative, axis=0).astype(F32)

    last = absolute(gather_ctx(last))
    tails = jnp.sum(last[:, :, 3 * width :], axis=0)

    def columns(index, tail):
        body = last[:, :, index * width : (index + 1) * width].transpose(1, 0, 2)
        return [body.reshape(own, main), tails[:, tail * head_size : (tail + 1) * head_size]]

    grad_merged = jnp.concatenate(columns(0, 2) + columns(1, 0) + columns(2, 1), axis=1)
    vector_sums = tails[:, 3 * head_size :].T
    grad_up = absolute(gather_ctx(grad_up)).reshape(blocks, own, shards, piece)
    grad_up = grad_up.transpose(1, 2, 0, 3).reshape(own, hidden)
    grad_down = absolute(gather_ctx(grad_down)).reshape(blocks * piece, wide)
    return (
        jnp.stack(layer_output)[:, None],
        jnp.stack(input_grad)[:, None],
        vector_sums[0],
        vector_sums[1],
        grad_merged,
        vector_sums[2],
        vector_sums[3],
        grad_out_weight,
        vector_sums[4],
        vector_sums[5],
        vector_sums[6],
        grad_up,
        vector_sums[8:].reshape(quads * own),
        grad_down,
        vector_sums[7],
    )


def gather_blocks(array):
    one = swap(array, 1)
    two = swap(array, 2)
    fourth = [swap(two[m], 1) if m % 2 == 0 else swap(one[m], 2) for m in range(array.shape[0])]
    return [array, one, two], fourth


def exchange(parts):
    return lax.all_to_all(parts, "ctx", 0, 0, tiled=True)


def gather_straight(block):
    return [block] + [swap(block, r) for r in range(1, 4)]


def gather_four(block, which):
    one = swap(block, 1)
    two = swap(block, 2)
    return [block, one, two, swap(two, 1) if which % 2 == 0 else swap(one, 2)]


class Reduction:
    def __init__(self, parts, fourths):
        self.parts = parts
        self.coming = [swap(fourths[0], 1), swap(fourths[1], 2)]

    def relay(self, after):
        own, one, two = self.parts
        one, two = relay(one, two, *self.coming, after)
        self.got = [own, swap(one, 1), swap(two, 2)]
        return one


def whole_spec():
    return pl.BlockSpec(memory_space=pltpu.VMEM)


def scalar_spec():
    return pl.BlockSpec(memory_space=pltpu.SMEM)


def any_spec():
    return pl.BlockSpec(memory_space=pl.ANY)


def micro_spec(shape, which):
    rest = tuple(shape[1:])
    return pl.BlockSpec((1,) + rest, lambda i: (which,) + (0,) * len(rest))


def each_spec(dims):
    rest = tuple(dims[1:])
    return pl.BlockSpec((1,) + rest, lambda i: (i,) + (0,) * len(rest))


def call(
    kernel,
    operands,
    in_specs,
    outs,
    out_specs,
    flops,
    scratch=(),
    after=(),
    old=None,
    cost=COST,
    steps=1,
):
    extra = list(after)
    aliases = {}
    for index, array in (old or {}).items():
        aliases[len(operands) + len(extra)] = index
        extra.append(array)
    count = len(operands)

    def body(*refs):
        kernel(*refs[:count], *refs[count + len(extra) :])

    moved = sum(o.size * o.dtype.itemsize for o in (*operands, *outs))
    return pl.pallas_call(
        body,
        grid=(steps,),
        out_shape=tuple(outs),
        in_specs=list(in_specs) + [any_spec()] * len(extra),
        out_specs=tuple(out_specs),
        scratch_shapes=list(scratch),
        input_output_aliases=aliases,
        compiler_params=pltpu.CompilerParams(vmem_limit_bytes=VMEM_BYTES),
        cost_estimate=pl.CostEstimate(
            flops=cost * flops, bytes_accessed=cost * moved, transcendentals=0
        ),
        name=getattr(kernel, "func", kernel).__name__,
    )(*operands, *extra)


def shape(*sizes, dtype=BF):
    return jax.ShapeDtypeStruct(sizes, dtype)


def relay_kernel(one, two, first, second, one_out, two_out):
    two_out[0] = add_f32(two[0], first[...]).astype(BF)
    one_out[0] = add_f32(one[0], second[...]).astype(BF)


def relay(one, two, first, second, after):
    count = len(after)
    dims = one.shape
    return pl.pallas_call(
        lambda *refs: relay_kernel(*refs[:4], *refs[4 + count :]),
        grid=(1,),
        out_shape=(shape(*dims), shape(*dims)),
        in_specs=[micro_spec(dims, 1), micro_spec(dims, 0)] + [whole_spec()] * 2 + [any_spec()] * count,
        out_specs=(micro_spec(dims, 1), micro_spec(dims, 0)),
        input_output_aliases={0: 0, 1: 1},
        compiler_params=pltpu.CompilerParams(vmem_limit_bytes=VMEM_BYTES),
        cost_estimate=pl.CostEstimate(
            flops=dims[1] * dims[2], bytes_accessed=12 * dims[1] * dims[2], transcendentals=0
        ),
        name="relay_kernel",
    )(one, two, first, second, *after)


def pass_kernel(source, out):
    out[...] = source[...]


def pass_micro_kernel(source, out):
    out[...] = source[0]


def pass_micro(array, which, after):
    return call(
        pass_micro_kernel,
        [array],
        [micro_spec(array.shape, which)],
        [shape(*array.shape[1:])],
        [whole_spec()],
        0,
        after=after,
        cost=0,
    )[0]


def pass_on(array, after):
    return call(
        pass_kernel,
        [array],
        [whole_spec()],
        [shape(*array.shape)],
        [whole_spec()],
        0,
        after=after,
        cost=0,
    )[0]


def padded(columns):
    return (columns + 127) // 128 * 128


def pick_kernel(width, head_size, wide, place, weight, *refs):
    vectors, out = refs[:-1], refs[-1]
    own = out.shape[0]
    main = 4 * width
    for k in range(4):

        @pl.when(place[0] == k)
        def _(k=k):
            for part in range(3):
                begin = part * wide + k * width
                out[:, part * width : (part + 1) * width] = weight[:, begin : begin + width]

    for place_to, begin in enumerate((wide + main, 2 * wide + main, main)):
        at = 3 * width + place_to * head_size
        out[:, at : at + head_size] = weight[:, begin : begin + head_size]
    at = 3 * width + 3 * head_size
    rows = []
    for vector in vectors:
        row = vector[...].astype(F32).reshape(1, vector.shape[0])
        rows += [row[:, begin : begin + own] for begin in range(0, vector.shape[0], own)]
    row_id = lax.broadcasted_iota(jnp.int32, (len(rows), own), 0)
    table = jnp.zeros((len(rows), own), F32)
    for index, row in enumerate(rows):
        table = jnp.where(row_id == index, row, table)
    out[:, at:] = table.T.astype(BF)


def pick(place, weight, vectors, width, head_size):
    own, wide = weight.shape[0], weight.shape[1] // 3
    columns = 3 * width + 3 * head_size + sum(v.shape[0] for v in vectors) // own
    return call(
        functools.partial(pick_kernel, width, head_size, wide),
        [place, weight, *vectors],
        [scalar_spec()] + [whole_spec()] * (1 + len(vectors)),
        [shape(own, columns)],
        [whole_spec()],
        0,
    )[0]


def pick_hidden_kernel(shards, piece, second, place, up, down, out):
    for k in range(4):

        @pl.when(place[0] == k)
        def _(k=k):
            for f in range(shards):
                begin = (f * 4 + k) * piece
                out[:, f * piece : (f + 1) * piece] = up[:, begin : begin + piece]

    rows = out.shape[0]
    filled = shards * piece
    out[:, filled:second] = jnp.zeros((rows, second - filled), BF)
    out[:, second : second + down.shape[1]] = down[...]
    end = second + down.shape[1]
    out[:, end:] = jnp.zeros((rows, out.shape[1] - end), BF)


def pick_hidden(place, up, down, shards, piece, after=()):
    own = up.shape[0]
    second = padded(shards * piece)
    return call(
        functools.partial(pick_hidden_kernel, shards, piece, second),
        [place, up, down],
        [scalar_spec(), whole_spec(), whole_spec()],
        [shape(own, second + padded(down.shape[1]))],
        [whole_spec()],
        0,
        after=after,
        cost=0,
    )[0]


def feature_mean(v):
    return jnp.sum(v, axis=0, keepdims=True) * (1.0 / v.shape[0])


def normal_columns(values):
    centre = values - feature_mean(values)
    rate = lax.rsqrt(feature_mean(centre * centre) + EPSILON)
    return centre * rate, rate


def norm_back_columns(normed, rate, scaled):
    return rate * (scaled - feature_mean(scaled) - normed * feature_mean(scaled * normed))


def column(vectors, index):
    return vectors[:, index : index + 1].astype(F32)


def front_kernel(heads, head_size, first_call, place, *refs):
    x = refs[:4]
    weight = refs[4]
    refs = refs[5:]
    if first_call:
        normed_out, qkv, attended, log, tail_log, turned, vectors, keys = refs
        turned[...] = weight[:, : turned.shape[0]].T
        vectors[...] = weight[:, turned.shape[0] :]
    else:
        turned, vectors, normed_out, qkv, attended, log, tail_log, keys = refs
    normed_out, qkv, log, tail_log = (ref.at[0] for ref in (normed_out, qkv, log, tail_log))
    wide, rows = x[3].shape
    width = heads * head_size
    used = 3 * width + 3 * head_size
    me = place[0]
    gain, shift = column(vectors, 0), column(vectors, 1)
    mine = pl.ds(pl.multiple_of(me * width, width), width)
    query_bias = vectors[mine, 2:3].astype(F32)
    value_bias = vectors[mine, 3:4].astype(F32)
    last = slice(4 * width, 4 * width + head_size)
    bias = jnp.concatenate(
        (
            query_bias,
            jnp.zeros((width, 1), F32),
            value_bias,
            jnp.zeros((head_size, 1), F32),
            vectors[last, 3:4].astype(F32),
            vectors[last, 2:3].astype(F32),
        ),
        axis=0,
    )
    row = lax.broadcasted_iota(jnp.int32, (used, 1), 0)
    scale = jnp.where((row < width) | (row >= used - head_size), head_size**-0.5, 1.0)
    for r in range(4):
        normed, _ = normal_columns((x[r][...] if r == 3 else x[r][0]).astype(F32))
        normed_out[:, r * rows : (r + 1) * rows] = normed.astype(BF)
        full = (normed * gain + shift).astype(BF)
        projected = dot(turned[...], full, NN) + bias
        projected = (projected.astype(BF).astype(F32) * scale).astype(BF)
        qkv[:, r * rows : (r + 1) * rows] = projected
        here = slice(r * rows, (r + 1) * rows)
        keys[here, :width] = projected[width : 2 * width, :].T
        keys[here, width:] = projected[3 * width : 3 * width + 2 * head_size, :].T
    key_row = lax.broadcasted_iota(jnp.int32, (rows, rows), 0)
    query_row = lax.broadcasted_iota(jnp.int32, (rows, rows), 1)
    head_row = lax.broadcasted_iota(jnp.int32, (width, rows), 0) // head_size

    def slot(j):
        return pl.ds(pl.multiple_of((me ^ j) * rows, rows), rows)

    def softmax_values(scores, value_rows):
        peak = scores[0].max(axis=0, keepdims=True)
        for s in scores[1:]:
            peak = jnp.maximum(peak, s.max(axis=0, keepdims=True))
        total = jnp.zeros((1, rows), F32)
        product = jnp.zeros((head_size, rows), F32)
        for j, s in enumerate(scores):
            e = jnp.exp(s - peak)
            total = total + e.sum(axis=0, keepdims=True)
            product = product + dot(qkv[value_rows, slot(j)], e.astype(BF), NN)
        return product / total, peak + jnp.log(total)

    for i in range(4):
        query = qkv[:width, slot(i)]
        for h in range(heads):
            masked = jnp.where(head_row == h, query, jnp.zeros_like(query))
            scores = []
            for j in range(i + 1):
                s = dot(keys[slot(j), :width], masked, NN)
                if j == i:
                    s = jnp.where(key_row <= query_row, s, MASKED)
                scores.append(s)
            begin = 2 * width + h * head_size
            product, total = softmax_values(scores, slice(begin, begin + head_size))
            band = slice(h * head_size, (h + 1) * head_size)
            attended[band, i * rows : (i + 1) * rows] = product.astype(BF)
            log[h : h + 1, i * rows : (i + 1) * rows] = total
    begin = 3 * width + head_size
    query = qkv[begin + head_size :, 0:rows]
    query = jnp.concatenate((query, jnp.zeros_like(query)), axis=0)
    scores = []
    for j in range(4):
        s = dot(keys[slot(j), width:], query, NN)
        scores.append(jnp.where(j * rows + key_row <= me * rows + query_row, s, MASKED))
    product, total = softmax_values(scores, slice(begin, begin + head_size))
    quarter = head_size // 4
    for j in range(4):
        attended[width:, j * rows : (j + 1) * rows] = product[
            j * quarter : (j + 1) * quarter, :
        ].astype(BF)
    tail_log[...] = total


def front(place, x, fourth, which, weight, turned, vectors, old, heads, head_size, after=()):
    wide, rows = fourth.shape
    length = 4 * rows
    width = heads * head_size
    used = 3 * width + 3 * head_size
    first_call = turned is None
    micros = x[0].shape[0]
    outs = [
        shape(micros, wide, length),
        shape(micros, used, length),
        shape(width + head_size // 4, length),
        shape(micros, heads, length, dtype=F32),
        shape(micros, 1, rows, dtype=F32),
    ]
    out_specs = [micro_spec(o.shape, which) if len(o.shape) == 3 else whole_spec() for o in outs]
    operands = [place, *x, fourth, weight]
    in_specs = [scalar_spec()] + [micro_spec(x[0].shape, which)] * 3 + [whole_spec()] * 2
    if first_call:
        outs += [shape(used, wide), shape(wide, weight.shape[1] - used)]
        out_specs += [whole_spec()] * 2
    else:
        operands += [turned, vectors]
        in_specs += [whole_spec()] * 2
    return call(
        functools.partial(front_kernel, heads, head_size, first_call),
        operands,
        in_specs,
        outs,
        out_specs,
        12_000_000_000,
        old=None if old is None else {k: old[k] for k in (0, 1, 3, 4)},
        scratch=[pltpu.VMEM((length, width + 2 * head_size), BF)],
        after=after,
        cost=2,
    )


def middle_kernel(heads, head_size, first_call, place, *refs):
    parts = refs[:4]
    x = refs[4:8]
    weight, vectors = refs[8:10]
    refs = refs[10:]
    if first_call:
        middle, normed_two, attended, turned = refs
        turned[...] = weight[...].T
    else:
        turned, middle, normed_two, attended = refs
    middle, normed_two = middle.at[0], normed_two.at[0]
    wide, rows = x[3].shape
    width = heads * head_size
    me = place[0]
    own = pl.ds(pl.multiple_of(me * rows, rows), rows)
    for source in range(4):
        band = pl.ds(pl.multiple_of((me ^ source) * width, width), width)
        attended[0, band, :] = parts[source][:width, own]
    for r in range(4):
        lanes = pl.ds(pl.multiple_of((me ^ r) * rows, rows), rows)
        sums = (x[r][...] if r == 3 else x[r][0]).astype(F32) + column(vectors, 4)
        for source in range(4):
            band = pl.ds(pl.multiple_of((me ^ source) * width, width), width)
            sums = sums + dot(turned[:, band], parts[source][:width, lanes], NN)
        tail = jnp.concatenate(
            [parts[r][width:, j * rows : (j + 1) * rows] for j in range(4)], axis=0
        )
        sums = sums + dot(turned[:, 4 * width :], tail, NN)
        if r == 0:
            attended[0, 4 * width :, :] = tail
        if r == 0:
            middle[...] = sums
        normed, _ = normal_columns(sums)
        normed = normed * column(vectors, 5) + column(vectors, 6)
        normed_two[:, r * rows : (r + 1) * rows] = normed.astype(BF)


def middle_part(
    place, parts, x, fourth, which, weight, vectors, turned, old, heads, head_size, after=()
):
    wide, rows = fourth.shape
    first_call = turned is None
    operands = [place, *parts, *x, fourth, weight, vectors]
    in_specs = [scalar_spec()] + [whole_spec()] * 4 + [micro_spec(x[0].shape, which)] * 3
    in_specs += [whole_spec()] * 3
    dims = x[0].shape
    outs = [shape(*dims, dtype=F32), shape(dims[0], wide, 4 * rows), shape(*dims)]
    out_specs = [micro_spec(o.shape, which) for o in outs]
    if first_call:
        outs.append(shape(weight.shape[1], weight.shape[0]))
        out_specs.append(whole_spec())
    else:
        operands.append(turned)
        in_specs.append(whole_spec())
    return call(
        functools.partial(middle_kernel, heads, head_size, first_call),
        operands,
        in_specs,
        outs,
        out_specs,
        8 * rows * wide * wide,
        after=after,
        old=None if old is None else {k: old[k] for k in range(3)},
        cost=6,
    )


def keep_fourth(step, fourths, value):
    for m, target in enumerate(fourths):

        @pl.when(step == m)
        def _(target=target):
            target[...] = value


def feed_kernel(second, place, normed, *refs):
    grad = refs[:3]
    fourths = refs[3:5]
    weights, vectors = refs[5:7]
    kept_hidden, kept_grad_pre = refs[7].at[0], refs[8].at[0]
    grad_parts = refs[9:12]
    part_fourths = refs[12:14]
    bias_out, turned = refs[14:]
    step = pl.program_id(0)
    wide, rows = fourths[0].shape
    hidden_size = turned.shape[0]

    @pl.when(step == 0)
    def _():
        turned[...] = weights[:, :hidden_size].T

    lane = lax.broadcasted_iota(jnp.int32, (hidden_size, 4), 1)
    bias = jnp.where(lane == place[0], vectors[:, 8:12].astype(F32), 0.0)
    bias = bias.sum(axis=1, keepdims=True)
    total = jnp.zeros((hidden_size, rows), F32)
    for r in range(4):
        here = slice(r * rows, (r + 1) * rows)
        pre = dot(turned[...], normed[0, :, here], NN) + bias
        bell = jnp.exp(-0.5 * pre * pre) * 0.3989422804014327
        below = 0.5 + 0.5 * lax.erf(pre * 0.7071067811865476)
        kept_hidden[:, here] = (pre * below).astype(BF)
        back = jnp.where(step == 0, fourths[0][...], fourths[1][...]) if r == 3 else grad[r][0]
        grad_pre = (below + pre * bell) * dot(weights[:, second : second + wide], back, NN)
        grad_pre = grad_pre.astype(BF)
        kept_grad_pre[:, here] = grad_pre
        part = dot(weights[:, :hidden_size], grad_pre, NN).astype(BF)
        if r == 3:
            keep_fourth(step, part_fourths, part)
        else:
            grad_parts[r][0] = part
        total = total + grad_pre.astype(F32)
    total = total.sum(axis=1, keepdims=True)

    @pl.when(step == 0)
    def _():
        bias_out[...] = total

    @pl.when(step > 0)
    def _():
        bias_out[...] += total


def feed(place, normed, grads, fourths, weights, vectors, after=()):
    wide, rows = fourths[0].shape
    micros = len(fourths)
    hidden_size = weights.shape[0]
    length = 4 * rows
    dims = (micros, wide, rows)
    operands = [place, normed, *grads, *fourths, weights, vectors]
    in_specs = [scalar_spec(), each_spec(normed.shape)] + [each_spec(dims)] * 3
    in_specs += [whole_spec()] * (micros + 2)
    outs = [shape(micros, hidden_size, length)] * 2 + [shape(*dims)] * 3
    out_specs = [each_spec(o.shape) for o in outs] + [whole_spec()] * (micros + 1)
    outs += [shape(wide, rows)] * micros + [shape(hidden_size, 1, dtype=F32)]
    return call(
        functools.partial(feed_kernel, padded(hidden_size)),
        operands,
        in_specs,
        outs,
        out_specs,
        6 * micros * length * wide * hidden_size,
        scratch=[pltpu.VMEM((hidden_size, wide), BF)],
        after=after,
        steps=micros,
    )


def feed_out_kernel(second, hidden, weights, *refs):
    parts, fourths, turned = refs[:3], refs[3:-1], refs[-1]
    step = pl.program_id(0)

    @pl.when(step == 0)
    def _():
        turned[...] = weights[:, second : second + turned.shape[0]].T

    rows = fourths[0].shape[1]
    for r in range(4):
        here = slice(r * rows, (r + 1) * rows)
        part = dot(turned[...], hidden[0, :, here], NN).astype(BF)
        if r == 3:
            keep_fourth(step, fourths, part)
        else:
            parts[r][0] = part


def feed_out(hidden, weights, wide, after=()):
    micros, hidden_size, length = hidden.shape
    rows = length // 4
    outs = [shape(micros, wide, rows)] * 3
    return call(
        functools.partial(feed_out_kernel, padded(hidden_size)),
        [hidden, weights],
        [each_spec(hidden.shape), whole_spec()],
        outs + [shape(wide, rows)] * micros,
        [each_spec(o.shape) for o in outs] + [whole_spec()] * micros,
        2 * micros * length * wide * hidden_size,
        scratch=[pltpu.VMEM((wide, hidden_size), BF)],
        after=after,
        steps=micros,
    )


def weights_kernel(second, hidden, grad_pre, normed, *refs):
    grads, fourths = refs[:3], refs[3:5]
    out, left, right = refs[5:]
    micros, hidden_size, length = hidden.shape
    wide, rows = fourths[0].shape
    for m in range(micros):
        here = slice(m * length, (m + 1) * length)
        left[:, here] = normed[m]
        right[:, here] = grad_pre[m]
    out[:, :hidden_size] = dot(left[...], right[...], NT).astype(BF)
    out[:, hidden_size:second] = jnp.zeros((wide, second - hidden_size), BF)
    for m in range(micros):
        left[:, m * length : (m + 1) * length] = hidden[m]
        for r in range(4):
            here = slice(m * length + r * rows, m * length + (r + 1) * rows)
            right[:, here] = fourths[m][...] if r == 3 else grads[r][m]
    out[:, second : second + wide] = dot(left[...], right[...], NT).astype(BF)
    end = second + wide
    out[:, end:] = jnp.zeros((wide, out.shape[1] - end), BF)


def weights_part(hidden, grad_pre, normed, grads, fourths, after=()):
    micros, hidden_size, length = hidden.shape
    wide = fourths[0].shape[0]
    second = padded(hidden_size)
    operands = [hidden, grad_pre, normed, *grads, *fourths]
    return call(
        functools.partial(weights_kernel, second),
        operands,
        [whole_spec()] * len(operands),
        [shape(hidden_size, second + padded(wide))],
        [whole_spec()],
        4 * micros * length * wide * hidden_size,
        scratch=[pltpu.VMEM((wide, micros * length), BF)] * 2,
        after=after,
    )[0]


def turn_kernel(width, *refs):
    got = refs[:3]
    middle, grad, weight, vectors = refs[3:7]
    grad_middle, grad_attn, traded, tail, sums = refs[7:]
    step = pl.program_id(0)
    dy = grad[0].astype(F32)
    total = got[0][0].astype(F32) + got[1][0].astype(F32) + got[2][0].astype(F32)
    normed, rate = normal_columns(middle[0])
    result = dy + norm_back_columns(normed, rate, total * column(vectors, 5))
    grad_middle[0] = result
    low = result.astype(BF)
    grad_attn[0] = low
    for j in range(4):
        traded[j, 0] = dot(weight[j * width : (j + 1) * width, :], low, NN).astype(BF)
    tail[0] = dot(weight[4 * width :, :], low, NN).astype(BF)

    @pl.when(step == 0)
    def _():
        sums[...] = jnp.zeros(sums.shape, F32)

    for k, rows in enumerate((low.astype(F32), total * normed, total, dy)):
        sums[:, k : k + 1] += rows.sum(axis=1, keepdims=True)


def turn(got, middle, grads, weight, vectors, heads, head_size, after=()):
    micros, wide, rows = middle.shape
    width = heads * head_size
    dims = middle.shape
    outs = [shape(*dims, dtype=F32), shape(*dims), shape(4, micros, width, rows)]
    outs += [shape(micros, head_size, rows), shape(wide, 4, dtype=F32)]
    traded_spec = pl.BlockSpec((4, 1, width, rows), lambda i: (0, i, 0, 0))
    return call(
        functools.partial(turn_kernel, width),
        [*got, middle, grads, weight, vectors],
        [each_spec(dims)] * 5 + [whole_spec()] * 2,
        outs,
        [each_spec(dims)] * 2 + [traded_spec, each_spec(outs[3].shape), whole_spec()],
        2 * micros * rows * wide * wide,
        after=after,
        steps=micros,
    )


def rear_kernel(heads, head_size, place, *refs):
    step = pl.program_id(0)
    qkv, tail_grad, log, tail_log, out, sums = (refs[k].at[0] for k in (0, 2, 3, 4, 6, 12))
    traded, weight = refs[1], refs[5]
    parts, fourths = refs[7:10], refs[10:12]
    keys, values, key_sum, value_sum = refs[13:]
    rows = tail_grad.shape[1]
    used = qkv.shape[0]
    width = heads * head_size
    me = place[0]
    scale = head_size**-0.5
    tail_at = 3 * width
    for r in range(4):
        here = slice(r * rows, (r + 1) * rows)
        keys[here, :width] = qkv[width : 2 * width, here].T
        keys[here, width:] = qkv[tail_at : tail_at + 2 * head_size, here].T
        values[here, :] = qkv[2 * width : 3 * width, here].T
    key_row = lax.broadcasted_iota(jnp.int32, (rows, rows), 0)
    query_row = lax.broadcasted_iota(jnp.int32, (rows, rows), 1)
    head_row = lax.broadcasted_iota(jnp.int32, (width, rows), 0) // head_size

    def slot(j):
        return pl.ds(pl.multiple_of((me ^ j) * rows, rows), rows)

    for i in range(4):
        query = qkv[:width, slot(i)]
        grad_out = traded[i, 0]
        for h in range(heads):
            band = slice(h * head_size, (h + 1) * head_size)
            masked = jnp.where(head_row == h, query, jnp.zeros_like(query))
            masked_grad = jnp.where(head_row == h, grad_out, jnp.zeros_like(grad_out))
            shift = log[h : h + 1, i * rows : (i + 1) * rows]
            probs, weighted = [], []
            delta = jnp.zeros((1, rows), F32)
            for j in range(i + 1):
                s = dot(keys[slot(j), :width], masked, NN)
                if j == i:
                    s = jnp.where(key_row <= query_row, s, MASKED)
                p = jnp.exp(s - shift)
                g = dot(values[slot(j), :], masked_grad, NN)
                delta = delta + (p * g).sum(axis=0, keepdims=True)
                probs.append(p)
                weighted.append(g)
            part = jnp.zeros((head_size, rows), F32)
            for j in range(i + 1):
                here = slice(j * rows, (j + 1) * rows)
                ds = (probs[j] * (weighted[j] - delta)).astype(BF)
                p = probs[j].astype(BF)
                key_part = dot(query[band, :], ds, NT)
                value_part = dot(grad_out[band, :], p, NT)
                if j == i:
                    key_sum[band, here] = key_part
                    value_sum[band, here] = value_part
                else:
                    key_sum[band, here] += key_part
                    value_sum[band, here] += value_part
                at = width + h * head_size
                part = part + dot(qkv[at : at + head_size, slot(j)], ds, NN)
            out[band, slot(i)] = (part * scale).astype(BF)

    query = qkv[used - head_size :, 0:rows]
    grad_out = tail_grad[...]
    blank = jnp.zeros_like(query)
    wide_query = jnp.concatenate((query, blank), axis=0)
    wide_grad = jnp.concatenate((blank, grad_out), axis=0)
    probs, weighted = [], []
    delta = jnp.zeros((1, rows), F32)
    for j in range(4):
        s = dot(keys[slot(j), width:], wide_query, NN)
        s = jnp.where(j * rows + key_row <= me * rows + query_row, s, MASKED)
        p = jnp.exp(s - tail_log[...])
        g = dot(keys[slot(j), width:], wide_grad, NN)
        delta = delta + (p * g).sum(axis=0, keepdims=True)
        probs.append(p)
        weighted.append(g)
    part = jnp.zeros((head_size, rows), F32)
    for j in range(4):
        here = slice(j * rows, (j + 1) * rows)
        ds = (probs[j] * (weighted[j] - delta)).astype(BF)
        part = part + dot(qkv[tail_at : tail_at + head_size, slot(j)], ds, NN)
        out[tail_at : tail_at + head_size, slot(j)] = dot(query, ds, NT).astype(BF)
        out[tail_at + head_size : tail_at + 2 * head_size, slot(j)] = dot(
            grad_out, probs[j].astype(BF), NT
        ).astype(BF)
        out[width : 2 * width, slot(j)] = key_sum[:, here].astype(BF)
        out[2 * width : 3 * width, slot(j)] = value_sum[:, here].astype(BF)
    out[used - head_size :, 0:rows] = (part * scale).astype(BF)
    out[used - head_size :, rows:] = jnp.zeros((head_size, 3 * rows), BF)
    total = jnp.zeros((used, rows), F32)
    for r in range(4):
        block = out[:, r * rows : (r + 1) * rows]
        part = dot(weight[:, :used], block, NN).astype(BF)
        if r == 3:
            keep_fourth(step, fourths, part)
        else:
            parts[r][0] = part
        total = total + block.astype(F32)
    sums[...] = total.sum(axis=1, keepdims=True)


def rear(place, qkv, traded, tail_grad, log, tail_log, weight, heads, head_size, after=()):
    micros, used, length = qkv.shape
    rows = length // 4
    wide = weight.shape[0]
    width = heads * head_size
    first = [shape(*qkv.shape)] + [shape(micros, wide, rows)] * 3
    last = shape(micros, used, 1, dtype=F32)
    traded_spec = pl.BlockSpec((4, 1, width, rows), lambda i: (0, i, 0, 0))
    return call(
        functools.partial(rear_kernel, heads, head_size),
        [place, qkv, traded, tail_grad, log, tail_log, weight],
        [scalar_spec(), each_spec(qkv.shape), traded_spec]
        + [each_spec(a.shape) for a in (tail_grad, log, tail_log)]
        + [whole_spec()],
        first + [shape(wide, rows)] * micros + [last],
        [each_spec(o.shape) for o in first] + [whole_spec()] * micros + [each_spec(last.shape)],
        40_000_000_000,
        scratch=[
            pltpu.VMEM((length, width + 2 * head_size), BF),
            pltpu.VMEM((length, width), BF),
            pltpu.VMEM((width, length), F32),
            pltpu.VMEM((width, length), F32),
        ],
        after=after,
        steps=micros,
    )


def merged_kernel(heads, head_size, place, normed, grads, columns, others, up_sum, *refs):
    weight, vectors, out, small = refs
    micros, used, length = grads.shape
    wide = normed.shape[1]
    width = heads * head_size
    me = place[0]
    ones = jnp.ones((8, length), BF)
    product = dot(normed[0], grads[0], NT)
    total = dot(ones, grads[0], NT)
    down_columns = columns[0]
    for m in range(1, micros):
        product = product + dot(normed[m], grads[m], NT)
        total = total + dot(ones, grads[m], NT)
        down_columns = down_columns + columns[m]
    total = total[0:1, :]
    matrix = weight[:, :used].astype(F32)
    out[:, :used] = (column(vectors, 0) * product + column(vectors, 1) * total).astype(BF)
    gain = (product * matrix).sum(axis=1, keepdims=True)
    shift = (matrix * total).sum(axis=1, keepdims=True)
    small[...] = jnp.zeros(small.shape, F32)
    mine = pl.ds(pl.multiple_of(me * width, width), width)
    small[:, 0:1] = gain
    small[:, 1:2] = shift
    small[mine, 2:3] = down_columns[:width, :]
    small[mine, 3:4] = down_columns[2 * width : 3 * width, :]
    small[4 * width :, 2:3] = down_columns[used - head_size :, :]
    small[4 * width :, 3:4] = down_columns[3 * width + head_size : 3 * width + 2 * head_size, :]
    small[:, 4:8] = others[...]
    lane = lax.broadcasted_iota(jnp.int32, (wide, 4), 1)
    small[:, 8:12] = jnp.where(lane == me, up_sum[...], 0.0)
    out[:, used:] = small[:, : out.shape[1] - used].astype(BF)


def merged_part(
    place, normed, grads, columns, others, up_sum, weight, vectors, heads, head_size, after=()
):
    micros, wide, length = normed.shape
    used = grads.shape[1]
    operands = [place, normed, grads, columns, others, up_sum, weight, vectors]
    return call(
        functools.partial(merged_kernel, heads, head_size),
        operands,
        [scalar_spec()] + [whole_spec()] * (len(operands) - 1),
        [shape(*weight.shape)],
        [whole_spec()],
        2 * micros * length * wide * used,
        scratch=[pltpu.VMEM((wide, 128), F32)],
        after=after,
    )[0]


def out_weight_kernel(attended, grads, out):
    total = dot(attended[0], grads[0], NT)
    for m in range(1, attended.shape[0]):
        total = total + dot(attended[m], grads[m], NT)
    out[...] = total.astype(BF)


def out_weight_part(attended, grads, after=()):
    micros, wide, rows = attended.shape
    return call(
        out_weight_kernel,
        [attended, grads],
        [whole_spec()] * 2,
        [shape(wide, wide)],
        [whole_spec()],
        2 * micros * rows * wide * wide,
        after=after,
    )[0]


def finish_input_kernel(one, two, three, x, grad_middle, vectors, out):
    total = one[0].astype(F32) + two[0].astype(F32) + three[0].astype(F32)
    normed, rate = normal_columns(x[0].astype(F32))
    out[0] = grad_middle[0] + norm_back_columns(normed, rate, total * column(vectors, 0))


def finish_output_kernel(one, two, three, middle, vectors, out):
    total = one[0].astype(F32) + two[0].astype(F32) + three[0].astype(F32)
    out[0] = (middle[0] + total + column(vectors, 7)).astype(BF)


def finish(kernel, arrays, vectors, dtype, after=()):
    dims = arrays[0].shape
    return call(
        kernel,
        [*arrays, vectors],
        [each_spec(dims)] * len(arrays) + [whole_spec()],
        [shape(*dims, dtype=dtype)],
        [each_spec(dims)],
        20 * dims[0] * dims[1] * dims[2],
        after=after,
        cost=0,
        steps=dims[0],
    )[0]


def spread_kernel(piece, second, place, *refs):
    sources = refs[:4]
    grad_up, grad_down = refs[4:]
    shards = grad_up.shape[1] // (4 * piece)
    wide = grad_down.shape[1]
    for k in range(4):

        @pl.when(place[0] == k)
        def _(k=k):
            for j in range(4):
                source = sources[j ^ k]
                for f in range(shards):
                    at = (f * 4 + j) * piece
                    grad_up[:, at : at + piece] = source[:, f * piece : (f + 1) * piece].astype(F32)
                grad_down[j * piece : (j + 1) * piece, :] = source[:, second : second + wide].astype(
                    F32
                )


def spread(place, sources, shards, piece, wide, after=()):
    own = sources[0].shape[0]
    return call(
        functools.partial(spread_kernel, piece, padded(shards * piece)),
        [place, *sources],
        [scalar_spec()] + [whole_spec()] * 4,
        [shape(own, 4 * shards * piece, dtype=F32), shape(4 * piece, wide, dtype=F32)],
        [whole_spec()] * 2,
        0,
        after=after,
        cost=0,
    )


def spread_heads_kernel(width, head_size, place, *refs):
    sources = refs[:4]
    out_parts = refs[4:8]
    grad_merged, grad_out = refs[8:10]
    rows = refs[10:]
    wide = grad_merged.shape[1] // 3
    total = sources[0][:, 3 * width :].astype(F32)
    total_out = out_parts[0][...].astype(F32)
    for r in range(1, 4):
        total = total + sources[r][:, 3 * width :].astype(F32)
        total_out = total_out + out_parts[r][...].astype(F32)
    grad_out[...] = total_out
    table = total[:, 3 * head_size :].T
    own = table.shape[1]
    for index, row in enumerate(rows):
        if index < 8:
            row[...] = table[index]
        else:
            for part in range(row.shape[0] // own):
                row[part * own : (part + 1) * own] = table[8 + part]
    for part, tail in enumerate((2, 0, 1)):
        at = part * wide + 4 * width
        grad_merged[:, at : at + head_size] = total[:, tail * head_size : (tail + 1) * head_size]
    for k in range(4):

        @pl.when(place[0] == k)
        def _(k=k):
            for j in range(4):
                source = sources[j ^ k]
                for part in range(3):
                    at = part * wide + j * width
                    grad_merged[:, at : at + width] = source[
                        :, part * width : (part + 1) * width
                    ].astype(F32)


def spread_heads(place, sources, out_parts, width, head_size, wide, after=()):
    own, columns = sources[0].shape
    quads = columns - 3 * width - 3 * head_size - 8
    return call(
        functools.partial(spread_heads_kernel, width, head_size),
        [place, *sources, *out_parts],
        [scalar_spec()] + [whole_spec()] * 8,
        [
            shape(own, 3 * wide, dtype=F32),
            shape(own, wide, dtype=F32),
        ]
        + [shape(own, dtype=F32)] * 8
        + [shape(own * quads, dtype=F32)],
        [whole_spec()] * 11,
        0,
        after=after,
        cost=0,
    )


def on_device(
    layer_input,
    output_grad,
    attn_gain,
    attn_shift,
    merged_weight,
    query_bias,
    value_bias,
    out_weight,
    out_bias,
    mlp_gain,
    mlp_shift,
    up_weight,
    up_bias,
    down_weight,
    down_bias,
):
    micros, _, rows, wide = layer_input.shape
    assert micros == 2
    head_size = wide // HEADS
    shards = lax.axis_size("fsdp")
    me = lax.axis_index("ctx")
    heads = HEADS // 4
    width = heads * head_size
    own = merged_weight.shape[0]
    hidden = up_weight.shape[1]
    piece = hidden // shards // 4
    quads = hidden // wide
    used = 3 * width + 3 * head_size
    place = me.astype(jnp.int32).reshape(1)
    x = layer_input.transpose(0, 1, 3, 2).reshape(micros, wide, rows)
    dy = output_grad.transpose(0, 1, 3, 2).reshape(micros, wide, rows)

    small = [
        attn_gain,
        attn_shift,
        query_bias,
        value_bias,
        out_bias,
        mlp_gain,
        mlp_shift,
        down_bias,
        up_bias,
    ]
    first = pick(place, merged_weight, small, width, head_size)
    x_ctx, x_fourth = gather_blocks(x)
    dy_ctx = [dy] + [swap(pass_on(dy, x_fourth), bit) for bit in (1, 2)]
    first = lax.all_gather(first, "fsdp", axis=0, tiled=True)
    out_full = lax.all_gather(out_weight, "fsdp", axis=0, tiled=True)
    second = pick_hidden(
        place,
        up_weight,
        lax.dynamic_slice_in_dim(down_weight, me * piece, piece, 0),
        shards,
        piece,
        after=x_ctx[1:],
    )
    done = [second]
    second = lax.all_gather(second, "fsdp", axis=0, tiled=True)

    def then(*others):
        return (*done[-1:], *others)

    fronts = []
    parts = []
    for m in range(micros):
        fronts.append(
            front(
                place,
                x_ctx,
                x_fourth[m],
                m,
                first,
                fronts[0][5] if m else None,
                fronts[0][6] if m else None,
                fronts[-1] if m else None,
                heads,
                head_size,
                after=then(),
            )
        )
        done.append(fronts[-1][2])
        parts.append(gather_four(fronts[m][2], m))
        if m == 0:
            vectors = fronts[0][6]
    normed, qkv, _, log, tail_log = fronts[-1][:5]
    dy_fourth = []
    for m in range(micros):
        bit = 1 if m % 2 == 0 else 2
        done.append(pass_micro(dy_ctx[3 - bit], m, then(*([] if m else parts[0][1:3]))))
        dy_fourth.append(swap(done[-1], bit))
    middles = []
    for m in range(micros):
        middles.append(
            middle_part(
                place,
                parts[m],
                x_ctx,
                x_fourth[m],
                m,
                out_full,
                vectors,
                middles[0][3] if m else None,
                middles[-1] if m else None,
                heads,
                head_size,
                after=() if m else then(),
            )
        )
    middle, normed_two, attended = middles[-1][:3]
    done.append(normed_two)

    result = feed(place, normed_two, dy_ctx, dy_fourth, second, vectors, after=then())
    hidden_rows, grad_pre, back, up_sum = result[0], result[1], result[2:7], result[7]
    done.append(hidden_rows)
    back = Reduction(list(back[:3]), list(back[3:]))
    grad_second = weights_part(
        hidden_rows, grad_pre, normed_two, dy_ctx, dy_fourth, after=then()
    )
    done.append(grad_second)
    summed_second = lax.psum_scatter(grad_second, "fsdp", scatter_dimension=0, tiled=True)
    shared_second = gather_straight(summed_second)
    done.append(back.relay(then()))
    result = feed_out(hidden_rows, second, wide, after=then())
    done.append(result[0])
    outs = Reduction(list(result[:3]), list(result[3:]))

    grad_middle, grad_attn, traded, tail_grad, row_sums = turn(
        back.got, middle, dy, out_full, vectors, heads, head_size, after=then()
    )
    done.append(grad_attn)
    traded = exchange(traded)
    done.append(outs.relay(then()))
    grad_out_weight = out_weight_part(attended, grad_attn, after=then())
    done.append(grad_out_weight)
    summed_out = lax.psum_scatter(grad_out_weight, "fsdp", scatter_dimension=0, tiled=True)
    result = rear(
        place, qkv, traded, tail_grad, log, tail_log, first, heads, head_size, after=then()
    )
    grad_qkv, column_sums = result[0], result[6]
    done.append(grad_qkv)
    summed = Reduction(list(result[1:4]), list(result[4:6]))
    layer_output = finish(finish_output_kernel, [*outs.got, middle], vectors, BF, after=then())
    done.append(layer_output)
    done.append(summed.relay(then()))
    last = merged_part(
        place,
        normed,
        grad_qkv,
        column_sums,
        row_sums,
        up_sum,
        first,
        vectors,
        heads,
        head_size,
        after=then(*shared_second, summed_out),
    )
    done.append(last)
    summed_last = lax.psum_scatter(last, "fsdp", scatter_dimension=0, tiled=True)
    parts = pass_on(summed_last, then())
    done.append(parts)
    parts = gather_straight(parts)
    input_grad = finish(
        finish_input_kernel, [*summed.got, x, grad_middle], vectors, F32, after=then()
    )
    done.append(input_grad)

    grad_up, grad_down = spread(
        place, shared_second, shards, piece, wide, after=then()
    )
    done.append(grad_up)
    grad_merged, grad_out_weight, *vector_sums = spread_heads(
        place, parts, gather_straight(summed_out), width, head_size, wide, after=then()
    )
    def rows_first(a):
        return a.reshape(micros, 1, wide, rows).transpose(0, 1, 3, 2)

    return (
        rows_first(layer_output),
        rows_first(input_grad),
        vector_sums[0],
        vector_sums[1],
        grad_merged,
        vector_sums[2],
        vector_sums[3],
        grad_out_weight,
        vector_sums[4],
        vector_sums[5],
        vector_sums[6],
        grad_up,
        vector_sums[8],
        grad_down,
        vector_sums[7],
    )


def solution(mesh):
    rows = P(None, "fsdp", "ctx", None)
    matrix = P("fsdp", None)
    vector = P("fsdp")
    in_specs = (
        rows,
        rows,
        vector,
        vector,
        matrix,
        vector,
        vector,
        matrix,
        vector,
        vector,
        vector,
        matrix,
        vector,
        matrix,
        vector,
    )
    out_specs = (rows, rows) + in_specs[2:]
    step = on_device if mesh.shape["ctx"] == 4 else general_device
    return jax.shard_map(
        step, mesh=mesh, in_specs=in_specs, out_specs=out_specs, check_vma=False
    )
```
